128 devices in a mesh: ctx: 64 (over y_hi, z, x, core), shard: 2 (over y_lo).
Axes of the slice: x: 4, y: 4 (y_hi: 2, y_lo: 2; y = y_hi * 2 + y_lo), z: 4, core: 2. Of those that a mesh axis runs over, the one named last changes fastest.
Arguments:
- hidden_in: float32 [8192, 1152], P('ctx'), may hold values from -6 to 6
- out_grad: float32 [8192, 1152], P('ctx'), may hold values from -16 to 16
- block_order: int32 [64], replicated, may hold values from 0 to 63, each once
- norm_gains: float32 [4, 1152], replicated, may hold values from 0.1 to 1.9
- head_gains: float32 [2, 256], replicated, may hold values from 0.1 to 1.9
- w_query: bfloat16 [1152, 1024], P('ctx', 'shard'), may hold values from -0.1875 to 0.1875
- w_key: bfloat16 [1152, 256], P('ctx'), may hold values from -0.1875 to 0.1875
- w_value: bfloat16 [1152, 256], P('ctx'), may hold values from -0.1875 to 0.1875
- w_out: bfloat16 [1024, 1152], P('shard', 'ctx'), may hold values from -0.1875 to 0.1875
- w_gate: bfloat16 [1152, 6912], P('ctx', 'shard'), may hold values from -0.1875 to 0.1875
- w_up: bfloat16 [1152, 6912], P('ctx', 'shard'), may hold values from -0.1875 to 0.1875
- w_down: bfloat16 [6912, 1152], P('shard', 'ctx'), may hold values from -0.078125 to 0.078125
Outputs:
- block_out: float32 [8192, 1152], P('ctx')
- input_grad: float32 [8192, 1152], P('ctx')
- query_wgrad: float32 [1152, 1024], P('ctx', 'shard')
- key_wgrad: float32 [1152, 256], P('ctx')
- value_wgrad: float32 [1152, 256], P('ctx')
- out_wgrad: float32 [1024, 1152], P('shard', 'ctx')
- gate_wgrad: float32 [1152, 6912], P('ctx', 'shard')
- up_wgrad: float32 [1152, 6912], P('ctx', 'shard')
- down_wgrad: float32 [6912, 1152], P('shard', 'ctx')
- norm_grads: float32 [4, 1152], P(None, 'ctx')
- head_grads: float32 [2, 256], P(None, 'ctx')
The draws below stay inside these ranges and needn't reach their ends.
Inputs may be any that keep to these rules, and one draw needn't show every extreme that they name: The i-th device of ctx holds sequence block block_order[i] of 128 positions; every block appears once.
All inputs are finite; a program needn't handle non-finite values.
Results may differ from the reference program's by a relative error of at most 0.04.
Values may be sent and summed in bfloat16 or wider, within the bound.
No kernel may reach another device: no remote copies, remote signals or barrier semaphores. Data moves between devices by JAX's collectives and lax.ppermute only.
A program may use at most 256 MiB of HBM per device.

```python
import math
import jax
import jax.numpy as jnp
from jax import lax

D = 1152
HEADS = 4
HD = 256
FF = 6912
BLK = 128
SEQ = 8192
N_CTX = 64


def raised(drawn, key, source, target, parts, factor):
    owner, partner = [(jnp.arange(drawn.shape[axis_at]) // (drawn.shape[axis_at] // parts)).reshape([-1 if axis == axis_at else 1 for axis in range(drawn.ndim)]) for axis_at in (source, target)]
    chosen = jax.random.permutation(key, parts)[partner]
    strong = (owner == chosen) | (owner == (partner + parts // 2) % parts)
    return jnp.where(strong, factor * drawn, drawn)


def steps_of(stream_key, dims, shards, smallest, top_value):
    def one(dim, blocks):
        heights = jax.random.uniform(jax.random.fold_in(jax.random.fold_in(stream_key, 6), dim), (blocks,), jnp.float32, smallest / len(shards), top_value / len(shards))
        return jnp.repeat(jnp.exp(heights), dims[dim] // blocks).reshape((-1,) + (1,) * (len(dims) - dim - 1))

    level = one(*shards[0])
    for cut in shards[1:]:
        level = level * one(*cut)
    return level


def centred(own_key, shape, width, bound, split=(), held_as=jnp.bfloat16):
    level = steps_of(own_key, shape, split, -0.22, 0.18) if split else 1.0
    entries = jax.random.normal(own_key, shape, jnp.float32) * width * level
    return jnp.minimum(jnp.maximum(entries, -bound), bound).astype(held_as)


def gaussian_with(key, dims, scale, bound, shards, heavy, kind=jnp.bfloat16):
    entries = scale * jax.random.normal(key, dims, jnp.float32)
    if shards:
        entries = entries * steps_of(key, dims, shards, -0.22, 0.18)
    return jnp.clip(raised(entries, jax.random.fold_in(key, 3), *heavy), -bound, bound).astype(kind)


def setup_inputs(seed: int = 0) -> dict:
    splits = jax.random.split(jax.random.key(seed), 13)
    hidden_in = centred(splits[0], (SEQ, D), 1.0, 6.0, ((0, 64),), jnp.float32)
    out_grad = gaussian_with(splits[1], (SEQ, D), 1.0, 16.0, ((0, 64),), (0, 1, 64, 4.0), jnp.float32)
    block_order = jax.random.permutation(splits[2], N_CTX).astype(jnp.int32)
    norm_gains = jnp.clip(1.0 + 0.18 * jax.random.normal(splits[3], (4, D), jnp.float32), 0.1, 1.9)
    head_gains = jnp.clip(1.0 + 0.18 * jax.random.normal(splits[4], (2, HD), jnp.float32), 0.1, 1.9)
    w_query = centred(splits[5], (D, HEADS * HD), D ** -0.5, 0.1875, ((0, 64), (1, 2)))
    w_key = centred(splits[6], (D, HD), D ** -0.5, 0.1875, ((0, 64),))
    w_value = centred(splits[7], (D, HD), D ** -0.5, 0.1875, ((0, 64),))
    w_out = centred(splits[8], (HEADS * HD, D), (HEADS * HD) ** -0.5, 0.1875, ((0, 2), (1, 64)))
    w_gate = centred(splits[9], (D, FF), D ** -0.5, 0.1875, ((0, 64), (1, 2)))
    w_up = centred(splits[10], (D, FF), D ** -0.5, 0.1875, ((0, 64), (1, 2)))
    w_down = centred(splits[11], (FF, D), FF ** -0.5, 0.078125, ((0, 2), (1, 64)))
    return {"hidden_in": hidden_in, "out_grad": out_grad, "block_order": block_order, "norm_gains": norm_gains, "head_gains": head_gains, "w_query": w_query, "w_key": w_key, "w_value": w_value, "w_out": w_out, "w_gate": w_gate, "w_up": w_up, "w_down": w_down}


EPS = 1e-06
THETA = 1000000.0
NEG = -1e+30

@jax.custom_vjp
def low(v):
    return lax.optimization_barrier(v.astype(jnp.bfloat16)).astype(jnp.float32)

@jax.custom_vjp
def low_back(v):
    return v

def low_keep(v):
    return (low(v), None)

def low_pass(kept, grad):
    return (grad,)

def back_keep(v):
    return (v, None)

def back_low(kept, grad):
    return (low(grad),)
low.defvjp(low_keep, low_pass)
low_back.defvjp(back_keep, back_low)

def product(left, right):
    return jnp.dot(left, right, precision=lax.Precision.HIGHEST, preferred_element_type=jnp.float32)

def rms_scale(values, gain):
    return values * lax.rsqrt(lax.optimization_barrier(jnp.mean(values * values, axis=-1, keepdims=True)) + EPS) * gain

def rotate(values, cosine_table, sine_table):
    half_width = values.shape[-1] // 2
    first = values[..., :half_width]
    second = values[..., half_width:]
    return jnp.concatenate([first * cosine_table - second * sine_table, second * cosine_table + first * sine_table], axis=-1)

def head_path(values, gain, cosine_table, sine_table):
    return rotate(rms_scale(values, gain), cosine_table, sine_table)

def geglu(gate_pre, up_pre):
    return jax.nn.gelu(gate_pre, approximate=True) * up_pre

def tables(positions, head_width):
    frequency = jnp.arange(head_width // 2, dtype=jnp.float32)
    inverse = jnp.exp(frequency * (-2.0 * math.log(THETA) / head_width))
    angles = positions.astype(jnp.float32)[:, None] * inverse[None, :]
    return (jnp.cos(angles), jnp.sin(angles))

def attention(queries, keys, values, positions):
    block_rows = math.gcd(SEQ, 512)
    blocks = SEQ // block_rows
    query_blocks = queries.reshape(blocks, block_rows, HEADS, HD)
    place_blocks = positions.reshape(blocks, block_rows)

    @jax.checkpoint
    def one_block(pair):
        query_block, place_block = pair
        scores = jnp.einsum('qhd,kd->hqk', query_block, keys, precision=lax.Precision.HIGHEST, preferred_element_type=jnp.float32) * HD ** (-0.5)
        scores = low_back(scores)
        allowed = place_block[None, :, None] >= positions[None, None, :]
        probs = jax.nn.softmax(jnp.where(allowed, scores, NEG), axis=-1)
        probs = low(probs)
        return jnp.einsum('hqk,kd->qhd', probs, values, precision=lax.Precision.HIGHEST, preferred_element_type=jnp.float32)
    results = lax.map(one_block, (query_blocks, place_blocks))
    return results.reshape(SEQ, HEADS, HD)

def reference(hidden_in, out_grad, block_order, norm_gains, head_gains, w_query, w_key, w_value, w_out, w_gate, w_up, w_down):
    offsets = jnp.arange(BLK, dtype=jnp.int32)
    positions = (block_order[:, None].astype(jnp.int32) * BLK + offsets[None, :]).reshape(SEQ).astype(jnp.int32)
    cosine_table, sine_table = tables(positions, HD)

    def forward(inputs, gains, heads_gain, query_w, key_w, value_w, out_w, gate_w, up_w, down_w):
        attn_norm = low(rms_scale(inputs, gains[0]))
        query_pre = low_back(product(attn_norm, query_w)).reshape(SEQ, HEADS, HD)
        key_pre = low_back(product(attn_norm, key_w))
        values = low(low_back(product(attn_norm, value_w)))
        queries = low(head_path(query_pre, heads_gain[0], cosine_table[:, None, :], sine_table[:, None, :]))
        keys = low(head_path(key_pre, heads_gain[1], cosine_table, sine_table))
        mixed = attention(queries, keys, values, positions)
        mixed = low(low_back(mixed)).reshape(SEQ, HEADS * HD)
        attn_out = low_back(product(mixed, out_w))
        mid_state = inputs + rms_scale(attn_out, gains[1])
        ffn_norm = low(rms_scale(mid_state, gains[2]))
        gate_pre = low_back(product(ffn_norm, gate_w))
        up_pre = low_back(product(ffn_norm, up_w))
        hidden = low(geglu(gate_pre, up_pre))
        ffn_out = low_back(product(hidden, down_w))
        return mid_state + rms_scale(ffn_out, gains[3])
    block_out, backward = jax.vjp(forward, hidden_in, norm_gains, head_gains, w_query.astype(jnp.float32), w_key.astype(jnp.float32), w_value.astype(jnp.float32), w_out.astype(jnp.float32), w_gate.astype(jnp.float32), w_up.astype(jnp.float32), w_down.astype(jnp.float32))
    grads = backward(out_grad)
    return (block_out, grads[0], grads[3], grads[4], grads[5], grads[6], grads[7], grads[8], grads[9], grads[1], grads[2])
```

```python
import math

import jax
import jax.numpy as jnp
from jax import lax
from jax.sharding import Mesh, PartitionSpec as P

HD = 256
EPS = 1e-06
THETA = 1000000.0
BF = jnp.bfloat16
F32 = jnp.float32
CTX = ("y", "z", "x", "c")


def matmul(left, right):
    return jnp.dot(left, right, preferred_element_type=F32)


def inner_rows(left, right):
    return lax.dot_general(left, right, (((0,), (0,)), ((), ())), preferred_element_type=F32)


def inner_cols(left, right):
    return lax.dot_general(left, right, (((1,), (1,)), ((), ())), preferred_element_type=F32)


def rms_scale(values, gain):
    return values * lax.rsqrt(jnp.mean(values * values, axis=-1, keepdims=True) + EPS) * gain


def rotate(values, cosine_table, sine_table):
    half_width = values.shape[-1] // 2
    first = values[..., :half_width]
    second = values[..., half_width:]
    return jnp.concatenate(
        [first * cosine_table - second * sine_table, second * cosine_table + first * sine_table],
        axis=-1,
    )


def geglu(gate_pre, up_pre):
    return jax.nn.gelu(gate_pre, approximate=True) * up_pre


def tables(positions, head_width):
    frequency = jnp.arange(head_width // 2, dtype=F32)
    inverse = jnp.exp(frequency * (-2.0 * math.log(THETA) / head_width))
    angles = positions.astype(F32)[:, None] * inverse[None, :]
    return (jnp.cos(angles), jnp.sin(angles))


def shift(values, axis, step=1):
    size = lax.axis_size(axis)
    return lax.ppermute(values, axis, [(i, (i + step) % size) for i in range(size)])


def gather_ring(block, axis):
    half = block.shape[0] // 2
    previous = shift(block, axis, 1)
    following = shift(block, axis, -1)
    far_low = shift(previous[:half], axis, 1)
    far_high = shift(following[half:], axis, -1)
    return [block, following, jnp.concatenate([far_low, far_high], 0), previous]


def reduce_ring(chunks, axis):
    rows = chunks[0].shape[0]
    half = (rows // 2 + 7) // 8 * 8
    from_previous = shift(chunks[2][:half], axis, 1)
    from_next = shift(chunks[2][half:], axis, -1)
    forward = jnp.concatenate(
        [(chunks[1][:half].astype(F32) + from_previous.astype(F32)).astype(BF), chunks[1][half:]], 0
    )
    backward = jnp.concatenate(
        [chunks[3][:half], (chunks[3][half:].astype(F32) + from_next.astype(F32)).astype(BF)], 0
    )
    return (
        chunks[0].astype(F32)
        + shift(forward, axis, 1).astype(F32)
        + shift(backward, axis, -1).astype(F32)
    )


def split_rows(values, parts):
    size = values.shape[0] // parts
    return [values[i * size : (i + 1) * size] for i in range(parts)]


def pick(core, first, second):
    return jnp.where(core == 0, first, second)


def shards(
    hidden_in,
    out_grad,
    block_order,
    norm_gains,
    head_gains,
    w_query,
    w_key,
    w_value,
    w_out,
    w_gate,
    w_up,
    w_down,
):
    tokens, width = hidden_in.shape
    y, z, x, core = (lax.axis_index(name) for name in CTX)
    other = 1 - core
    piece = width // 64
    units = w_gate.shape[1] // 2
    padded = (units + 127) // 128 * 128
    quarter = width // 4

    out_t, down_t = w_out.T, w_down.T

    def units_of(which):
        cut = [
            jnp.pad(lax.dynamic_slice_in_dim(w, which * units, units, 1), ((0, 0), (0, padded - units)))
            for w in (w_gate, w_up, down_t)
        ]
        return jnp.concatenate(cut, 1)

    def heads_of(which):
        cut = [lax.dynamic_slice_in_dim(w, which * HD, HD, 1) for w in (w_query, out_t)]
        return jnp.concatenate(cut + [w_key, w_value], 1)

    def chip_rows(of):
        mine, got = of(core), shift(of(other), "c")
        rows = pick(core, jnp.concatenate([mine, got], 0), jnp.concatenate([got, mine], 0))
        return jnp.concatenate([rows, shift(rows, "y")], 0)

    head_rows = chip_rows(heads_of)
    ffn_rows = chip_rows(units_of)
    ffn_w = lax.all_gather(ffn_rows, ("z", "x"), axis=0, tiled=True)
    head_z = jnp.concatenate(gather_ring(head_rows, "z"), 0)
    head_w = jnp.concatenate(gather_ring(head_z, "x"), 0)
    gate_up_w, down_w = ffn_w[:, : 2 * padded], ffn_w[:, 2 * padded :]
    query_w, out_w = head_w[:, :HD], head_w[:, HD : 2 * HD]
    key_w, value_w, pair_w = head_w[:, 2 * HD : 3 * HD], head_w[:, 3 * HD :], head_w[:, 2 * HD :]

    place = jnp.arange(width, dtype=jnp.int32)
    major, second = place // quarter, place // (quarter // 4) % 4
    tail_y, tail = place // (2 * piece) % 2, place % (2 * piece)

    def natural(z_at, x_at):
        return ((y + tail_y) % 2) * (width // 2) + z_at * (8 * piece) + x_at * (2 * piece) + tail

    by_gather = natural(major, second)
    by_x = natural((z + second) % 4, (x + major) % 4)
    by_z = natural((z + major) % 4, (x + second) % 4)

    def order(source, target):
        return (source[:, None] == target[None, :]).astype(BF)

    to_gather, to_x = order(place, by_gather), order(place, by_x)
    from_gather, from_x = order(by_gather, place), order(by_x, place)

    def reorder(values, moves):
        return matmul(values, moves).astype(BF)

    def both_cores(values):
        return jnp.concatenate([values, shift(values, "c")], 0)

    def sum_parts(partial, moves):
        low = reorder(partial.astype(BF), moves)
        chip = (low[:tokens].astype(F32) + shift(low[tokens:], "c").astype(F32)).astype(BF)
        return chip.astype(F32) + shift(chip, "s").astype(F32)

    offsets = jnp.arange(tokens, dtype=jnp.int32)

    def positions_of(places):
        return (block_order[places.reshape(-1)][:, None] * tokens + offsets[None, :]).reshape(-1)

    def device_of(y_at, z_at, x_at, core_at):
        return y_at * 32 + z_at * 8 + x_at * 2 + core_at

    steps = jnp.arange(4, dtype=jnp.int32)
    ring = device_of(
        (y + steps[None, None, :2]) % 2, (z + steps[None, :, None]) % 4, (x + steps[:, None, None]) % 4, 0
    )
    key_pos = [positions_of(ring + core), positions_of(ring + other)]
    own_pos = positions_of(device_of(y, z, x, core))
    chip_pos = jnp.concatenate([own_pos, positions_of(device_of(y, z, x, other))])
    cosine_table, sine_table = tables(chip_pos, HD)

    attn_val, pre_attn_back = jax.vjp(rms_scale, hidden_in, norm_gains[0])
    attn_x = reorder(attn_val.astype(BF), to_x)
    attn_chip = both_cores(attn_x)
    key_pre = matmul(attn_x, key_w)
    value_low = matmul(attn_x, value_w).astype(BF)
    key_val, key_back = jax.vjp(
        lambda values, gain: rotate(rms_scale(values, gain), cosine_table[:tokens], sine_table[:tokens]),
        key_pre,
        head_gains[1],
    )
    key_low = key_val.astype(BF)
    pair_low = jnp.concatenate([key_low, value_low], 1)
    pair_rows = jnp.concatenate([pair_low, shift(pair_low, "y")], 0)
    key_z = jnp.concatenate(gather_ring(pair_rows[:, :HD], "z"), 0)
    keys = jnp.concatenate(gather_ring(key_z, "x"), 0)
    value_x = jnp.concatenate(gather_ring(pair_rows[:, HD:], "x"), 0)
    value_parts = [split_rows(part, 4) for part in gather_ring(value_x, "z")]
    values = jnp.concatenate([value_parts[j][i] for i in range(4) for j in range(4)], 0)
    all_keys = [keys, shift(keys, "c")]
    all_values = [values, shift(values, "c")]

    query_pre = matmul(attn_chip, query_w)
    query_val, query_back = jax.vjp(
        lambda values, gain: rotate(rms_scale(values, gain), cosine_table, sine_table),
        query_pre,
        head_gains[0],
    )
    score_scale = HD ** (-0.5)
    queries = (query_val.astype(BF).astype(F32) * score_scale).astype(BF)
    weights, total, accum = [], 0.0, 0.0
    for part in range(2):
        scores = inner_cols(queries, all_keys[part])
        allowed = chip_pos[:, None] >= key_pos[part][None, :]
        weight = jnp.where(allowed, jnp.exp(scores), 0.0)
        total = total + jnp.sum(weight, axis=1)
        weights.append(weight.astype(BF))
        accum = accum + matmul(weights[part], all_values[part])
    inverse_total = (1.0 / total)[:, None]
    attn_rows = accum * inverse_total
    mixed_low = attn_rows.astype(BF)
    attn_out = sum_parts(inner_cols(mixed_low, out_w), from_x)
    post_attn, post_attn_back = jax.vjp(rms_scale, attn_out, norm_gains[1])
    mid_state = hidden_in + post_attn

    ffn_val, ffn_norm_back = jax.vjp(rms_scale, mid_state, norm_gains[2])
    ffn_chip = both_cores(reorder(ffn_val.astype(BF), to_gather))
    gate_up = matmul(ffn_chip, gate_up_w)
    hidden_val, geglu_back = jax.vjp(geglu, gate_up[:, :padded], gate_up[:, padded:])
    hidden_low = hidden_val.astype(BF)
    ffn_out = sum_parts(inner_cols(hidden_low, down_w), from_gather)
    post_ffn, post_ffn_back = jax.vjp(rms_scale, ffn_out, norm_gains[3])
    block_out = mid_state + post_ffn

    ffn_grad, gain_four = post_ffn_back(out_grad)
    ffn_grad_chip = both_cores(reorder(ffn_grad.astype(BF), to_gather))
    gate_grad, up_grad = geglu_back(matmul(ffn_grad_chip, down_w))
    gate_up_low = jnp.concatenate([gate_grad.astype(BF), up_grad.astype(BF)], 1)
    ffn_norm_grad = sum_parts(inner_cols(gate_up_low, gate_up_w), from_gather)
    mid_from, gain_three = ffn_norm_back(ffn_norm_grad)
    mid_grad = out_grad + mid_from

    half = padded // 2
    sources = jnp.concatenate([ffn_chip, ffn_grad_chip], 0)
    none_wide, none_half = jnp.zeros((2 * tokens, padded), BF), jnp.zeros((2 * tokens, half), BF)

    def ffn_chunks(first, second, target):
        grads = jnp.concatenate(
            [jnp.concatenate([first, none_half], 1), jnp.concatenate([none_wide, second], 1)], 0
        )
        chunks = {}
        for k in (2, 1, 3, 0):
            rows = reorder(sources, order(by_gather, target[k * quarter : (k + 1) * quarter]))
            chunks[k] = inner_rows(rows, grads).astype(BF)
        return [chunks[k] for k in range(4)]

    def reduce_two(chunks, first, second):
        low = reduce_ring(chunks, first).astype(BF)
        return reduce_ring(split_rows(low, 4), second)

    def reduce_y(values):
        low = values.astype(BF)
        own, far = split_rows(low, 2)
        return own.astype(F32) + shift(far, "y").astype(F32)

    def swap_cores(rows):
        low = rows.astype(BF)
        first, second = split_rows(low, 2)
        return pick(core, first, second).astype(F32), shift(pick(core, second, first), "c").astype(F32)

    ffn_first = reduce_two(ffn_chunks(gate_up_low[:, :padded], hidden_low[:, :half], by_x), "x", "z")
    ffn_second = reduce_two(ffn_chunks(gate_up_low[:, padded:], hidden_low[:, half:], by_z), "z", "x")
    ffn_mine, ffn_got = swap_cores(reduce_y(jnp.concatenate([ffn_first, ffn_second], 1)))

    def joined(start, size, mine, got):
        left, right = mine[:, start : start + size], got[:, start : start + size]
        return pick(core, jnp.concatenate([left, right], 1), jnp.concatenate([right, left], 1))

    gate_wgrad = joined(0, units, ffn_mine, ffn_got)
    up_wgrad = joined(padded + half, units, ffn_mine, ffn_got)

    def down_of(values):
        return jnp.concatenate([values[:, padded : padded + half], values[:, 2 * padded + half :]], 1)

    down_wgrad = joined(0, units, down_of(ffn_mine), down_of(ffn_got)).T

    attn_grad, gain_two = post_attn_back(mid_grad)
    attn_grad_chip = both_cores(reorder(attn_grad.astype(BF), to_x))
    rows_grad = matmul(attn_grad_chip, out_w).astype(BF)
    rows_wide = rows_grad.astype(F32)
    row_dot = jnp.sum(rows_wide * attn_rows, axis=1)[:, None]
    rows_scaled = (rows_wide * inverse_total).astype(BF)
    query_grad, key_parts, value_parts = 0.0, {}, {}
    for part in (1, 0):
        prob_grad = inner_cols(rows_grad, all_values[part])
        score_grad = (weights[part].astype(F32) * ((prob_grad - row_dot) * inverse_total)).astype(BF)
        query_grad = query_grad + matmul(score_grad, all_keys[part])
        key_parts[part] = inner_rows(score_grad, queries).astype(BF)
        value_parts[part] = inner_rows(weights[part], rows_scaled).astype(BF)
    key_sum = (key_parts[0].astype(F32) + shift(key_parts[1], "c").astype(F32)).astype(BF)
    value_sum = (value_parts[0].astype(F32) + shift(value_parts[1], "c").astype(F32)).astype(BF)
    key_own = reduce_two(split_rows(key_sum, 4), "x", "z")
    value_grid = value_sum.reshape(4, 4, 2 * tokens, HD)
    value_own = reduce_two([value_grid[:, k].reshape(-1, HD) for k in range(4)], "z", "x")
    pair_low = reduce_y(jnp.concatenate([key_own, value_own], 1)).astype(BF)
    pair_grad = pair_low.astype(F32) + shift(pair_low, "s").astype(F32)

    query_pre_grad, query_gain = query_back(query_grad * score_scale)
    query_gain = query_gain + shift(query_gain, "s")
    query_pre_low = query_pre_grad.astype(BF)
    attn_norm_sum = sum_parts(inner_cols(query_pre_low, query_w), from_x)
    key_pre_grad, key_gain = key_back(pair_grad[:, :HD])
    key_pre_low = key_pre_grad.astype(BF)
    value_grad_low = pair_grad[:, HD:].astype(BF)
    pair_part = inner_cols(jnp.concatenate([key_pre_low, value_grad_low], 1), pair_w).astype(BF)
    attn_norm_grad = attn_norm_sum + reorder(pair_part, from_x).astype(F32)
    input_from, gain_one = pre_attn_back(attn_norm_grad)
    input_grad = mid_grad + input_from

    kept, sent = pick(core, key_pre_low, value_grad_low), pick(core, value_grad_low, key_pre_low)
    pair_chip = jnp.concatenate([kept, shift(sent, "c")], 0)
    heads = [
        jnp.pad(gain.reshape(64, HD // 64), ((0, 0), (0, piece - HD // 64))).reshape(width)
        for gain in (query_gain, key_gain)
    ]
    gains = jnp.stack([gain_one, gain_two, gain_three, gain_four] + heads, 1)
    gains = jnp.pad(gains, ((0, 0), (0, 128 - gains.shape[1]))).astype(BF)
    head_grads_all = jnp.concatenate(
        [
            inner_rows(attn_chip, query_pre_low),
            inner_rows(attn_grad_chip, mixed_low),
            inner_rows(attn_chip, pair_chip),
            inner_rows(to_x, gains),
        ],
        1,
    ).astype(BF)
    head_own = reduce_two(split_rows(head_grads_all, 4), "x", "z")
    head_mine, head_got = swap_cores(reduce_y(head_own))
    query_wgrad = joined(0, HD, head_mine, head_got)
    out_wgrad = joined(HD, HD, head_mine, head_got).T
    pair_wgrad = joined(2 * HD, HD, head_mine, head_got)
    gain_sums = head_mine[:, 3 * HD :] + head_got[:, 3 * HD :]
    return (
        block_out,
        input_grad,
        query_wgrad,
        pair_wgrad[:, :HD],
        pair_wgrad[:, HD:],
        out_wgrad,
        gate_wgrad,
        up_wgrad,
        down_wgrad,
        gain_sums[:, :4].T,
        gain_sums[: HD // 64, 4:6].T,
    )


def solution(mesh):
    fine = Mesh(mesh.devices.reshape(2, 4, 4, 2, 2), ("y", "z", "x", "c", "s"))
    placed = (
        P(CTX, None),
        P(CTX, None),
        P(),
        P(),
        P(),
        P(CTX, "s"),
        P(CTX, None),
        P(CTX, None),
        P("s", CTX),
        P(CTX, "s"),
        P(CTX, "s"),
        P("s", CTX),
    )
    return jax.shard_map(
        shards,
        mesh=fine,
        in_specs=placed,
        out_specs=(
            P(CTX, None),
            P(CTX, None),
            P(CTX, "s"),
            P(CTX, None),
            P(CTX, None),
            P("s", CTX),
            P(CTX, "s"),
            P(CTX, "s"),
            P("s", CTX),
            P(None, CTX),
            P(None, CTX),
        ),
        check_vma=False,
    )
```

```python
import math

import jax
import jax.numpy as jnp
from jax import lax
from jax.experimental import pallas as pl
from jax.experimental.pallas import tpu as pltpu
from jax.sharding import Mesh, PartitionSpec as P

HD = 256
EPS = 1e-06
THETA = 1000000.0
BF = jnp.bfloat16
F32 = jnp.float32
CTX = ("y", "z", "x", "c")


def matmul(left, right):
    return jnp.dot(left, right, preferred_element_type=F32)


def inner_rows(left, right):
    return lax.dot_general(left, right, (((0,), (0,)), ((), ())), preferred_element_type=F32)


def inner_cols(left, right):
    return lax.dot_general(left, right, (((1,), (1,)), ((), ())), preferred_element_type=F32)


def rms_scale(values, gain):
    return values * lax.rsqrt(jnp.mean(values * values, axis=-1, keepdims=True) + EPS) * gain


def rotate(values, cosine_table, sine_table):
    half_width = values.shape[-1] // 2
    first = values[..., :half_width]
    second = values[..., half_width:]
    return jnp.concatenate(
        [first * cosine_table - second * sine_table, second * cosine_table + first * sine_table],
        axis=-1,
    )


def geglu(gate_pre, up_pre):
    return jax.nn.gelu(gate_pre, approximate=True) * up_pre


def tables(positions, head_width):
    frequency = jnp.arange(head_width // 2, dtype=F32)
    inverse = jnp.exp(frequency * (-2.0 * math.log(THETA) / head_width))
    angles = positions.astype(F32)[:, None] * inverse[None, :]
    return (jnp.cos(angles), jnp.sin(angles))


def shift(values, axis, step=1):
    size = lax.axis_size(axis)
    return lax.ppermute(values, axis, [(i, (i + step) % size) for i in range(size)])


def ring(values, major, step):
    moves = []
    for z in range(4):
        for x in range(4):
            for core in range(2):
                along_x = major == (core == 0)
                to_z, to_x = (z, (x + step) % 4) if along_x else ((z + step) % 4, x)
                moves.append((z * 8 + x * 2 + core, to_z * 8 + to_x * 2 + core))
    return lax.ppermute(values, ("z", "x", "c"), moves)


def gather_direct(block, major):
    return jnp.concatenate([block] + [ring(block, major, -k) for k in (1, 2, 3)], 0)


def gather_ring(block, major):
    half = block.shape[0] // 2
    previous = ring(block, major, 1)
    following = ring(block, major, -1)
    far_low = ring(previous[:half], major, 1)
    far_high = ring(following[half:], major, -1)
    return jnp.concatenate([block, following, far_low, far_high, previous], 0)


def wide_sum(*parts):
    return sum(part.astype(F32) for part in parts)


def reduce_direct(chunks, major):
    return wide_sum(chunks[0], *[ring(chunks[k], major, k) for k in (1, 2, 3)])


def reduce_ring(own, following, far_low, far_high, previous, major):
    half = far_low.shape[0]
    from_previous = ring(far_low, major, 1)
    from_next = ring(far_high, major, -1)
    forward = jnp.concatenate(
        [wide_sum(following[:half], from_previous).astype(BF), following[half:]], 0
    )
    backward = jnp.concatenate(
        [previous[:half], wide_sum(previous[half:], from_next).astype(BF)], 0
    )
    return wide_sum(own, ring(forward, major, 1), ring(backward, major, -1))


def reduce_rows(values, major):
    own, following, far, previous = split_rows(values, 4)
    half = (far.shape[0] // 2 + 7) // 8 * 8
    return reduce_ring(own, following, far[:half], far[half:], previous, major)


ATTN_BLOCK = 1024
VMEM = pltpu.CompilerParams(vmem_limit_bytes=48 * 1024 * 1024)


def attend_kernel(query, pair, key_pos, query_pos, weight, total, accum):
    scores = inner_cols(query[...], pair[:, :HD])
    exps = jnp.where(query_pos[...] >= key_pos[...], jnp.exp(scores), 0.0)
    low = exps.astype(BF)
    weight[...] = low

    @pl.when(pl.program_id(0) == 0)
    def _():
        total[...] = jnp.zeros_like(total)
        accum[...] = jnp.zeros_like(accum)

    total[...] += jnp.sum(exps, axis=1, keepdims=True)
    accum[...] += matmul(low, pair[:, HD:])


def attend(queries, pairs, key_pos, query_pos):
    rows, keys = queries.shape[0], pairs.shape[0]
    whole = lambda i: (0, 0)
    return pl.pallas_call(
        attend_kernel,
        grid=(keys // ATTN_BLOCK,),
        in_specs=[
            pl.BlockSpec((rows, HD), whole),
            pl.BlockSpec((ATTN_BLOCK, 2 * HD), lambda i: (i, 0)),
            pl.BlockSpec((1, ATTN_BLOCK), lambda i: (0, i)),
            pl.BlockSpec((rows, 1), whole),
        ],
        out_specs=[
            pl.BlockSpec((rows, ATTN_BLOCK), lambda i: (0, i)),
            pl.BlockSpec((rows, 1), whole),
            pl.BlockSpec((rows, HD), whole),
        ],
        out_shape=[
            jax.ShapeDtypeStruct((rows, keys), BF),
            jax.ShapeDtypeStruct((rows, 1), F32),
            jax.ShapeDtypeStruct((rows, HD), F32),
        ],
        compiler_params=VMEM,
        name="attend",
    )(queries, pairs, key_pos[None, :], query_pos[:, None])


def attend_back_kernel(query, pair, weight, grad, scaled, dot, inverse, pair_grad, query_grad):
    weights = weight[...]
    prob_grad = inner_cols(grad[...], pair[:, HD:])
    score_grad = (weights.astype(F32) * ((prob_grad - dot[...]) * inverse[...])).astype(BF)
    pair_grad[:, :HD] = inner_rows(score_grad, query[...]).astype(BF)
    pair_grad[:, HD:] = inner_rows(weights, scaled[...]).astype(BF)

    @pl.when(pl.program_id(0) == 0)
    def _():
        query_grad[...] = jnp.zeros_like(query_grad)

    query_grad[...] += matmul(score_grad, pair[:, :HD])


def attend_back(queries, pairs, weights, grads, scaled, dot, inverse):
    rows, keys = queries.shape[0], pairs.shape[0]
    whole = lambda i: (0, 0)
    return pl.pallas_call(
        attend_back_kernel,
        grid=(keys // ATTN_BLOCK,),
        in_specs=[
            pl.BlockSpec((rows, HD), whole),
            pl.BlockSpec((ATTN_BLOCK, 2 * HD), lambda i: (i, 0)),
            pl.BlockSpec((rows, ATTN_BLOCK), lambda i: (0, i)),
            pl.BlockSpec((rows, HD), whole),
            pl.BlockSpec((rows, HD), whole),
            pl.BlockSpec((rows, 1), whole),
            pl.BlockSpec((rows, 1), whole),
        ],
        out_specs=[
            pl.BlockSpec((ATTN_BLOCK, 2 * HD), lambda i: (i, 0)),
            pl.BlockSpec((rows, HD), whole),
        ],
        out_shape=[
            jax.ShapeDtypeStruct((keys, 2 * HD), BF),
            jax.ShapeDtypeStruct((rows, HD), F32),
        ],
        compiler_params=VMEM,
        name="attend_back",
    )(queries, pairs, weights, grads, scaled, dot, inverse)


def ffn_wgrad_kernel(count, left, gate_up, hidden, *outs):
    def store(first, right):
        start = 0
        for out in outs:
            rows = out.shape[0]
            out[...] = matmul(left[start : start + rows, first : first + right.shape[0]], right[...]).astype(BF)
            start += rows

    @pl.when(pl.program_id(0) < count)
    def _():
        store(0, gate_up)

    @pl.when(pl.program_id(0) >= count)
    def _():
        store(gate_up.shape[0], hidden)


def ffn_wgrad(left, gate_up, hidden, tile=256):
    width, rows = left.shape[0], gate_up.shape[0]
    count, more = gate_up.shape[1] // tile, hidden.shape[1] // tile
    sizes = [width // 4, width // 4, width // 8, width // 8, width // 4]
    return pl.pallas_call(
        lambda *refs: ffn_wgrad_kernel(count, *refs),
        grid=(count + more,),
        in_specs=[
            pl.BlockSpec(left.shape, lambda j: (0, 0)),
            pl.BlockSpec((rows, tile), lambda j: (0, jnp.minimum(j, count - 1))),
            pl.BlockSpec((rows, tile), lambda j: (0, jnp.maximum(j - count, 0))),
        ],
        out_specs=[pl.BlockSpec((size, tile), lambda j: (0, j)) for size in sizes],
        out_shape=[jax.ShapeDtypeStruct((size, (count + more) * tile), BF) for size in sizes],
        compiler_params=VMEM,
        name="ffn_wgrad",
    )(left, gate_up, hidden)


def split_rows(values, parts):
    size = values.shape[0] // parts
    return [values[i * size : (i + 1) * size] for i in range(parts)]


def pick(core, first, second):
    return jnp.where(core == 0, first, second)


def shards(
    hidden_in,
    out_grad,
    block_order,
    norm_gains,
    head_gains,
    w_query,
    w_key,
    w_value,
    w_out,
    w_gate,
    w_up,
    w_down,
):
    tokens, width = hidden_in.shape
    y, z, x, core = (lax.axis_index(name) for name in CTX)
    other = 1 - core
    piece = width // 64
    units = w_gate.shape[1] // 2
    padded = (units + 127) // 128 * 128
    quarter = width // 4

    out_t, down_t = w_out.T, w_down.T

    def units_of(which):
        cut = [
            jnp.pad(lax.dynamic_slice_in_dim(w, which * units, units, 1), ((0, 0), (0, padded - units)))
            for w in (w_gate, w_up, down_t)
        ]
        return jnp.concatenate(cut, 1)

    def heads_of(which):
        cut = [lax.dynamic_slice_in_dim(w, which * HD, HD, 1) for w in (w_query, out_t)]
        return jnp.concatenate(cut + [w_key, w_value], 1)

    def chip_rows(of):
        mine, got = of(core), shift(of(other), "c")
        rows = pick(core, jnp.concatenate([mine, got], 0), jnp.concatenate([got, mine], 0))
        return jnp.concatenate([rows, shift(rows, "y")], 0)

    head_minor = gather_direct(chip_rows(heads_of), False)
    head_w = gather_ring(head_minor, True)
    w_gate, w_up, down_t, head_minor = lax.optimization_barrier((w_gate, w_up, down_t, head_minor))
    ffn_w = lax.all_gather(chip_rows(units_of), ("z", "x"), axis=0, tiled=True)
    gate_up_w, down_w = ffn_w[:, : 2 * padded], ffn_w[:, 2 * padded :]
    query_w, out_w = head_w[:, :HD], head_w[:, HD : 2 * HD]
    key_w, value_w, pair_w = head_w[:, 2 * HD : 3 * HD], head_w[:, 3 * HD :], head_w[:, 2 * HD :]

    place = jnp.arange(width, dtype=jnp.int32)
    first, second = place // quarter, place // (quarter // 4) % 4
    tail_y, tail = place // (2 * piece) % 2, place % (2 * piece)

    def natural(z_at, x_at):
        return ((y + tail_y) % 2) * (width // 2) + z_at * (8 * piece) + x_at * (2 * piece) + tail

    by_gather = natural(first, second)
    by_ring = natural((z + pick(core, second, first)) % 4, (x + pick(core, first, second)) % 4)

    def order(source, target):
        return (source[:, None] == target[None, :]).astype(BF)

    to_gather, to_ring = order(place, by_gather), order(place, by_ring)
    from_gather, from_ring = order(by_gather, place), order(by_ring, place)

    def reorder(values, moves):
        return matmul(values, moves).astype(BF)

    def both_cores(values):
        return jnp.concatenate([values, shift(values, "c")], 0)

    def sum_parts(partial, moves):
        low = reorder(partial.astype(BF), moves)
        chip = (low[:tokens].astype(F32) + shift(low[tokens:], "c").astype(F32)).astype(BF)
        return chip.astype(F32) + shift(chip, "s").astype(F32)

    offsets = jnp.arange(tokens, dtype=jnp.int32)

    def positions_of(places):
        return (block_order[places.reshape(-1)][:, None] * tokens + offsets[None, :]).reshape(-1)

    def device_of(y_at, z_at, x_at, core_at):
        return y_at * 32 + z_at * 8 + x_at * 2 + core_at

    steps = jnp.arange(4, dtype=jnp.int32)
    outer, inner = steps[:, None, None], steps[None, :, None]

    def keys_of(which):
        z_at, x_at = (z + pick(which, inner, outer)) % 4, (x + pick(which, outer, inner)) % 4
        return positions_of(device_of((y + steps[None, None, :2]) % 2, z_at, x_at, which))

    key_pos = [keys_of(core), keys_of(other)]
    own_pos = positions_of(device_of(y, z, x, core))
    chip_pos = jnp.concatenate([own_pos, positions_of(device_of(y, z, x, other))])
    cosine_table, sine_table = tables(chip_pos, HD)

    attn_val, pre_attn_back = jax.vjp(rms_scale, hidden_in, norm_gains[0])
    attn_chip = reorder(both_cores(attn_val.astype(BF)), to_ring)
    attn_ring = attn_chip[:tokens]
    key_pre = matmul(attn_ring, key_w)
    value_low = matmul(attn_ring, value_w).astype(BF)
    key_val, key_back = jax.vjp(
        lambda values, gain: rotate(rms_scale(values, gain), cosine_table[:tokens], sine_table[:tokens]),
        key_pre,
        head_gains[1],
    )
    key_low = key_val.astype(BF)
    pair_low = jnp.concatenate([key_low, value_low], 1)
    pair_rows = jnp.concatenate([pair_low, shift(pair_low, "y")], 0)
    own_pairs = gather_ring(gather_direct(pair_rows, False), True)
    pairs = [own_pairs, shift(own_pairs, "c")]

    query_pre = matmul(attn_chip, query_w)
    query_val, query_back = jax.vjp(
        lambda values, gain: rotate(rms_scale(values, gain), cosine_table, sine_table),
        query_pre,
        head_gains[0],
    )
    score_scale = HD ** (-0.5)
    queries = (query_val.astype(BF).astype(F32) * score_scale).astype(BF)
    parts = [attend(queries, pairs[part], key_pos[part], chip_pos) for part in range(2)]
    weights = [part[0] for part in parts]
    inverse_total = 1.0 / (parts[0][1] + parts[1][1])
    accum = parts[0][2] + parts[1][2]
    attn_rows = accum * inverse_total
    mixed_low = attn_rows.astype(BF)
    attn_out = sum_parts(inner_cols(mixed_low, out_w), from_ring)
    post_attn, post_attn_back = jax.vjp(rms_scale, attn_out, norm_gains[1])
    mid_state = hidden_in + post_attn

    ffn_val, ffn_norm_back = jax.vjp(rms_scale, mid_state, norm_gains[2])
    ffn_chip = both_cores(reorder(ffn_val.astype(BF), to_gather))
    gate_up = matmul(ffn_chip, gate_up_w)
    hidden_val, geglu_back = jax.vjp(geglu, gate_up[:, :padded], gate_up[:, padded:])
    hidden_low = hidden_val.astype(BF)
    ffn_out = sum_parts(inner_cols(hidden_low, down_w), from_gather)
    post_ffn, post_ffn_back = jax.vjp(rms_scale, ffn_out, norm_gains[3])
    block_out = mid_state + post_ffn

    ffn_grad, gain_four = post_ffn_back(out_grad)
    ffn_grad_chip = both_cores(reorder(ffn_grad.astype(BF), to_gather))
    gate_grad, up_grad = geglu_back(matmul(ffn_grad_chip, down_w))
    gate_up_low = jnp.concatenate([gate_grad.astype(BF), up_grad.astype(BF)], 1)
    ffn_norm_grad = sum_parts(inner_cols(gate_up_low, gate_up_w), from_gather)
    mid_from, gain_three = ffn_norm_back(ffn_norm_grad)
    mid_grad = out_grad + mid_from

    sources = jnp.concatenate([ffn_chip, ffn_grad_chip], 0)
    left = inner_cols(order(by_ring, by_gather), sources).astype(BF)
    ffn_chunks = ffn_wgrad(left, gate_up_low, hidden_low)

    def reduce_y(values):
        low = values.astype(BF)
        own, far = split_rows(low, 2)
        return own.astype(F32) + shift(far, "y").astype(F32)

    def swap_cores(rows):
        low = rows.astype(BF)
        first, second = split_rows(low, 2)
        return pick(core, first, second).astype(F32), shift(pick(core, second, first), "c").astype(F32)

    ffn_major = reduce_ring(*ffn_chunks, True).astype(BF)
    ffn_mine, ffn_got = swap_cores(reduce_y(reduce_rows(ffn_major, False)))

    def joined(start, size, mine, got):
        left, right = mine[:, start : start + size], got[:, start : start + size]
        return pick(core, jnp.concatenate([left, right], 1), jnp.concatenate([right, left], 1))

    gate_wgrad = joined(0, units, ffn_mine, ffn_got)
    up_wgrad = joined(padded, units, ffn_mine, ffn_got)
    down_wgrad = joined(2 * padded, units, ffn_mine, ffn_got).T

    attn_grad, gain_two = post_attn_back(mid_grad)
    attn_grad_chip = reorder(both_cores(attn_grad.astype(BF)), to_ring)
    rows_grad = matmul(attn_grad_chip, out_w).astype(BF)
    rows_wide = rows_grad.astype(F32)
    row_dot = jnp.sum(rows_wide * attn_rows, axis=1)[:, None]
    rows_scaled = (rows_wide * inverse_total).astype(BF)
    pair_far, query_far = attend_back(
        queries, pairs[1], weights[1], rows_grad, rows_scaled, row_dot, inverse_total
    )
    pair_near, query_near = attend_back(
        queries, pairs[0], weights[0], rows_grad, rows_scaled, row_dot, inverse_total
    )
    query_grad = query_far + query_near
    pair_sum = wide_sum(pair_near, shift(pair_far, "c")).astype(BF)
    pair_major = reduce_rows(pair_sum, True).astype(BF)
    pair_low = reduce_y(reduce_direct(split_rows(pair_major, 4), False)).astype(BF)
    pair_grad = pair_low.astype(F32) + shift(pair_low, "s").astype(F32)

    query_pre_grad, query_gain = query_back(query_grad * score_scale)
    query_gain = query_gain + shift(query_gain, "s")
    query_pre_low = query_pre_grad.astype(BF)
    attn_norm_sum = sum_parts(inner_cols(query_pre_low, query_w), from_ring)
    key_pre_grad, key_gain = key_back(pair_grad[:, :HD])
    key_pre_low = key_pre_grad.astype(BF)
    value_grad_low = pair_grad[:, HD:].astype(BF)
    pair_part = inner_cols(jnp.concatenate([key_pre_low, value_grad_low], 1), pair_w).astype(BF)
    attn_norm_grad = attn_norm_sum + reorder(pair_part, from_ring).astype(F32)
    input_from, gain_one = pre_attn_back(attn_norm_grad)
    input_grad = mid_grad + input_from

    kept, sent = pick(core, key_pre_low, value_grad_low), pick(core, value_grad_low, key_pre_low)
    pair_chip = jnp.concatenate([kept, shift(sent, "c")], 0)
    heads = [
        jnp.pad(gain.reshape(64, HD // 64), ((0, 0), (0, piece - HD // 64))).reshape(width)
        for gain in (query_gain, key_gain)
    ]
    gains = jnp.stack([gain_one, gain_two, gain_three, gain_four] + heads, 1)
    gains = jnp.pad(gains, ((0, 0), (0, 128 - gains.shape[1]))).astype(BF)
    head_grads_all = jnp.concatenate(
        [
            inner_rows(attn_chip, query_pre_low),
            inner_rows(attn_grad_chip, mixed_low),
            inner_rows(attn_chip, pair_chip),
            inner_rows(to_ring, gains),
        ],
        1,
    ).astype(BF)
    head_major = reduce_rows(head_grads_all, True).astype(BF)
    head_mine, head_got = swap_cores(reduce_y(reduce_direct(split_rows(head_major, 4), False)))
    query_wgrad = joined(0, HD, head_mine, head_got)
    out_wgrad = joined(HD, HD, head_mine, head_got).T
    pair_wgrad = joined(2 * HD, HD, head_mine, head_got)
    gain_sums = head_mine[:, 3 * HD :] + head_got[:, 3 * HD :]
    return (
        block_out,
        input_grad,
        query_wgrad,
        pair_wgrad[:, :HD],
        pair_wgrad[:, HD:],
        out_wgrad,
        gate_wgrad,
        up_wgrad,
        down_wgrad,
        gain_sums[:, :4].T,
        gain_sums[: HD // 64, 4:6].T,
    )


def solution(mesh):
    fine = Mesh(mesh.devices.reshape(2, 4, 4, 2, 2), ("y", "z", "x", "c", "s"))
    placed = (
        P(CTX, None),
        P(CTX, None),
        P(),
        P(),
        P(),
        P(CTX, "s"),
        P(CTX, None),
        P(CTX, None),
        P("s", CTX),
        P(CTX, "s"),
        P(CTX, "s"),
        P("s", CTX),
    )
    return jax.shard_map(
        shards,
        mesh=fine,
        in_specs=placed,
        out_specs=(
            P(CTX, None),
            P(CTX, None),
            P(CTX, "s"),
            P(CTX, None),
            P(CTX, None),
            P("s", CTX),
            P(CTX, "s"),
            P(CTX, "s"),
            P("s", CTX),
            P(None, CTX),
            P(None, CTX),
        ),
        check_vma=False,
    )
```

```python
import math

import jax
import jax.numpy as jnp
from jax import lax
from jax.experimental import pallas as pl
from jax.experimental.pallas import tpu as pltpu
from jax.sharding import Mesh, PartitionSpec as P

HD = 256
EPS = 1e-06
THETA = 1000000.0
BF = jnp.bfloat16
F32 = jnp.float32
CTX = ("y", "z", "x", "c")


def matmul(left, right):
    return jnp.dot(left, right, preferred_element_type=F32)


def inner_rows(left, right):
    return lax.dot_general(left, right, (((0,), (0,)), ((), ())), preferred_element_type=F32)


def inner_cols(left, right):
    return lax.dot_general(left, right, (((1,), (1,)), ((), ())), preferred_element_type=F32)


def rms_scale(values, gain):
    return values * lax.rsqrt(jnp.mean(values * values, axis=-1, keepdims=True) + EPS) * gain


def rotate(values, cosine_table, sine_table):
    half_width = values.shape[-1] // 2
    first = values[..., :half_width]
    second = values[..., half_width:]
    return jnp.concatenate(
        [first * cosine_table - second * sine_table, second * cosine_table + first * sine_table],
        axis=-1,
    )


def tables(positions, head_width):
    frequency = jnp.arange(head_width // 2, dtype=F32)
    inverse = jnp.exp(frequency * (-2.0 * math.log(THETA) / head_width))
    angles = positions.astype(F32)[:, None] * inverse[None, :]
    return (jnp.cos(angles), jnp.sin(angles))


def shift(values, axis, step=1):
    size = lax.axis_size(axis)
    return lax.ppermute(values, axis, [(i, (i + step) % size) for i in range(size)])


def ring(values, major, step):
    moves = []
    for z in range(4):
        for x in range(4):
            for core in range(2):
                along_x = major == (core == 0)
                to_z, to_x = (z, (x + step) % 4) if along_x else ((z + step) % 4, x)
                moves.append((z * 8 + x * 2 + core, to_z * 8 + to_x * 2 + core))
    return lax.ppermute(values, ("z", "x", "c"), moves)


def gather_direct(block, major):
    return jnp.concatenate([block] + [ring(block, major, -k) for k in (1, 2, 3)], 0)


def after(value, *others):
    return lax.optimization_barrier((value, *others))[0]


def gather_ring(block, major, *others):
    half = (block.shape[0] // 2 + 7) // 8 * 8
    previous = ring(block, major, 1)
    following = ring(block, major, -1)
    far_low = ring(after(previous, *others)[:half], major, 1)
    far_high = ring(after(following, *others)[half:], major, -1)
    return [block, following, far_low, far_high, previous]


def wide_sum(*parts):
    return sum(part.astype(F32) for part in parts)


def reduce_direct(chunks, major):
    return wide_sum(chunks[0], *[ring(chunks[k], major, k) for k in (1, 2, 3)])


def reduce_ring(own, following, far_low, far_high, previous, major, *others):
    half = far_low.shape[0]
    from_previous = after(ring(far_low, major, 1), *others)
    from_next = after(ring(far_high, major, -1), *others)
    forward = jnp.concatenate(
        [wide_sum(following[:half], from_previous).astype(BF), following[half:]], 0
    )
    backward = jnp.concatenate(
        [previous[:half], wide_sum(previous[half:], from_next).astype(BF)], 0
    )
    return wide_sum(own, ring(forward, major, 1), ring(backward, major, -1))


def reduce_rows(values, major):
    own, following, far, previous = split_rows(values, 4)
    half = (far.shape[0] // 2 + 7) // 8 * 8
    return reduce_ring(own, following, far[:half], far[half:], previous, major)


ATTN_BLOCK = 1024
VMEM = pltpu.CompilerParams(vmem_limit_bytes=48 * 1024 * 1024)


def attend_kernel(query, pair, key_pos, query_pos, weight, total, accum):
    scores = inner_cols(query[...], pair[:, :HD])
    exps = jnp.where(query_pos[...] >= key_pos[...], jnp.exp(scores), 0.0)
    low = exps.astype(BF)
    weight[...] = low

    @pl.when(pl.program_id(0) == 0)
    def _():
        total[...] = jnp.zeros_like(total)
        accum[...] = jnp.zeros_like(accum)

    total[...] += jnp.sum(exps, axis=1, keepdims=True)
    accum[...] += matmul(low, pair[:, HD:])


def attend(queries, pairs, key_pos, query_pos):
    rows, keys = queries.shape[0], pairs.shape[0]
    whole = lambda i: (0, 0)
    return pl.pallas_call(
        attend_kernel,
        grid=(keys // ATTN_BLOCK,),
        in_specs=[
            pl.BlockSpec((rows, HD), whole),
            pl.BlockSpec((ATTN_BLOCK, 2 * HD), lambda i: (i, 0)),
            pl.BlockSpec((1, ATTN_BLOCK), lambda i: (0, i)),
            pl.BlockSpec((rows, 1), whole),
        ],
        out_specs=[
            pl.BlockSpec((rows, ATTN_BLOCK), lambda i: (0, i)),
            pl.BlockSpec((rows, 1), whole),
            pl.BlockSpec((rows, HD), whole),
        ],
        out_shape=[
            jax.ShapeDtypeStruct((rows, keys), BF),
            jax.ShapeDtypeStruct((rows, 1), F32),
            jax.ShapeDtypeStruct((rows, HD), F32),
        ],
        compiler_params=VMEM,
        name="attend",
    )(queries, pairs, key_pos[None, :], query_pos[:, None])


def attend_back_kernel(query, pair, weight, grad, scaled, dot, inverse, pair_grad, query_grad):
    weights = weight[...]
    prob_grad = inner_cols(grad[...], pair[:, HD:])
    score_grad = (weights.astype(F32) * ((prob_grad - dot[...]) * inverse[...])).astype(BF)
    pair_grad[:, :HD] = inner_rows(score_grad, query[...]).astype(BF)
    pair_grad[:, HD:] = inner_rows(weights, scaled[...]).astype(BF)

    @pl.when(pl.program_id(0) == 0)
    def _():
        query_grad[...] = jnp.zeros_like(query_grad)

    query_grad[...] += matmul(score_grad, pair[:, :HD])


def attend_back(queries, pairs, weights, grads, scaled, dot, inverse):
    rows, keys = queries.shape[0], pairs.shape[0]
    whole = lambda i: (0, 0)
    return pl.pallas_call(
        attend_back_kernel,
        grid=(keys // ATTN_BLOCK,),
        in_specs=[
            pl.BlockSpec((rows, HD), whole),
            pl.BlockSpec((ATTN_BLOCK, 2 * HD), lambda i: (i, 0)),
            pl.BlockSpec((rows, ATTN_BLOCK), lambda i: (0, i)),
            pl.BlockSpec((rows, HD), whole),
            pl.BlockSpec((rows, HD), whole),
            pl.BlockSpec((rows, 1), whole),
            pl.BlockSpec((rows, 1), whole),
        ],
        out_specs=[
            pl.BlockSpec((ATTN_BLOCK, 2 * HD), lambda i: (i, 0)),
            pl.BlockSpec((rows, HD), whole),
        ],
        out_shape=[
            jax.ShapeDtypeStruct((keys, 2 * HD), BF),
            jax.ShapeDtypeStruct((rows, HD), F32),
        ],
        compiler_params=VMEM,
        name="attend_back",
    )(queries, pairs, weights, grads, scaled, dot, inverse)


def stack_kernel(*refs):
    start = 0
    for piece in refs[:-1]:
        refs[-1][start : start + piece.shape[0], :] = piece[...]
        start += piece.shape[0]


def stack_rows(pieces, tile=256):
    rows, columns = sum(piece.shape[0] for piece in pieces), pieces[0].shape[1]
    return pl.pallas_call(
        stack_kernel,
        grid=(columns // tile,),
        in_specs=[pl.BlockSpec((piece.shape[0], tile), lambda j: (0, j)) for piece in pieces],
        out_specs=pl.BlockSpec((rows, tile), lambda j: (0, j)),
        out_shape=jax.ShapeDtypeStruct((rows, columns), pieces[0].dtype),
        compiler_params=VMEM,
        name="stack_rows",
    )(*pieces)


UNIT_TILE = 256
GELU_IN = math.sqrt(2.0 / math.pi)
GELU_CUBE = 0.044715


def joined_rows(refs):
    return jnp.concatenate([ref[...] for ref in refs], 0)


def ffn_kernel(source, *refs):
    count = (len(refs) - 4) // 3
    gate_w, up_w, down_w = (joined_rows(refs[i * count : (i + 1) * count]) for i in range(3))
    gate, up, hidden, total = refs[3 * count :]
    gate_pre = matmul(source[...], gate_w)
    up_pre = matmul(source[...], up_w)
    gate[...] = gate_pre
    up[...] = up_pre
    inner = GELU_IN * (gate_pre + GELU_CUBE * (gate_pre * gate_pre * gate_pre))
    low = (0.5 * gate_pre * (1.0 + jnp.tanh(inner)) * up_pre).astype(BF)
    hidden[...] = low

    @pl.when(pl.program_id(0) == 0)
    def _():
        total[...] = jnp.zeros_like(total)

    total[...] += inner_cols(low, down_w)


def ffn_back_kernel(grad, gate, up, *refs):
    count = (len(refs) - 3) // 3
    gate_w, up_w, down_w = (joined_rows(refs[i * count : (i + 1) * count]) for i in range(3))
    gate_grad, up_grad, total = refs[3 * count :]
    hidden_grad = matmul(grad[...], down_w)
    gate_pre = gate[...]
    square = gate_pre * gate_pre
    bend = jnp.tanh(GELU_IN * (gate_pre + GELU_CUBE * (square * gate_pre)))
    rise = 0.5 * (1.0 + bend)
    slope = rise + 0.5 * gate_pre * (1.0 - bend * bend) * (GELU_IN * (1.0 + 3.0 * GELU_CUBE * square))
    gate_low = (hidden_grad * up[...] * slope).astype(BF)
    up_low = (hidden_grad * (gate_pre * rise)).astype(BF)
    gate_grad[...] = gate_low
    up_grad[...] = up_low

    @pl.when(pl.program_id(0) == 0)
    def _():
        total[...] = jnp.zeros_like(total)

    total[...] += inner_cols(gate_low, gate_w) + inner_cols(up_low, up_w)


def unit_specs(rows, pieces, tiles):
    own = pl.BlockSpec((rows, UNIT_TILE), lambda j: (0, j))
    weights = [
        pl.BlockSpec((piece.shape[0], UNIT_TILE), lambda j, i=i: (0, j + i * tiles))
        for i in range(3)
        for piece in pieces
    ]
    return own, weights


def ffn_forward(source, pieces):
    rows, width = source.shape
    units = pieces[0].shape[1] // 3
    tiles = units // UNIT_TILE
    own, weights = unit_specs(rows, pieces, tiles)
    whole = pl.BlockSpec((rows, width), lambda j: (0, 0))
    return pl.pallas_call(
        ffn_kernel,
        grid=(tiles,),
        in_specs=[whole] + weights,
        out_specs=[own, own, own, whole],
        out_shape=[
            jax.ShapeDtypeStruct((rows, units), F32),
            jax.ShapeDtypeStruct((rows, units), F32),
            jax.ShapeDtypeStruct((rows, units), BF),
            jax.ShapeDtypeStruct((rows, width), F32),
        ],
        compiler_params=VMEM,
        name="ffn_forward",
    )(source, *pieces, *pieces, *pieces)


def ffn_backward(grad, gate, up, pieces):
    rows, width = grad.shape
    units = pieces[0].shape[1] // 3
    tiles = units // UNIT_TILE
    own, weights = unit_specs(rows, pieces, tiles)
    whole = pl.BlockSpec((rows, width), lambda j: (0, 0))
    return pl.pallas_call(
        ffn_back_kernel,
        grid=(tiles,),
        in_specs=[whole, own, own] + weights,
        out_specs=[own, own, whole],
        out_shape=[
            jax.ShapeDtypeStruct((rows, units), BF),
            jax.ShapeDtypeStruct((rows, units), BF),
            jax.ShapeDtypeStruct((rows, width), F32),
        ],
        compiler_params=VMEM,
        name="ffn_backward",
    )(grad, gate, up, *pieces, *pieces, *pieces)


def ffn_wgrad_kernel(steps, left, gate, up, hidden, *outs):
    rows = gate.shape[0]

    def store(first, right):
        start = 0
        for out in outs:
            size = out.shape[0]
            out[...] = matmul(left[start : start + size, first : first + rows], right[...]).astype(BF)
            start += size

    for i, (first, right) in enumerate([(0, gate), (0, up), (rows, hidden)]):
        pl.when(pl.program_id(0) // steps == i)(lambda first=first, right=right: store(first, right))


def ffn_wgrad(left, gate, up, hidden):
    width, (rows, units) = left.shape[0], gate.shape
    steps = 2
    tile = units // steps
    sizes = [width // 4, width // 4, width // 8, width // 8, width // 4]

    def right(i):
        return pl.BlockSpec((rows, tile), lambda j: (0, jnp.clip(j - i * steps, 0, steps - 1)))

    return pl.pallas_call(
        lambda *refs: ffn_wgrad_kernel(steps, *refs),
        grid=(3 * steps,),
        in_specs=[pl.BlockSpec(left.shape, lambda j: (0, 0)), right(0), right(1), right(2)],
        out_specs=[pl.BlockSpec((size, tile), lambda j: (0, j)) for size in sizes],
        out_shape=[jax.ShapeDtypeStruct((size, 3 * units), BF) for size in sizes],
        compiler_params=VMEM,
        name="ffn_wgrad",
    )(left, gate, up, hidden)


def split_rows(values, parts):
    size = values.shape[0] // parts
    return [values[i * size : (i + 1) * size] for i in range(parts)]


def pick(core, first, second):
    return jnp.where(core == 0, first, second)


def shards(
    hidden_in,
    out_grad,
    block_order,
    norm_gains,
    head_gains,
    w_query,
    w_key,
    w_value,
    w_out,
    w_gate,
    w_up,
    w_down,
):
    tokens, width = hidden_in.shape
    y, z, x, core = (lax.axis_index(name) for name in CTX)
    other = 1 - core
    piece = width // 64
    units = w_gate.shape[1] // 2
    padded = (units + 127) // 128 * 128
    quarter = width // 4

    out_t, down_t = w_out.T, w_down.T

    def units_of(which):
        cut = [
            jnp.pad(lax.dynamic_slice_in_dim(w, which * units, units, 1), ((0, 0), (0, padded - units)))
            for w in (w_gate, w_up, down_t)
        ]
        return jnp.concatenate(cut, 1)

    def heads_of(which):
        cut = [lax.dynamic_slice_in_dim(w, which * HD, HD, 1) for w in (w_query, out_t)]
        return jnp.concatenate(cut + [w_key, w_value], 1)

    def chip_rows(of):
        mine, got = of(core), shift(of(other), "c")
        rows = pick(core, jnp.concatenate([mine, got], 0), jnp.concatenate([got, mine], 0))
        return jnp.concatenate([rows, shift(rows, "y")], 0)

    head_minor = gather_direct(chip_rows(heads_of), False)
    head_w = stack_rows(gather_ring(head_minor, True))
    ffn_rows = after(chip_rows(units_of), head_minor)
    ffn_minor = after(jnp.concatenate(gather_ring(ffn_rows, False), 0), head_w)
    query_w, out_w = head_w[:, :HD], head_w[:, HD : 2 * HD]
    key_w, value_w, pair_w = head_w[:, 2 * HD : 3 * HD], head_w[:, 3 * HD :], head_w[:, 2 * HD :]

    place = jnp.arange(width, dtype=jnp.int32)
    first, second = place // quarter, place // (quarter // 4) % 4
    z_at, x_at = (z + pick(core, second, first)) % 4, (x + pick(core, first, second)) % 4
    y_at = (y + place // (2 * piece)) % 2
    by_ring = y_at * (width // 2) + z_at * (8 * piece) + x_at * (2 * piece) + place % (2 * piece)
    to_ring = (place[:, None] == by_ring[None, :]).astype(BF)
    from_ring = (by_ring[:, None] == place[None, :]).astype(BF)

    def reorder(values, moves):
        return matmul(values, moves).astype(BF)

    def both_cores(values):
        return jnp.concatenate([values, shift(values, "c")], 0)

    def sum_parts(partial):
        low = reorder(partial.astype(BF), from_ring)
        chip = (low[:tokens].astype(F32) + shift(low[tokens:], "c").astype(F32)).astype(BF)
        return chip.astype(F32) + shift(chip, "s").astype(F32)

    offsets = jnp.arange(tokens, dtype=jnp.int32)

    def positions_of(places):
        return (block_order[places.reshape(-1)][:, None] * tokens + offsets[None, :]).reshape(-1)

    def device_of(y_at, z_at, x_at, core_at):
        return y_at * 32 + z_at * 8 + x_at * 2 + core_at

    steps = jnp.arange(4, dtype=jnp.int32)
    outer, inner = steps[:, None, None], steps[None, :, None]

    def keys_of(which):
        z_at, x_at = (z + pick(which, inner, outer)) % 4, (x + pick(which, outer, inner)) % 4
        return positions_of(device_of((y + steps[None, None, :2]) % 2, z_at, x_at, which))

    key_pos = [keys_of(core), keys_of(other)]
    own_pos = positions_of(device_of(y, z, x, core))
    chip_pos = jnp.concatenate([own_pos, positions_of(device_of(y, z, x, other))])
    cosine_table, sine_table = tables(chip_pos, HD)

    attn_val, pre_attn_back = jax.vjp(rms_scale, hidden_in, norm_gains[0])
    attn_chip = reorder(both_cores(attn_val.astype(BF)), to_ring)
    attn_ring = attn_chip[:tokens]
    key_pre = matmul(attn_ring, key_w)
    value_low = matmul(attn_ring, value_w).astype(BF)
    key_val, key_back = jax.vjp(
        lambda values, gain: rotate(rms_scale(values, gain), cosine_table[:tokens], sine_table[:tokens]),
        key_pre,
        head_gains[1],
    )
    key_low = key_val.astype(BF)
    pair_low = jnp.concatenate([key_low, value_low], 1)
    pair_rows = jnp.concatenate([pair_low, shift(pair_low, "y")], 0)
    own_pairs = jnp.concatenate(gather_ring(gather_direct(pair_rows, False), True), 0)
    ffn_w = gather_ring(ffn_minor, True, own_pairs)
    pairs = [own_pairs, shift(own_pairs, "c")]

    query_pre = matmul(attn_chip, query_w)
    query_val, query_back = jax.vjp(
        lambda values, gain: rotate(rms_scale(values, gain), cosine_table, sine_table),
        query_pre,
        head_gains[0],
    )
    score_scale = HD ** (-0.5)
    queries = (query_val.astype(BF).astype(F32) * score_scale).astype(BF)
    parts = [attend(queries, pairs[part], key_pos[part], chip_pos) for part in range(2)]
    weights = [part[0] for part in parts]
    inverse_total = 1.0 / (parts[0][1] + parts[1][1])
    accum = parts[0][2] + parts[1][2]
    attn_rows = accum * inverse_total
    mixed_low = attn_rows.astype(BF)
    attn_out = sum_parts(inner_cols(mixed_low, out_w))
    post_attn, post_attn_back = jax.vjp(rms_scale, attn_out, norm_gains[1])
    mid_state = hidden_in + post_attn

    ffn_val, ffn_norm_back = jax.vjp(rms_scale, mid_state, norm_gains[2])
    ffn_chip = both_cores(ffn_val.astype(BF))
    gate_pre, up_pre, hidden_low, ffn_part = ffn_forward(reorder(ffn_chip, to_ring), ffn_w)
    ffn_out = sum_parts(ffn_part)
    post_ffn, post_ffn_back = jax.vjp(rms_scale, ffn_out, norm_gains[3])
    block_out = mid_state + post_ffn

    ffn_grad, gain_four = post_ffn_back(out_grad)
    ffn_grad_chip = both_cores(ffn_grad.astype(BF))
    gate_low, up_low, ffn_norm_part = ffn_backward(reorder(ffn_grad_chip, to_ring), gate_pre, up_pre, ffn_w)
    ffn_norm_grad = sum_parts(ffn_norm_part)
    mid_from, gain_three = ffn_norm_back(ffn_norm_grad)
    mid_grad = out_grad + mid_from

    sources = jnp.concatenate([ffn_chip, ffn_grad_chip], 0)
    left = inner_cols(from_ring, sources).astype(BF)
    ffn_chunks = ffn_wgrad(left, gate_low, up_low, hidden_low)

    def exchange(values, axis):
        both = [(i, 3 - i) for i in range(4)]
        return shift(values[0], "y"), shift(values[1], axis), lax.ppermute(values[2], ("y", axis), both)

    def last_stage(values):
        parts = split_rows(values.astype(BF), 4)
        kept = [pick(core, parts[i], parts[i + 1]) for i in (0, 2)]
        sent = [pick(core, parts[i + 1], parts[i]) for i in (0, 2)]
        from_y, from_core, from_both = exchange((kept[1], sent[0], sent[1]), "c")
        return wide_sum(kept[0], from_y), wide_sum(from_core, from_both)

    ffn_major = reduce_ring(*ffn_chunks, True, ffn_norm_grad).astype(BF)
    ffn_mine, ffn_got = last_stage(reduce_rows(ffn_major, False))

    def joined(start, size, mine, got):
        left, right = mine[:, start : start + size], got[:, start : start + size]
        return pick(core, jnp.concatenate([left, right], 1), jnp.concatenate([right, left], 1))

    gate_wgrad = joined(0, units, ffn_mine, ffn_got)
    up_wgrad = joined(padded, units, ffn_mine, ffn_got)
    down_wgrad = joined(2 * padded, units, ffn_mine, ffn_got).T

    attn_grad, gain_two = post_attn_back(mid_grad)
    attn_grad_chip = reorder(both_cores(attn_grad.astype(BF)), to_ring)
    rows_grad = matmul(attn_grad_chip, out_w).astype(BF)
    rows_wide = rows_grad.astype(F32)
    row_dot = jnp.sum(rows_wide * attn_rows, axis=1)[:, None]
    rows_scaled = (rows_wide * inverse_total).astype(BF)
    pair_far, query_far = attend_back(
        queries, pairs[1], weights[1], rows_grad, rows_scaled, row_dot, inverse_total
    )
    pair_near, query_near = attend_back(
        queries, pairs[0], weights[0], rows_grad, rows_scaled, row_dot, inverse_total
    )
    query_grad = query_far + query_near
    pair_sum = wide_sum(pair_near, shift(pair_far, "c")).astype(BF)
    pair_major = reduce_rows(pair_sum, True).astype(BF)
    pair_own, pair_far_y = split_rows(reduce_direct(split_rows(pair_major, 4), False).astype(BF), 2)
    from_y, from_shard, from_both = exchange((pair_far_y, pair_own, pair_far_y), "s")
    pair_grad = wide_sum(pair_own, from_y) + wide_sum(from_shard, from_both)

    query_pre_grad, query_gain = query_back(query_grad * score_scale)
    query_gain = query_gain + shift(query_gain, "s")
    query_pre_low = query_pre_grad.astype(BF)
    attn_norm_sum = sum_parts(inner_cols(query_pre_low, query_w))
    key_pre_grad, key_gain = key_back(pair_grad[:, :HD])
    key_pre_low = key_pre_grad.astype(BF)
    value_grad_low = pair_grad[:, HD:].astype(BF)
    pair_part = inner_cols(jnp.concatenate([key_pre_low, value_grad_low], 1), pair_w).astype(BF)
    attn_norm_grad = attn_norm_sum + reorder(pair_part, from_ring).astype(F32)
    input_from, gain_one = pre_attn_back(attn_norm_grad)
    input_grad = mid_grad + input_from

    kept, sent = pick(core, key_pre_low, value_grad_low), pick(core, value_grad_low, key_pre_low)
    pair_chip = jnp.concatenate([kept, shift(sent, "c")], 0)
    heads = [
        jnp.pad(gain.reshape(64, HD // 64), ((0, 0), (0, piece - HD // 64))).reshape(width)
        for gain in (query_gain, key_gain)
    ]
    gains = jnp.stack([gain_one, gain_two, gain_three, gain_four] + heads, 1)
    gains = jnp.pad(gains, ((0, 0), (0, 128 - gains.shape[1]))).astype(BF)
    head_grads_all = jnp.concatenate(
        [
            inner_rows(attn_chip, query_pre_low),
            inner_rows(attn_grad_chip, mixed_low),
            inner_rows(attn_chip, pair_chip),
            inner_rows(to_ring, gains),
        ],
        1,
    ).astype(BF)
    head_major = reduce_rows(head_grads_all, True).astype(BF)
    head_mine, head_got = last_stage(reduce_direct(split_rows(head_major, 4), False))
    query_wgrad = joined(0, HD, head_mine, head_got)
    out_wgrad = joined(HD, HD, head_mine, head_got).T
    pair_wgrad = joined(2 * HD, HD, head_mine, head_got)
    gain_sums = head_mine[:, 3 * HD :] + head_got[:, 3 * HD :]
    return (
        block_out,
        input_grad,
        query_wgrad,
        pair_wgrad[:, :HD],
        pair_wgrad[:, HD:],
        out_wgrad,
        gate_wgrad,
        up_wgrad,
        down_wgrad,
        gain_sums[:, :4].T,
        gain_sums[: HD // 64, 4:6].T,
    )


def solution(mesh):
    fine = Mesh(mesh.devices.reshape(2, 4, 4, 2, 2), ("y", "z", "x", "c", "s"))
    placed = (
        P(CTX, None),
        P(CTX, None),
        P(),
        P(),
        P(),
        P(CTX, "s"),
        P(CTX, None),
        P(CTX, None),
        P("s", CTX),
        P(CTX, "s"),
        P(CTX, "s"),
        P("s", CTX),
    )
    return jax.shard_map(
        shards,
        mesh=fine,
        in_specs=placed,
        out_specs=(
            P(CTX, None),
            P(CTX, None),
            P(CTX, "s"),
            P(CTX, None),
            P(CTX, None),
            P("s", CTX),
            P(CTX, "s"),
            P(CTX, "s"),
            P("s", CTX),
            P(None, CTX),
            P(None, CTX),
        ),
        check_vma=False,
    )
```

```python
import math

import jax
import jax.numpy as jnp
from jax import lax
from jax.experimental import pallas as pl
from jax.experimental.pallas import tpu as pltpu
from jax.sharding import Mesh, PartitionSpec as P

HD = 256
EPS = 1e-06
THETA = 1000000.0
BF = jnp.bfloat16
F32 = jnp.float32
CTX = ("y", "z", "x", "c")


def matmul(left, right):
    return jnp.dot(left, right, preferred_element_type=F32)


def inner_rows(left, right):
    return lax.dot_general(left, right, (((0,), (0,)), ((), ())), preferred_element_type=F32)


def inner_cols(left, right):
    return lax.dot_general(left, right, (((1,), (1,)), ((), ())), preferred_element_type=F32)


def rms_scale(values, gain):
    return values * lax.rsqrt(jnp.mean(values * values, axis=-1, keepdims=True) + EPS) * gain


def rotate(values, cosine_table, sine_table):
    half_width = values.shape[-1] // 2
    first = values[..., :half_width]
    second = values[..., half_width:]
    return jnp.concatenate(
        [first * cosine_table - second * sine_table, second * cosine_table + first * sine_table],
        axis=-1,
    )


def tables(positions, head_width):
    frequency = jnp.arange(head_width // 2, dtype=F32)
    inverse = jnp.exp(frequency * (-2.0 * math.log(THETA) / head_width))
    angles = positions.astype(F32)[:, None] * inverse[None, :]
    return (jnp.cos(angles), jnp.sin(angles))


def shift(values, axis, step=1):
    size = lax.axis_size(axis)
    return lax.ppermute(values, axis, [(i, (i + step) % size) for i in range(size)])


def ring(values, major, step, cross_y=False):
    moves = []
    for y in range(2):
        for z in range(4):
            for x in range(4):
                for core in range(2):
                    along_x = major == (core == 0)
                    to_z, to_x = (z, (x + step) % 4) if along_x else ((z + step) % 4, x)
                    to_y = 1 - y if cross_y else y
                    moves.append((y * 32 + z * 8 + x * 2 + core, to_y * 32 + to_z * 8 + to_x * 2 + core))
    return lax.ppermute(values, CTX, moves)


def gather_direct(block, major):
    return jnp.concatenate([block] + [ring(block, major, -k) for k in (1, 2, 3)], 0)


def gather_minor_y(block):
    blocks = [block if k == 0 else ring(block, False, -k) for k in range(4)]
    others = [ring(block, False, -k, True) for k in range(4)]
    return jnp.concatenate([part for pair in zip(blocks, others) for part in pair], 0)


def exchange(values, axis):
    both = [(i, 3 - i) for i in range(4)]
    return shift(values[0], "y"), shift(values[1], axis), lax.ppermute(values[2], ("y", axis), both)


def after(value, *others):
    return lax.optimization_barrier((value, *others))[0]


def gather_ring(block, major, *others):
    half = (block.shape[0] // 2 + 7) // 8 * 8
    previous = ring(block, major, 1)
    following = ring(block, major, -1)
    far_low = ring(after(previous, *others)[:half], major, 1)
    far_high = ring(after(following, *others)[half:], major, -1)
    return [block, following, far_low, far_high, previous]


def wide_sum(*parts):
    return sum(part.astype(F32) for part in parts)


def reduce_direct(chunks, major):
    return wide_sum(chunks[0], *[ring(chunks[k], major, k) for k in (1, 2, 3)])


def reduce_ring(own, following, far_low, far_high, previous, major, others=(), last=()):
    half = far_low.shape[0]
    from_previous = after(ring(far_low, major, 1), *others)
    from_next = after(ring(far_high, major, -1), *others)
    forward = jnp.concatenate(
        [wide_sum(following[:half], from_previous).astype(BF), following[half:]], 0
    )
    backward = jnp.concatenate(
        [previous[:half], wide_sum(previous[half:], from_next).astype(BF)], 0
    )
    return wide_sum(after(own, *last), ring(forward, major, 1), ring(backward, major, -1))


def reduce_chunks(own, following, far, previous, major):
    half = (far.shape[0] // 2 + 7) // 8 * 8
    return reduce_ring(own, following, far[:half], far[half:], previous, major)


ATTN_BLOCK = 1024
VMEM = pltpu.CompilerParams(vmem_limit_bytes=48 * 1024 * 1024)


def attend_kernel(query, pair, key_pos, query_pos, weight, total, accum):
    scores = inner_cols(query[...], pair[:, :HD])
    exps = jnp.where(query_pos[...] >= key_pos[...], jnp.exp(scores), 0.0)
    low = exps.astype(BF)
    weight[...] = low

    @pl.when(pl.program_id(0) == 0)
    def _():
        total[...] = jnp.zeros_like(total)
        accum[...] = jnp.zeros_like(accum)

    total[...] += jnp.sum(exps, axis=1, keepdims=True)
    accum[...] += matmul(low, pair[:, HD:])


def attend(queries, pairs, key_pos, query_pos):
    rows, keys = queries.shape[0], pairs.shape[0]
    whole = lambda i: (0, 0)
    return pl.pallas_call(
        attend_kernel,
        grid=(keys // ATTN_BLOCK,),
        in_specs=[
            pl.BlockSpec((rows, HD), whole),
            pl.BlockSpec((ATTN_BLOCK, 2 * HD), lambda i: (i, 0)),
            pl.BlockSpec((1, ATTN_BLOCK), lambda i: (0, i)),
            pl.BlockSpec((rows, 1), whole),
        ],
        out_specs=[
            pl.BlockSpec((rows, ATTN_BLOCK), lambda i: (0, i)),
            pl.BlockSpec((rows, 1), whole),
            pl.BlockSpec((rows, HD), whole),
        ],
        out_shape=[
            jax.ShapeDtypeStruct((rows, keys), BF),
            jax.ShapeDtypeStruct((rows, 1), F32),
            jax.ShapeDtypeStruct((rows, HD), F32),
        ],
        compiler_params=VMEM,
        name="attend",
    )(queries, pairs, key_pos[None, :], query_pos[:, None])


def attend_back_kernel(query, pair, weight, grad, scaled, dot, inverse, pair_grad, query_grad):
    weights = weight[...]
    prob_grad = inner_cols(grad[...], pair[:, HD:])
    score_grad = (weights.astype(F32) * ((prob_grad - dot[...]) * inverse[...])).astype(BF)
    pair_grad[:, :HD] = inner_rows(score_grad, query[...]).astype(BF)
    pair_grad[:, HD:] = inner_rows(weights, scaled[...]).astype(BF)

    @pl.when(pl.program_id(0) == 0)
    def _():
        query_grad[...] = jnp.zeros_like(query_grad)

    query_grad[...] += matmul(score_grad, pair[:, :HD])


def attend_back(queries, pairs, weights, grads, scaled, dot, inverse):
    rows, keys = queries.shape[0], pairs.shape[0]
    whole = lambda i: (0, 0)
    return pl.pallas_call(
        attend_back_kernel,
        grid=(keys // ATTN_BLOCK,),
        in_specs=[
            pl.BlockSpec((rows, HD), whole),
            pl.BlockSpec((ATTN_BLOCK, 2 * HD), lambda i: (i, 0)),
            pl.BlockSpec((rows, ATTN_BLOCK), lambda i: (0, i)),
            pl.BlockSpec((rows, HD), whole),
            pl.BlockSpec((rows, HD), whole),
            pl.BlockSpec((rows, 1), whole),
            pl.BlockSpec((rows, 1), whole),
        ],
        out_specs=[
            pl.BlockSpec((ATTN_BLOCK, 2 * HD), lambda i: (i, 0)),
            pl.BlockSpec((rows, HD), whole),
        ],
        out_shape=[
            jax.ShapeDtypeStruct((keys, 2 * HD), BF),
            jax.ShapeDtypeStruct((rows, HD), F32),
        ],
        compiler_params=VMEM,
        name="attend_back",
    )(queries, pairs, weights, grads, scaled, dot, inverse)


def stack_kernel(*refs):
    start = 0
    for piece in refs[:-1]:
        refs[-1][start : start + piece.shape[0], :] = piece[...]
        start += piece.shape[0]


def stack_rows(pieces, tile=256):
    rows, columns = sum(piece.shape[0] for piece in pieces), pieces[0].shape[1]
    return pl.pallas_call(
        stack_kernel,
        grid=(columns // tile,),
        in_specs=[pl.BlockSpec((piece.shape[0], tile), lambda j: (0, j)) for piece in pieces],
        out_specs=pl.BlockSpec((rows, tile), lambda j: (0, j)),
        out_shape=jax.ShapeDtypeStruct((rows, columns), pieces[0].dtype),
        compiler_params=VMEM,
        name="stack_rows",
    )(*pieces)


UNIT_TILE = 256
GELU_IN = math.sqrt(2.0 / math.pi)
GELU_CUBE = 0.044715


def joined_rows(refs):
    return jnp.concatenate([ref[...] for ref in refs], 0)


def ffn_kernel(source, *refs):
    count = (len(refs) - 4) // 3
    gate_w, up_w, down_w = (joined_rows(refs[i * count : (i + 1) * count]) for i in range(3))
    gate, up, hidden, total = refs[3 * count :]
    gate_pre = matmul(source[...], gate_w)
    up_pre = matmul(source[...], up_w)
    gate[...] = gate_pre
    up[...] = up_pre
    inner = GELU_IN * (gate_pre + GELU_CUBE * (gate_pre * gate_pre * gate_pre))
    low = (0.5 * gate_pre * (1.0 + jnp.tanh(inner)) * up_pre).astype(BF)
    hidden[...] = low

    @pl.when(pl.program_id(0) == 0)
    def _():
        total[...] = jnp.zeros_like(total)

    total[...] += inner_cols(low, down_w)


def ffn_back_kernel(grad, gate, up, *refs):
    count = (len(refs) - 3) // 3
    gate_w, up_w, down_w = (joined_rows(refs[i * count : (i + 1) * count]) for i in range(3))
    gate_grad, up_grad, total = refs[3 * count :]
    hidden_grad = matmul(grad[...], down_w)
    gate_pre = gate[...]
    square = gate_pre * gate_pre
    bend = jnp.tanh(GELU_IN * (gate_pre + GELU_CUBE * (square * gate_pre)))
    rise = 0.5 * (1.0 + bend)
    slope = rise + 0.5 * gate_pre * (1.0 - bend * bend) * (GELU_IN * (1.0 + 3.0 * GELU_CUBE * square))
    gate_low = (hidden_grad * up[...] * slope).astype(BF)
    up_low = (hidden_grad * (gate_pre * rise)).astype(BF)
    gate_grad[...] = gate_low
    up_grad[...] = up_low

    @pl.when(pl.program_id(0) == 0)
    def _():
        total[...] = jnp.zeros_like(total)

    total[...] += inner_cols(gate_low, gate_w) + inner_cols(up_low, up_w)


def unit_specs(rows, pieces, tiles):
    own = pl.BlockSpec((rows, UNIT_TILE), lambda j: (0, j))
    weights = [
        pl.BlockSpec((piece.shape[0], UNIT_TILE), lambda j, i=i: (0, j + i * tiles))
        for i in range(3)
        for piece in pieces
    ]
    return own, weights


def ffn_forward(source, pieces):
    rows, width = source.shape
    units = pieces[0].shape[1] // 3
    tiles = units // UNIT_TILE
    own, weights = unit_specs(rows, pieces, tiles)
    whole = pl.BlockSpec((rows, width), lambda j: (0, 0))
    return pl.pallas_call(
        ffn_kernel,
        grid=(tiles,),
        in_specs=[whole] + weights,
        out_specs=[own, own, own, whole],
        out_shape=[
            jax.ShapeDtypeStruct((rows, units), F32),
            jax.ShapeDtypeStruct((rows, units), F32),
            jax.ShapeDtypeStruct((rows, units), BF),
            jax.ShapeDtypeStruct((rows, width), F32),
        ],
        compiler_params=VMEM,
        name="ffn_forward",
    )(source, *pieces, *pieces, *pieces)


def ffn_backward(grad, gate, up, pieces):
    rows, width = grad.shape
    units = pieces[0].shape[1] // 3
    tiles = units // UNIT_TILE
    own, weights = unit_specs(rows, pieces, tiles)
    whole = pl.BlockSpec((rows, width), lambda j: (0, 0))
    return pl.pallas_call(
        ffn_back_kernel,
        grid=(tiles,),
        in_specs=[whole, own, own] + weights,
        out_specs=[own, own, whole],
        out_shape=[
            jax.ShapeDtypeStruct((rows, units), BF),
            jax.ShapeDtypeStruct((rows, units), BF),
            jax.ShapeDtypeStruct((rows, width), F32),
        ],
        compiler_params=VMEM,
        name="ffn_backward",
    )(grad, gate, up, *pieces, *pieces, *pieces)


def ffn_wgrad_kernel(steps, left, gate, up, hidden, *outs):
    rows = gate.shape[0]

    def store(first, right):
        start = 0
        for out in outs:
            size = out.shape[0]
            out[...] = matmul(left[start : start + size, first : first + rows], right[...]).astype(BF)
            start += size

    for i, (first, right) in enumerate([(0, gate), (0, up), (rows, hidden)]):
        pl.when(pl.program_id(0) // steps == i)(lambda first=first, right=right: store(first, right))


def ffn_wgrad(left, gate, up, hidden):
    width, (rows, units) = left.shape[0], gate.shape
    steps = 2
    tile = units // steps
    sizes = [width // 4, width // 4, width // 8, width // 8, width // 4]

    def right(i):
        return pl.BlockSpec((rows, tile), lambda j: (0, jnp.clip(j - i * steps, 0, steps - 1)))

    return pl.pallas_call(
        lambda *refs: ffn_wgrad_kernel(steps, *refs),
        grid=(3 * steps,),
        in_specs=[pl.BlockSpec(left.shape, lambda j: (0, 0)), right(0), right(1), right(2)],
        out_specs=[pl.BlockSpec((size, tile), lambda j: (0, j)) for size in sizes],
        out_shape=[jax.ShapeDtypeStruct((size, 3 * units), BF) for size in sizes],
        compiler_params=VMEM,
        name="ffn_wgrad",
    )(left, gate, up, hidden)


def split_rows(values, parts):
    size = values.shape[0] // parts
    return [values[i * size : (i + 1) * size] for i in range(parts)]


def pick(core, first, second):
    return jnp.where(core == 0, first, second)


def shards(
    hidden_in,
    out_grad,
    block_order,
    norm_gains,
    head_gains,
    w_query,
    w_key,
    w_value,
    w_out,
    w_gate,
    w_up,
    w_down,
):
    tokens, width = hidden_in.shape
    y, z, x, core = (lax.axis_index(name) for name in CTX)
    other = 1 - core
    piece = width // 64
    units = w_gate.shape[1] // 2
    padded = (units + 127) // 128 * 128
    quarter = width // 4

    out_t, down_t = w_out.T, w_down.T

    def units_of(which):
        cut = [
            jnp.pad(lax.dynamic_slice_in_dim(w, which * units, units, 1), ((0, 0), (0, padded - units)))
            for w in (w_gate, w_up, down_t)
        ]
        return jnp.concatenate(cut, 1)

    def heads_of(which):
        cut = [lax.dynamic_slice_in_dim(w, which * HD, HD, 1) for w in (w_query, out_t)]
        return jnp.concatenate(cut + [w_key, w_value], 1)

    def chip_rows(of):
        mine, theirs = of(core), of(other)
        from_y, from_core, from_both = exchange((mine, theirs, theirs), "c")
        return pick(
            core,
            jnp.concatenate([mine, from_core, from_y, from_both], 0),
            jnp.concatenate([from_core, mine, from_both, from_y], 0),
        )

    head_rows = chip_rows(heads_of)
    ffn_rows = chip_rows(units_of)
    head_minor = after(gather_direct(head_rows, False), ffn_rows)
    ffn_minor = jnp.concatenate(gather_ring(ffn_rows, False), 0)
    head_w = after(stack_rows(gather_ring(head_minor, True)), ffn_minor)
    ffn_w = gather_ring(ffn_minor, True)
    hidden_in = after(hidden_in, head_rows)
    query_w, out_w = head_w[:, :HD], head_w[:, HD : 2 * HD]
    key_w, value_w, pair_w = head_w[:, 2 * HD : 3 * HD], head_w[:, 3 * HD :], head_w[:, 2 * HD :]

    place = jnp.arange(width, dtype=jnp.int32)
    first, second = place // quarter, place // (quarter // 4) % 4
    z_at, x_at = (z + pick(core, second, first)) % 4, (x + pick(core, first, second)) % 4
    y_at = (y + place // (2 * piece)) % 2
    by_ring = y_at * (width // 2) + z_at * (8 * piece) + x_at * (2 * piece) + place % (2 * piece)
    to_ring = (place[:, None] == by_ring[None, :]).astype(BF)
    from_ring = (by_ring[:, None] == place[None, :]).astype(BF)

    def reorder(values, moves):
        return matmul(values, moves).astype(BF)

    def both_cores(values):
        return jnp.concatenate([values, shift(values, "c")], 0)

    def sum_parts(partial):
        low = reorder(partial.astype(BF), from_ring)
        chip = (low[:tokens].astype(F32) + shift(low[tokens:], "c").astype(F32)).astype(BF)
        return chip.astype(F32) + shift(chip, "s").astype(F32)

    offsets = jnp.arange(tokens, dtype=jnp.int32)

    def positions_of(places):
        return (block_order[places.reshape(-1)][:, None] * tokens + offsets[None, :]).reshape(-1)

    def device_of(y_at, z_at, x_at, core_at):
        return y_at * 32 + z_at * 8 + x_at * 2 + core_at

    steps = jnp.arange(4, dtype=jnp.int32)
    outer, inner = steps[:, None, None], steps[None, :, None]

    def keys_of(which):
        z_at, x_at = (z + pick(which, inner, outer)) % 4, (x + pick(which, outer, inner)) % 4
        return positions_of(device_of((y + steps[None, None, :2]) % 2, z_at, x_at, which))

    key_pos = [keys_of(core), keys_of(other)]
    own_pos = positions_of(device_of(y, z, x, core))
    chip_pos = jnp.concatenate([own_pos, positions_of(device_of(y, z, x, other))])
    cosine_table, sine_table = tables(chip_pos, HD)

    attn_val, pre_attn_back = jax.vjp(rms_scale, hidden_in, norm_gains[0])
    attn_chip = reorder(both_cores(attn_val.astype(BF)), to_ring)
    attn_ring = attn_chip[:tokens]
    key_pre = matmul(attn_ring, key_w)
    value_low = matmul(attn_ring, value_w).astype(BF)
    key_val, key_back = jax.vjp(
        lambda values, gain: rotate(rms_scale(values, gain), cosine_table[:tokens], sine_table[:tokens]),
        key_pre,
        head_gains[1],
    )
    key_low = key_val.astype(BF)
    pair_low = jnp.concatenate([key_low, value_low], 1)
    own_pairs = jnp.concatenate(gather_ring(gather_minor_y(pair_low), True), 0)
    own_pairs = after(own_pairs, ffn_w[1], ffn_w[4])
    pairs = [own_pairs, shift(own_pairs, "c")]

    query_pre = matmul(attn_chip, query_w)
    query_val, query_back = jax.vjp(
        lambda values, gain: rotate(rms_scale(values, gain), cosine_table, sine_table),
        query_pre,
        head_gains[0],
    )
    score_scale = HD ** (-0.5)
    queries = (query_val.astype(BF).astype(F32) * score_scale).astype(BF)
    parts = [attend(queries, pairs[part], key_pos[part], chip_pos) for part in range(2)]
    weights = [part[0] for part in parts]
    inverse_total = 1.0 / (parts[0][1] + parts[1][1])
    accum = parts[0][2] + parts[1][2]
    attn_rows = accum * inverse_total
    mixed_low = attn_rows.astype(BF)
    attn_out = sum_parts(inner_cols(mixed_low, out_w))
    post_attn, post_attn_back = jax.vjp(rms_scale, attn_out, norm_gains[1])
    mid_state = hidden_in + post_attn

    ffn_val, ffn_norm_back = jax.vjp(rms_scale, mid_state, norm_gains[2])
    ffn_chip = both_cores(ffn_val.astype(BF))
    gate_pre, up_pre, hidden_low, ffn_part = ffn_forward(reorder(ffn_chip, to_ring), ffn_w)
    ffn_out = sum_parts(ffn_part)
    post_ffn, post_ffn_back = jax.vjp(rms_scale, ffn_out, norm_gains[3])
    block_out = mid_state + post_ffn

    ffn_grad, gain_four = post_ffn_back(out_grad)
    ffn_grad_chip = both_cores(ffn_grad.astype(BF))
    gate_low, up_low, ffn_norm_part = ffn_backward(reorder(ffn_grad_chip, to_ring), gate_pre, up_pre, ffn_w)
    ffn_norm_grad = sum_parts(ffn_norm_part)
    mid_from, gain_three = ffn_norm_back(ffn_norm_grad)
    mid_grad = out_grad + mid_from

    sources = jnp.concatenate([ffn_chip, ffn_grad_chip], 0)
    left = inner_cols(from_ring, sources).astype(BF)
    ffn_chunks = ffn_wgrad(left, gate_low, up_low, hidden_low)

    def last_stage(values):
        parts = split_rows(values.astype(BF), 4)
        kept = [pick(core, parts[i], parts[i + 1]) for i in (0, 2)]
        sent = [pick(core, parts[i + 1], parts[i]) for i in (0, 2)]
        from_y, from_core, from_both = exchange((kept[1], sent[0], sent[1]), "c")
        return wide_sum(kept[0], from_y), wide_sum(from_core, from_both)

    attn_grad, gain_two = post_attn_back(mid_grad)
    attn_grad_chip = reorder(both_cores(attn_grad.astype(BF)), to_ring)
    rows_grad = matmul(attn_grad_chip, out_w).astype(BF)
    rows_wide = rows_grad.astype(F32)
    row_dot = jnp.sum(rows_wide * attn_rows, axis=1)[:, None]
    rows_scaled = (rows_wide * inverse_total).astype(BF)
    pair_far, query_far = attend_back(
        queries, pairs[1], weights[1], rows_grad, rows_scaled, row_dot, inverse_total
    )
    pair_near, query_near = attend_back(
        queries, pairs[0], weights[0], rows_grad, rows_scaled, row_dot, inverse_total
    )
    query_grad = query_far + query_near
    query_pre_grad, query_gain = query_back(query_grad * score_scale)
    query_gain = query_gain + shift(query_gain, "s")
    query_pre_low = query_pre_grad.astype(BF)
    early_grads = jnp.concatenate(
        [inner_rows(attn_chip, query_pre_low), inner_rows(attn_grad_chip, mixed_low)], 1
    ).astype(BF)
    pair_got = shift(pair_far, "c")
    chunks = [
        jnp.concatenate([wide_sum(near, got).astype(BF), early], 0)
        for near, got, early in zip(*(split_rows(part, 4) for part in (pair_near, pair_got, early_grads)))
    ]
    major_sum = reduce_chunks(*chunks, True).astype(BF)
    pair_chunks = split_rows(major_sum[: 8 * tokens], 4)
    early_chunks = split_rows(major_sum[8 * tokens :], 4)
    minor_sum = reduce_direct(
        [jnp.concatenate([pair, early], 0) for pair, early in zip(pair_chunks, early_chunks)], False
    )
    pair_own, pair_far_y = split_rows(minor_sum[: 2 * tokens].astype(BF), 2)
    from_y, from_shard, from_both = exchange((pair_far_y, pair_own, pair_far_y), "s")
    pair_grad = wide_sum(pair_own, from_y) + wide_sum(from_shard, from_both)
    attn_norm_sum = sum_parts(inner_cols(query_pre_low, query_w))
    key_pre_grad, key_gain = key_back(pair_grad[:, :HD])
    key_pre_low = key_pre_grad.astype(BF)
    value_grad_low = pair_grad[:, HD:].astype(BF)
    pair_part = inner_cols(jnp.concatenate([key_pre_low, value_grad_low], 1), pair_w).astype(BF)
    attn_norm_grad = attn_norm_sum + reorder(pair_part, from_ring).astype(F32)
    input_from, gain_one = pre_attn_back(attn_norm_grad)
    input_grad = mid_grad + input_from

    kept, sent = pick(core, key_pre_low, value_grad_low), pick(core, value_grad_low, key_pre_low)
    pair_chip = jnp.concatenate([kept, shift(sent, "c")], 0)
    heads = [
        jnp.pad(gain.reshape(64, HD // 64), ((0, 0), (0, piece - HD // 64))).reshape(width)
        for gain in (query_gain, key_gain)
    ]
    gains = jnp.stack([gain_one, gain_two, gain_three, gain_four] + heads, 1)
    gains = jnp.pad(gains, ((0, 0), (0, 128 - gains.shape[1]))).astype(BF)
    late_grads = jnp.concatenate([inner_rows(attn_chip, pair_chip), inner_rows(to_ring, gains)], 1).astype(BF)
    late_major = reduce_direct(split_rows(late_grads, 4), True).astype(BF)
    late_sum = reduce_direct(split_rows(late_major, 4), False)
    head_mine, head_got = last_stage(jnp.concatenate([minor_sum[2 * tokens :], late_sum], 1))

    ffn_major = reduce_ring(*ffn_chunks, True, (query_grad,), (pair_grad,)).astype(BF)
    ffn_mine, ffn_got = last_stage(reduce_chunks(*split_rows(ffn_major, 4), False))

    def joined(start, size, mine, got):
        left, right = mine[:, start : start + size], got[:, start : start + size]
        return pick(core, jnp.concatenate([left, right], 1), jnp.concatenate([right, left], 1))

    gate_wgrad = joined(0, units, ffn_mine, ffn_got)
    up_wgrad = joined(padded, units, ffn_mine, ffn_got)
    down_wgrad = joined(2 * padded, units, ffn_mine, ffn_got).T

    query_wgrad = joined(0, HD, head_mine, head_got)
    out_wgrad = joined(HD, HD, head_mine, head_got).T
    pair_wgrad = joined(2 * HD, HD, head_mine, head_got)
    gain_sums = head_mine[:, 3 * HD :] + head_got[:, 3 * HD :]
    return (
        block_out,
        input_grad,
        query_wgrad,
        pair_wgrad[:, :HD],
        pair_wgrad[:, HD:],
        out_wgrad,
        gate_wgrad,
        up_wgrad,
        down_wgrad,
        gain_sums[:, :4].T,
        gain_sums[: HD // 64, 4:6].T,
    )


def solution(mesh):
    fine = Mesh(mesh.devices.reshape(2, 4, 4, 2, 2), ("y", "z", "x", "c", "s"))
    placed = (
        P(CTX, None),
        P(CTX, None),
        P(),
        P(),
        P(),
        P(CTX, "s"),
        P(CTX, None),
        P(CTX, None),
        P("s", CTX),
        P(CTX, "s"),
        P(CTX, "s"),
        P("s", CTX),
    )
    return jax.shard_map(
        shards,
        mesh=fine,
        in_specs=placed,
        out_specs=(
            P(CTX, None),
            P(CTX, None),
            P(CTX, "s"),
            P(CTX, None),
            P(CTX, None),
            P("s", CTX),
            P(CTX, "s"),
            P(CTX, "s"),
            P("s", CTX),
            P(None, CTX),
            P(None, CTX),
        ),
        check_vma=False,
    )
```

```python
import math

import jax
import jax.numpy as jnp
from jax import lax
from jax.experimental import pallas as pl
from jax.experimental.pallas import tpu as pltpu
from jax.sharding import Mesh, PartitionSpec as P

HD = 256
EPS = 1e-06
THETA = 1000000.0
BF = jnp.bfloat16
F32 = jnp.float32
CTX = ("y", "z", "x", "c")


def matmul(left, right):
    return jnp.dot(left, right, preferred_element_type=F32)


def inner_rows(left, right):
    return lax.dot_general(left, right, (((0,), (0,)), ((), ())), preferred_element_type=F32)


def inner_cols(left, right):
    return lax.dot_general(left, right, (((1,), (1,)), ((), ())), preferred_element_type=F32)


def rms_scale(values, gain):
    return values * lax.rsqrt(jnp.mean(values * values, axis=-1, keepdims=True) + EPS) * gain


def rotate(values, cosine_table, sine_table):
    half_width = values.shape[-1] // 2
    first = values[..., :half_width]
    second = values[..., half_width:]
    return jnp.concatenate(
        [first * cosine_table - second * sine_table, second * cosine_table + first * sine_table],
        axis=-1,
    )


def tables(positions, head_width):
    frequency = jnp.arange(head_width // 2, dtype=F32)
    inverse = jnp.exp(frequency * (-2.0 * math.log(THETA) / head_width))
    angles = positions.astype(F32)[:, None] * inverse[None, :]
    return (jnp.cos(angles), jnp.sin(angles))


def shift(values, axis, step=1):
    size = lax.axis_size(axis)
    return lax.ppermute(values, axis, [(i, (i + step) % size) for i in range(size)])


def ring(values, major, step, cross_y=False):
    moves = []
    for y in range(2):
        for z in range(4):
            for x in range(4):
                for core in range(2):
                    along_x = major == (core == 0)
                    to_z, to_x = (z, (x + step) % 4) if along_x else ((z + step) % 4, x)
                    to_y = 1 - y if cross_y else y
                    moves.append((y * 32 + z * 8 + x * 2 + core, to_y * 32 + to_z * 8 + to_x * 2 + core))
    return lax.ppermute(values, CTX, moves)


def gather_direct(block, major):
    return jnp.concatenate([block] + [ring(block, major, -k) for k in (1, 2, 3)], 0)


def gather_minor_y(block):
    blocks = [block if k == 0 else ring(block, False, -k) for k in range(4)]
    others = [ring(block, False, -k, True) for k in range(4)]
    return jnp.concatenate([part for pair in zip(blocks, others) for part in pair], 0)


def exchange(values, axis):
    both = [(i, 3 - i) for i in range(4)]
    return shift(values[0], "y"), shift(values[1], axis), lax.ppermute(values[2], ("y", axis), both)


def after(value, *others):
    return lax.optimization_barrier((value, *others))[0]


def gather_ring(block, major, *others):
    half = (block.shape[0] // 2 + 7) // 8 * 8
    previous = ring(block, major, 1)
    following = ring(block, major, -1)
    far_low = ring(after(previous, *others)[:half], major, 1)
    far_high = ring(after(following, *others)[half:], major, -1)
    return [block, following, far_low, far_high, previous]


def wide_sum(*parts):
    return sum(part.astype(F32) for part in parts)


def reduce_direct(chunks, major):
    return wide_sum(chunks[0], *[ring(chunks[k], major, k) for k in (1, 2, 3)])


def reduce_ring(own, following, far_low, far_high, previous, major, others=(), last=()):
    half = far_low.shape[0]
    from_previous = after(ring(far_low, major, 1), *others)
    from_next = after(ring(far_high, major, -1), *others)
    forward = jnp.concatenate(
        [wide_sum(following[:half], from_previous).astype(BF), following[half:]], 0
    )
    backward = jnp.concatenate(
        [previous[:half], wide_sum(previous[half:], from_next).astype(BF)], 0
    )
    return wide_sum(after(own, *last), ring(forward, major, 1), ring(backward, major, -1))


def reduce_chunks(own, following, far, previous, major):
    half = (far.shape[0] // 2 + 7) // 8 * 8
    return reduce_ring(own, following, far[:half], far[half:], previous, major)


ATTN_BLOCK = 1024
VMEM = pltpu.CompilerParams(vmem_limit_bytes=48 * 1024 * 1024)


def attend_kernel(query, pair, key_pos, query_pos, weight, total, accum):
    scores = inner_cols(query[...], pair[:, :HD])
    exps = jnp.where(query_pos[...] >= key_pos[...], jnp.exp(scores), 0.0)
    low = exps.astype(BF)
    weight[...] = low

    @pl.when(pl.program_id(0) == 0)
    def _():
        total[...] = jnp.zeros_like(total)
        accum[...] = jnp.zeros_like(accum)

    total[...] += jnp.sum(exps, axis=1, keepdims=True)
    accum[...] += matmul(low, pair[:, HD:])


def attend(queries, pairs, key_pos, query_pos):
    rows, keys = queries.shape[0], pairs.shape[0]
    whole = lambda i: (0, 0)
    return pl.pallas_call(
        attend_kernel,
        grid=(keys // ATTN_BLOCK,),
        in_specs=[
            pl.BlockSpec((rows, HD), whole),
            pl.BlockSpec((ATTN_BLOCK, 2 * HD), lambda i: (i, 0)),
            pl.BlockSpec((1, ATTN_BLOCK), lambda i: (0, i)),
            pl.BlockSpec((rows, 1), whole),
        ],
        out_specs=[
            pl.BlockSpec((rows, ATTN_BLOCK), lambda i: (0, i)),
            pl.BlockSpec((rows, 1), whole),
            pl.BlockSpec((rows, HD), whole),
        ],
        out_shape=[
            jax.ShapeDtypeStruct((rows, keys), BF),
            jax.ShapeDtypeStruct((rows, 1), F32),
            jax.ShapeDtypeStruct((rows, HD), F32),
        ],
        compiler_params=VMEM,
        name="attend",
    )(queries, pairs, key_pos[None, :], query_pos[:, None])


def attend_back_kernel(query, pair, weight, grad, scaled, dot, inverse, pair_grad, query_grad):
    weights = weight[...]
    prob_grad = inner_cols(grad[...], pair[:, HD:])
    score_grad = (weights.astype(F32) * ((prob_grad - dot[...]) * inverse[...])).astype(BF)
    pair_grad[:, :HD] = inner_rows(score_grad, query[...]).astype(BF)
    pair_grad[:, HD:] = inner_rows(weights, scaled[...]).astype(BF)

    @pl.when(pl.program_id(0) == 0)
    def _():
        query_grad[...] = jnp.zeros_like(query_grad)

    query_grad[...] += matmul(score_grad, pair[:, :HD])


def attend_back(queries, pairs, weights, grads, scaled, dot, inverse):
    rows, keys = queries.shape[0], pairs.shape[0]
    whole = lambda i: (0, 0)
    return pl.pallas_call(
        attend_back_kernel,
        grid=(keys // ATTN_BLOCK,),
        in_specs=[
            pl.BlockSpec((rows, HD), whole),
            pl.BlockSpec((ATTN_BLOCK, 2 * HD), lambda i: (i, 0)),
            pl.BlockSpec((rows, ATTN_BLOCK), lambda i: (0, i)),
            pl.BlockSpec((rows, HD), whole),
            pl.BlockSpec((rows, HD), whole),
            pl.BlockSpec((rows, 1), whole),
            pl.BlockSpec((rows, 1), whole),
        ],
        out_specs=[
            pl.BlockSpec((ATTN_BLOCK, 2 * HD), lambda i: (i, 0)),
            pl.BlockSpec((rows, HD), whole),
        ],
        out_shape=[
            jax.ShapeDtypeStruct((keys, 2 * HD), BF),
            jax.ShapeDtypeStruct((rows, HD), F32),
        ],
        compiler_params=VMEM,
        name="attend_back",
    )(queries, pairs, weights, grads, scaled, dot, inverse)


def stack_kernel(*refs):
    start = 0
    for piece in refs[:-1]:
        refs[-1][start : start + piece.shape[0], :] = piece[...]
        start += piece.shape[0]


def stack_rows(pieces, tile=256):
    rows, columns = sum(piece.shape[0] for piece in pieces), pieces[0].shape[1]
    return pl.pallas_call(
        stack_kernel,
        grid=(columns // tile,),
        in_specs=[pl.BlockSpec((piece.shape[0], tile), lambda j: (0, j)) for piece in pieces],
        out_specs=pl.BlockSpec((rows, tile), lambda j: (0, j)),
        out_shape=jax.ShapeDtypeStruct((rows, columns), pieces[0].dtype),
        compiler_params=VMEM,
        name="stack_rows",
    )(*pieces)


UNIT_TILE = 256
GELU_IN = math.sqrt(2.0 / math.pi)
GELU_CUBE = 0.044715


def joined_rows(refs):
    return jnp.concatenate([ref[...] for ref in refs], 0)


def ffn_kernel(source, *refs):
    count = (len(refs) - 4) // 3
    gate_w, up_w, down_w = (joined_rows(refs[i * count : (i + 1) * count]) for i in range(3))
    gate, up, hidden, total = refs[3 * count :]
    gate_pre = matmul(source[...], gate_w)
    up_pre = matmul(source[...], up_w)
    gate[...] = gate_pre
    up[...] = up_pre
    inner = GELU_IN * (gate_pre + GELU_CUBE * (gate_pre * gate_pre * gate_pre))
    low = (0.5 * gate_pre * (1.0 + jnp.tanh(inner)) * up_pre).astype(BF)
    hidden[...] = low

    @pl.when(pl.program_id(0) == 0)
    def _():
        total[...] = jnp.zeros_like(total)

    total[...] += inner_cols(low, down_w)


def ffn_back_kernel(grad, gate, up, *refs):
    count = (len(refs) - 3) // 3
    gate_w, up_w, down_w = (joined_rows(refs[i * count : (i + 1) * count]) for i in range(3))
    gate_grad, up_grad, total = refs[3 * count :]
    hidden_grad = matmul(grad[...], down_w)
    gate_pre = gate[...]
    square = gate_pre * gate_pre
    bend = jnp.tanh(GELU_IN * (gate_pre + GELU_CUBE * (square * gate_pre)))
    rise = 0.5 * (1.0 + bend)
    slope = rise + 0.5 * gate_pre * (1.0 - bend * bend) * (GELU_IN * (1.0 + 3.0 * GELU_CUBE * square))
    gate_low = (hidden_grad * up[...] * slope).astype(BF)
    up_low = (hidden_grad * (gate_pre * rise)).astype(BF)
    gate_grad[...] = gate_low
    up_grad[...] = up_low

    @pl.when(pl.program_id(0) == 0)
    def _():
        total[...] = jnp.zeros_like(total)

    total[...] += inner_cols(gate_low, gate_w) + inner_cols(up_low, up_w)


def unit_specs(rows, pieces, tiles):
    own = pl.BlockSpec((rows, UNIT_TILE), lambda j: (0, j))
    weights = [
        pl.BlockSpec((piece.shape[0], UNIT_TILE), lambda j, i=i: (0, j + i * tiles))
        for i in range(3)
        for piece in pieces
    ]
    return own, weights


def ffn_forward(source, pieces):
    rows, width = source.shape
    units = pieces[0].shape[1] // 3
    tiles = units // UNIT_TILE
    own, weights = unit_specs(rows, pieces, tiles)
    whole = pl.BlockSpec((rows, width), lambda j: (0, 0))
    return pl.pallas_call(
        ffn_kernel,
        grid=(tiles,),
        in_specs=[whole] + weights,
        out_specs=[own, own, own, whole],
        out_shape=[
            jax.ShapeDtypeStruct((rows, units), F32),
            jax.ShapeDtypeStruct((rows, units), F32),
            jax.ShapeDtypeStruct((rows, units), BF),
            jax.ShapeDtypeStruct((rows, width), F32),
        ],
        compiler_params=VMEM,
        name="ffn_forward",
    )(source, *pieces, *pieces, *pieces)


def ffn_backward(grad, gate, up, pieces):
    rows, width = grad.shape
    units = pieces[0].shape[1] // 3
    tiles = units // UNIT_TILE
    own, weights = unit_specs(rows, pieces, tiles)
    whole = pl.BlockSpec((rows, width), lambda j: (0, 0))
    return pl.pallas_call(
        ffn_back_kernel,
        grid=(tiles,),
        in_specs=[whole, own, own] + weights,
        out_specs=[own, own, whole],
        out_shape=[
            jax.ShapeDtypeStruct((rows, units), BF),
            jax.ShapeDtypeStruct((rows, units), BF),
            jax.ShapeDtypeStruct((rows, width), F32),
        ],
        compiler_params=VMEM,
        name="ffn_backward",
    )(grad, gate, up, *pieces, *pieces, *pieces)


def ffn_wgrad_kernel(steps, left, gate, up, hidden, *outs):
    rows = gate.shape[0]

    def store(first, right):
        start = 0
        for out in outs:
            size = out.shape[0]
            out[...] = matmul(left[start : start + size, first : first + rows], right[...]).astype(BF)
            start += size

    for i, (first, right) in enumerate([(0, gate), (0, up), (rows, hidden)]):
        pl.when(pl.program_id(0) // steps == i)(lambda first=first, right=right: store(first, right))


def ffn_wgrad(left, gate, up, hidden):
    width, (rows, units) = left.shape[0], gate.shape
    steps = 2
    tile = units // steps
    sizes = [width // 4, width // 4, width // 8, width // 8, width // 4]

    def right(i):
        return pl.BlockSpec((rows, tile), lambda j: (0, jnp.clip(j - i * steps, 0, steps - 1)))

    return pl.pallas_call(
        lambda *refs: ffn_wgrad_kernel(steps, *refs),
        grid=(3 * steps,),
        in_specs=[pl.BlockSpec(left.shape, lambda j: (0, 0)), right(0), right(1), right(2)],
        out_specs=[pl.BlockSpec((size, tile), lambda j: (0, j)) for size in sizes],
        out_shape=[jax.ShapeDtypeStruct((size, 3 * units), BF) for size in sizes],
        compiler_params=VMEM,
        name="ffn_wgrad",
    )(left, gate, up, hidden)


def split_rows(values, parts):
    size = values.shape[0] // parts
    return [values[i * size : (i + 1) * size] for i in range(parts)]


def pick(core, first, second):
    return jnp.where(core == 0, first, second)


def shards(
    hidden_in,
    out_grad,
    block_order,
    norm_gains,
    head_gains,
    w_query,
    w_key,
    w_value,
    w_out,
    w_gate,
    w_up,
    w_down,
):
    tokens, width = hidden_in.shape
    y, z, x, core = (lax.axis_index(name) for name in CTX)
    other = 1 - core
    piece = width // 64
    units = w_gate.shape[1] // 2
    padded = (units + 127) // 128 * 128
    quarter = width // 4

    out_t, down_t = w_out.T, w_down.T

    def units_of(which):
        cut = [
            jnp.pad(lax.dynamic_slice_in_dim(w, which * units, units, 1), ((0, 0), (0, padded - units)))
            for w in (w_gate, w_up, down_t)
        ]
        return jnp.concatenate(cut, 1)

    def heads_of(which):
        cut = [lax.dynamic_slice_in_dim(w, which * HD, HD, 1) for w in (w_query, out_t)]
        return jnp.concatenate(cut + [w_key, w_value], 1)

    def chip_rows(of):
        mine, theirs = of(core), of(other)
        from_y, from_core, from_both = exchange((mine, theirs, theirs), "c")
        return pick(
            core,
            jnp.concatenate([mine, from_core, from_y, from_both], 0),
            jnp.concatenate([from_core, mine, from_both, from_y], 0),
        )

    head_rows = chip_rows(heads_of)
    ffn_rows = chip_rows(units_of)
    head_minor = after(gather_direct(head_rows, False), ffn_rows)
    head_pieces = gather_ring(head_minor, True)
    head_w = stack_rows(head_pieces)
    ffn_minor = jnp.concatenate(gather_ring(after(ffn_rows, head_pieces[1], head_pieces[4]), False), 0)
    ffn_w = gather_ring(ffn_minor, True)
    hidden_in = after(hidden_in, head_rows)
    query_w, out_w = head_w[:, :HD], head_w[:, HD : 2 * HD]
    key_w, value_w, pair_w = head_w[:, 2 * HD : 3 * HD], head_w[:, 3 * HD :], head_w[:, 2 * HD :]

    place = jnp.arange(width, dtype=jnp.int32)
    first, second = place // quarter, place // (quarter // 4) % 4
    z_at, x_at = (z + pick(core, second, first)) % 4, (x + pick(core, first, second)) % 4
    y_at = (y + place // (2 * piece)) % 2
    by_ring = y_at * (width // 2) + z_at * (8 * piece) + x_at * (2 * piece) + place % (2 * piece)
    to_ring = (place[:, None] == by_ring[None, :]).astype(BF)
    from_ring = (by_ring[:, None] == place[None, :]).astype(BF)

    def reorder(values, moves):
        return matmul(values, moves).astype(BF)

    def both_cores(values):
        return jnp.concatenate([values, shift(values, "c")], 0)

    def sum_parts(partial):
        low = reorder(partial.astype(BF), from_ring)
        chip = (low[:tokens].astype(F32) + shift(low[tokens:], "c").astype(F32)).astype(BF)
        return chip.astype(F32) + shift(chip, "s").astype(F32)

    offsets = jnp.arange(tokens, dtype=jnp.int32)

    def positions_of(places):
        return (block_order[places.reshape(-1)][:, None] * tokens + offsets[None, :]).reshape(-1)

    def device_of(y_at, z_at, x_at, core_at):
        return y_at * 32 + z_at * 8 + x_at * 2 + core_at

    steps = jnp.arange(4, dtype=jnp.int32)
    outer, inner = steps[:, None, None], steps[None, :, None]

    def keys_of(which):
        z_at, x_at = (z + pick(which, inner, outer)) % 4, (x + pick(which, outer, inner)) % 4
        return positions_of(device_of((y + steps[None, None, :2]) % 2, z_at, x_at, which))

    key_pos = [keys_of(core), keys_of(other)]
    own_pos = positions_of(device_of(y, z, x, core))
    chip_pos = jnp.concatenate([own_pos, positions_of(device_of(y, z, x, other))])
    cosine_table, sine_table = tables(chip_pos, HD)

    attn_val, pre_attn_back = jax.vjp(rms_scale, hidden_in, norm_gains[0])
    attn_chip = reorder(both_cores(attn_val.astype(BF)), to_ring)
    attn_ring = attn_chip[:tokens]
    key_pre = matmul(attn_ring, key_w)
    value_low = matmul(attn_ring, value_w).astype(BF)
    key_val, key_back = jax.vjp(
        lambda values, gain: rotate(rms_scale(values, gain), cosine_table[:tokens], sine_table[:tokens]),
        key_pre,
        head_gains[1],
    )
    key_low = key_val.astype(BF)
    pair_low = after(jnp.concatenate([key_low, value_low], 1), ffn_minor)
    own_pairs = jnp.concatenate(gather_ring(gather_minor_y(pair_low), True), 0)
    own_pairs = after(own_pairs, ffn_w[1], ffn_w[4])
    pairs = [own_pairs, shift(own_pairs, "c")]

    query_pre = matmul(attn_chip, query_w)
    query_val, query_back = jax.vjp(
        lambda values, gain: rotate(rms_scale(values, gain), cosine_table, sine_table),
        query_pre,
        head_gains[0],
    )
    score_scale = HD ** (-0.5)
    queries = (query_val.astype(BF).astype(F32) * score_scale).astype(BF)
    parts = [attend(queries, pairs[part], key_pos[part], chip_pos) for part in range(2)]
    weights = [part[0] for part in parts]
    inverse_total = 1.0 / (parts[0][1] + parts[1][1])
    accum = parts[0][2] + parts[1][2]
    attn_rows = accum * inverse_total
    mixed_low = after(attn_rows.astype(BF), ffn_w[2], ffn_w[3])
    attn_out = sum_parts(inner_cols(mixed_low, out_w))
    post_attn, post_attn_back = jax.vjp(rms_scale, attn_out, norm_gains[1])
    mid_state = hidden_in + post_attn

    ffn_val, ffn_norm_back = jax.vjp(rms_scale, mid_state, norm_gains[2])
    ffn_chip = both_cores(ffn_val.astype(BF))
    gate_pre, up_pre, hidden_low, ffn_part = ffn_forward(reorder(ffn_chip, to_ring), ffn_w)
    ffn_out = sum_parts(ffn_part)
    post_ffn, post_ffn_back = jax.vjp(rms_scale, ffn_out, norm_gains[3])
    block_out = mid_state + post_ffn

    ffn_grad, gain_four = post_ffn_back(out_grad)
    ffn_grad_chip = both_cores(ffn_grad.astype(BF))
    gate_low, up_low, ffn_norm_part = ffn_backward(reorder(ffn_grad_chip, to_ring), gate_pre, up_pre, ffn_w)
    ffn_norm_grad = sum_parts(ffn_norm_part)
    sources = jnp.concatenate([ffn_chip, ffn_grad_chip], 0)
    left = inner_cols(from_ring, sources).astype(BF)
    ffn_chunks = ffn_wgrad(left, gate_low, up_low, hidden_low)
    mid_from, gain_three = ffn_norm_back(after(ffn_norm_grad, *ffn_chunks))
    mid_grad = out_grad + mid_from

    def last_stage(values):
        parts = split_rows(values.astype(BF), 4)
        kept = [pick(core, parts[i], parts[i + 1]) for i in (0, 2)]
        sent = [pick(core, parts[i + 1], parts[i]) for i in (0, 2)]
        from_y, from_core, from_both = exchange((kept[1], sent[0], sent[1]), "c")
        return wide_sum(kept[0], from_y), wide_sum(from_core, from_both)

    attn_grad, gain_two = post_attn_back(mid_grad)
    attn_grad_chip = reorder(both_cores(attn_grad.astype(BF)), to_ring)
    rows_grad = matmul(attn_grad_chip, out_w).astype(BF)
    rows_wide = rows_grad.astype(F32)
    row_dot = jnp.sum(rows_wide * attn_rows, axis=1)[:, None]
    rows_scaled = (rows_wide * inverse_total).astype(BF)
    pair_far, query_far = attend_back(
        queries, pairs[1], weights[1], rows_grad, rows_scaled, row_dot, inverse_total
    )
    pair_near, query_near = attend_back(
        queries, pairs[0], weights[0], rows_grad, rows_scaled, row_dot, inverse_total
    )
    query_grad = query_far + query_near
    query_pre_grad, query_gain = query_back(query_grad * score_scale)
    query_gain = query_gain + shift(query_gain, "s")
    query_pre_low = query_pre_grad.astype(BF)
    early_grads = jnp.concatenate(
        [inner_rows(attn_chip, query_pre_low), inner_rows(attn_grad_chip, mixed_low)], 1
    ).astype(BF)
    pair_got = shift(pair_far, "c")
    chunks = [
        jnp.concatenate([wide_sum(near, got).astype(BF), early], 0)
        for near, got, early in zip(*(split_rows(part, 4) for part in (pair_near, pair_got, early_grads)))
    ]
    major_sum = reduce_chunks(*chunks, True).astype(BF)
    pair_chunks = split_rows(major_sum[: 8 * tokens], 4)
    early_chunks = split_rows(major_sum[8 * tokens :], 4)
    minor_sum = reduce_direct(
        [jnp.concatenate([pair, early], 0) for pair, early in zip(pair_chunks, early_chunks)], False
    )
    pair_own, pair_far_y = split_rows(minor_sum[: 2 * tokens].astype(BF), 2)
    from_y, from_shard, from_both = exchange((pair_far_y, pair_own, pair_far_y), "s")
    pair_grad = wide_sum(pair_own, from_y) + wide_sum(from_shard, from_both)
    attn_norm_sum = sum_parts(inner_cols(query_pre_low, query_w))
    key_pre_grad, key_gain = key_back(pair_grad[:, :HD])
    key_pre_low = key_pre_grad.astype(BF)
    value_grad_low = pair_grad[:, HD:].astype(BF)
    pair_part = inner_cols(jnp.concatenate([key_pre_low, value_grad_low], 1), pair_w).astype(BF)
    attn_norm_grad = attn_norm_sum + reorder(pair_part, from_ring).astype(F32)
    input_from, gain_one = pre_attn_back(attn_norm_grad)
    input_grad = mid_grad + input_from

    kept, sent = pick(core, key_pre_low, value_grad_low), pick(core, value_grad_low, key_pre_low)
    pair_chip = jnp.concatenate([kept, shift(sent, "c")], 0)
    heads = [
        jnp.pad(gain.reshape(64, HD // 64), ((0, 0), (0, piece - HD // 64))).reshape(width)
        for gain in (query_gain, key_gain)
    ]
    gains = jnp.stack([gain_one, gain_two, gain_three, gain_four] + heads, 1)
    gains = jnp.pad(gains, ((0, 0), (0, 128 - gains.shape[1]))).astype(BF)
    late_grads = jnp.concatenate([inner_rows(attn_chip, pair_chip), inner_rows(to_ring, gains)], 1).astype(BF)
    late_major = reduce_direct(split_rows(late_grads, 4), True).astype(BF)
    late_sum = reduce_direct(split_rows(late_major, 4), False)
    head_mine, head_got = last_stage(jnp.concatenate([minor_sum[2 * tokens :], late_sum], 1))

    ffn_major = reduce_ring(*ffn_chunks, True, (pair_far,), (major_sum,)).astype(BF)
    ffn_mine, ffn_got = last_stage(reduce_chunks(*split_rows(ffn_major, 4), False))

    def joined(start, size, mine, got):
        left, right = mine[:, start : start + size], got[:, start : start + size]
        return pick(core, jnp.concatenate([left, right], 1), jnp.concatenate([right, left], 1))

    gate_wgrad = joined(0, units, ffn_mine, ffn_got)
    up_wgrad = joined(padded, units, ffn_mine, ffn_got)
    down_wgrad = joined(2 * padded, units, ffn_mine, ffn_got).T

    query_wgrad = joined(0, HD, head_mine, head_got)
    out_wgrad = joined(HD, HD, head_mine, head_got).T
    pair_wgrad = joined(2 * HD, HD, head_mine, head_got)
    gain_sums = head_mine[:, 3 * HD :] + head_got[:, 3 * HD :]
    return (
        block_out,
        input_grad,
        query_wgrad,
        pair_wgrad[:, :HD],
        pair_wgrad[:, HD:],
        out_wgrad,
        gate_wgrad,
        up_wgrad,
        down_wgrad,
        gain_sums[:, :4].T,
        gain_sums[: HD // 64, 4:6].T,
    )


def solution(mesh):
    fine = Mesh(mesh.devices.reshape(2, 4, 4, 2, 2), ("y", "z", "x", "c", "s"))
    placed = (
        P(CTX, None),
        P(CTX, None),
        P(),
        P(),
        P(),
        P(CTX, "s"),
        P(CTX, None),
        P(CTX, None),
        P("s", CTX),
        P(CTX, "s"),
        P(CTX, "s"),
        P("s", CTX),
    )
    return jax.shard_map(
        shards,
        mesh=fine,
        in_specs=placed,
        out_specs=(
            P(CTX, None),
            P(CTX, None),
            P(CTX, "s"),
            P(CTX, None),
            P(CTX, None),
            P("s", CTX),
            P(CTX, "s"),
            P(CTX, "s"),
            P("s", CTX),
            P(None, CTX),
            P(None, CTX),
        ),
        check_vma=False,
    )
```

```python
import math

import jax
import jax.numpy as jnp
from jax import lax
from jax.experimental import pallas as pl
from jax.experimental.pallas import tpu as pltpu
from jax.sharding import Mesh, PartitionSpec as P

HD = 256
EPS = 1e-06
THETA = 1000000.0
BF = jnp.bfloat16
F32 = jnp.float32
CTX = ("y", "z", "x", "c")


def matmul(left, right):
    return jnp.dot(left, right, preferred_element_type=F32)


def inner_rows(left, right):
    return lax.dot_general(left, right, (((0,), (0,)), ((), ())), preferred_element_type=F32)


def inner_cols(left, right):
    return lax.dot_general(left, right, (((1,), (1,)), ((), ())), preferred_element_type=F32)


def rms_scale(values, gain):
    return values * lax.rsqrt(jnp.mean(values * values, axis=-1, keepdims=True) + EPS) * gain


def rotate(values, cosine_table, sine_table):
    half_width = values.shape[-1] // 2
    first = values[..., :half_width]
    second = values[..., half_width:]
    return jnp.concatenate(
        [first * cosine_table - second * sine_table, second * cosine_table + first * sine_table],
        axis=-1,
    )


def tables(positions, head_width):
    frequency = jnp.arange(head_width // 2, dtype=F32)
    inverse = jnp.exp(frequency * (-2.0 * math.log(THETA) / head_width))
    angles = positions.astype(F32)[:, None] * inverse[None, :]
    return (jnp.cos(angles), jnp.sin(angles))


def shift(values, axis, step=1):
    size = lax.axis_size(axis)
    return lax.ppermute(values, axis, [(i, (i + step) % size) for i in range(size)])


def ring(values, major, step, cross_y=False):
    moves = []
    for y in range(2):
        for z in range(4):
            for x in range(4):
                for core in range(2):
                    along_x = major == (core == 0)
                    to_z, to_x = (z, (x + step) % 4) if along_x else ((z + step) % 4, x)
                    to_y = 1 - y if cross_y else y
                    moves.append((y * 32 + z * 8 + x * 2 + core, to_y * 32 + to_z * 8 + to_x * 2 + core))
    return lax.ppermute(values, CTX, moves)


def gather_direct(block, major):
    return jnp.concatenate([block] + [ring(block, major, -k) for k in (1, 2, 3)], 0)


def gather_minor_y(block):
    blocks = [block if k == 0 else ring(block, False, -k) for k in range(4)]
    others = [ring(block, False, -k, True) for k in range(4)]
    return jnp.concatenate([part for pair in zip(blocks, others) for part in pair], 0)


def exchange(values, axis):
    both = [(i, 3 - i) for i in range(4)]
    return shift(values[0], "y"), shift(values[1], axis), lax.ppermute(values[2], ("y", axis), both)


def after(value, *others):
    return lax.optimization_barrier((value, *others))[0]


def gather_ring(block, major, *others):
    half = (block.shape[0] // 2 + 7) // 8 * 8
    previous = ring(block, major, 1)
    following = ring(block, major, -1)
    far_low = ring(after(previous, *others)[:half], major, 1)
    far_high = ring(after(following, *others)[half:], major, -1)
    return [block, following, far_low, far_high, previous]


def wide_sum(*parts):
    return sum(part.astype(F32) for part in parts)


def reduce_direct(chunks, major):
    return wide_sum(chunks[0], *[ring(chunks[k], major, k) for k in (1, 2, 3)])


def reduce_ring(own, following, far_low, far_high, previous, major, others=(), last=()):
    half = far_low.shape[0]
    from_previous = after(ring(far_low, major, 1), *others)
    from_next = after(ring(far_high, major, -1), *others)
    forward = jnp.concatenate(
        [wide_sum(following[:half], from_previous).astype(BF), following[half:]], 0
    )
    backward = jnp.concatenate(
        [previous[:half], wide_sum(previous[half:], from_next).astype(BF)], 0
    )
    return wide_sum(after(own, *last), ring(forward, major, 1), ring(backward, major, -1))


def reduce_chunks(own, following, far, previous, major):
    half = (far.shape[0] // 2 + 7) // 8 * 8
    return reduce_ring(own, following, far[:half], far[half:], previous, major)


ATTN_BLOCK = 1024
VMEM = pltpu.CompilerParams(vmem_limit_bytes=48 * 1024 * 1024)


def attend_kernel(query, pair, key_pos, query_pos, weight, total, accum):
    scores = inner_cols(query[...], pair[:, :HD])
    exps = jnp.where(query_pos[...] >= key_pos[...], jnp.exp(scores), 0.0)
    low = exps.astype(BF)
    weight[...] = low

    @pl.when(pl.program_id(0) == 0)
    def _():
        total[...] = jnp.zeros_like(total)
        accum[...] = jnp.zeros_like(accum)

    total[...] += jnp.sum(exps, axis=1, keepdims=True)
    accum[...] += matmul(low, pair[:, HD:])


def attend(queries, pairs, key_pos, query_pos):
    rows, keys = queries.shape[0], pairs.shape[0]
    whole = lambda i: (0, 0)
    return pl.pallas_call(
        attend_kernel,
        grid=(keys // ATTN_BLOCK,),
        in_specs=[
            pl.BlockSpec((rows, HD), whole),
            pl.BlockSpec((ATTN_BLOCK, 2 * HD), lambda i: (i, 0)),
            pl.BlockSpec((1, ATTN_BLOCK), lambda i: (0, i)),
            pl.BlockSpec((rows, 1), whole),
        ],
        out_specs=[
            pl.BlockSpec((rows, ATTN_BLOCK), lambda i: (0, i)),
            pl.BlockSpec((rows, 1), whole),
            pl.BlockSpec((rows, HD), whole),
        ],
        out_shape=[
            jax.ShapeDtypeStruct((rows, keys), BF),
            jax.ShapeDtypeStruct((rows, 1), F32),
            jax.ShapeDtypeStruct((rows, HD), F32),
        ],
        compiler_params=VMEM,
        name="attend",
    )(queries, pairs, key_pos[None, :], query_pos[:, None])


def attend_back_kernel(query, pair, weight, grad, scaled, dot, inverse, pair_grad, query_grad):
    weights = weight[...]
    prob_grad = inner_cols(grad[...], pair[:, HD:])
    score_grad = (weights.astype(F32) * ((prob_grad - dot[...]) * inverse[...])).astype(BF)
    pair_grad[:, :HD] = inner_rows(score_grad, query[...]).astype(BF)
    pair_grad[:, HD:] = inner_rows(weights, scaled[...]).astype(BF)

    @pl.when(pl.program_id(0) == 0)
    def _():
        query_grad[...] = jnp.zeros_like(query_grad)

    query_grad[...] += matmul(score_grad, pair[:, :HD])


def attend_back(queries, pairs, weights, grads, scaled, dot, inverse):
    rows, keys = queries.shape[0], pairs.shape[0]
    whole = lambda i: (0, 0)
    return pl.pallas_call(
        attend_back_kernel,
        grid=(keys // ATTN_BLOCK,),
        in_specs=[
            pl.BlockSpec((rows, HD), whole),
            pl.BlockSpec((ATTN_BLOCK, 2 * HD), lambda i: (i, 0)),
            pl.BlockSpec((rows, ATTN_BLOCK), lambda i: (0, i)),
            pl.BlockSpec((rows, HD), whole),
            pl.BlockSpec((rows, HD), whole),
            pl.BlockSpec((rows, 1), whole),
            pl.BlockSpec((rows, 1), whole),
        ],
        out_specs=[
            pl.BlockSpec((ATTN_BLOCK, 2 * HD), lambda i: (i, 0)),
            pl.BlockSpec((rows, HD), whole),
        ],
        out_shape=[
            jax.ShapeDtypeStruct((keys, 2 * HD), BF),
            jax.ShapeDtypeStruct((rows, HD), F32),
        ],
        compiler_params=VMEM,
        name="attend_back",
    )(queries, pairs, weights, grads, scaled, dot, inverse)


def stack_kernel(*refs):
    start = 0
    for piece in refs[:-1]:
        refs[-1][start : start + piece.shape[0], :] = piece[...]
        start += piece.shape[0]


def stack_rows(pieces, tile=256):
    rows, columns = sum(piece.shape[0] for piece in pieces), pieces[0].shape[1]
    return pl.pallas_call(
        stack_kernel,
        grid=(columns // tile,),
        in_specs=[pl.BlockSpec((piece.shape[0], tile), lambda j: (0, j)) for piece in pieces],
        out_specs=pl.BlockSpec((rows, tile), lambda j: (0, j)),
        out_shape=jax.ShapeDtypeStruct((rows, columns), pieces[0].dtype),
        compiler_params=VMEM,
        name="stack_rows",
    )(*pieces)


UNIT_TILE = 256
GELU_IN = math.sqrt(2.0 / math.pi)
GELU_CUBE = 0.044715


def joined_rows(refs):
    return jnp.concatenate([ref[...] for ref in refs], 0)


def ffn_kernel(source, *refs):
    count = (len(refs) - 4) // 3
    gate_w, up_w, down_w = (joined_rows(refs[i * count : (i + 1) * count]) for i in range(3))
    gate, up, hidden, total = refs[3 * count :]
    gate_pre = matmul(source[...], gate_w)
    up_pre = matmul(source[...], up_w)
    gate[...] = gate_pre
    up[...] = up_pre
    inner = GELU_IN * (gate_pre + GELU_CUBE * (gate_pre * gate_pre * gate_pre))
    low = (0.5 * gate_pre * (1.0 + jnp.tanh(inner)) * up_pre).astype(BF)
    hidden[...] = low

    @pl.when(pl.program_id(0) == 0)
    def _():
        total[...] = jnp.zeros_like(total)

    total[...] += inner_cols(low, down_w)


def ffn_back_kernel(grad, gate, up, *refs):
    count = (len(refs) - 3) // 3
    gate_w, up_w, down_w = (joined_rows(refs[i * count : (i + 1) * count]) for i in range(3))
    gate_grad, up_grad, total = refs[3 * count :]
    hidden_grad = matmul(grad[...], down_w)
    gate_pre = gate[...]
    square = gate_pre * gate_pre
    bend = jnp.tanh(GELU_IN * (gate_pre + GELU_CUBE * (square * gate_pre)))
    rise = 0.5 * (1.0 + bend)
    slope = rise + 0.5 * gate_pre * (1.0 - bend * bend) * (GELU_IN * (1.0 + 3.0 * GELU_CUBE * square))
    gate_low = (hidden_grad * up[...] * slope).astype(BF)
    up_low = (hidden_grad * (gate_pre * rise)).astype(BF)
    gate_grad[...] = gate_low
    up_grad[...] = up_low

    @pl.when(pl.program_id(0) == 0)
    def _():
        total[...] = jnp.zeros_like(total)

    total[...] += inner_cols(gate_low, gate_w) + inner_cols(up_low, up_w)


def unit_specs(rows, pieces, tiles):
    own = pl.BlockSpec((rows, UNIT_TILE), lambda j: (0, j))
    weights = [
        pl.BlockSpec((piece.shape[0], UNIT_TILE), lambda j, i=i: (0, j + i * tiles))
        for i in range(3)
        for piece in pieces
    ]
    return own, weights


def ffn_forward(source, pieces):
    rows, width = source.shape
    units = pieces[0].shape[1] // 3
    tiles = units // UNIT_TILE
    own, weights = unit_specs(rows, pieces, tiles)
    whole = pl.BlockSpec((rows, width), lambda j: (0, 0))
    return pl.pallas_call(
        ffn_kernel,
        grid=(tiles,),
        in_specs=[whole] + weights,
        out_specs=[own, own, own, whole],
        out_shape=[
            jax.ShapeDtypeStruct((rows, units), F32),
            jax.ShapeDtypeStruct((rows, units), F32),
            jax.ShapeDtypeStruct((rows, units), BF),
            jax.ShapeDtypeStruct((rows, width), F32),
        ],
        compiler_params=VMEM,
        name="ffn_forward",
    )(source, *pieces, *pieces, *pieces)


def ffn_backward(grad, gate, up, pieces):
    rows, width = grad.shape
    units = pieces[0].shape[1] // 3
    tiles = units // UNIT_TILE
    own, weights = unit_specs(rows, pieces, tiles)
    whole = pl.BlockSpec((rows, width), lambda j: (0, 0))
    return pl.pallas_call(
        ffn_back_kernel,
        grid=(tiles,),
        in_specs=[whole, own, own] + weights,
        out_specs=[own, own, whole],
        out_shape=[
            jax.ShapeDtypeStruct((rows, units), BF),
            jax.ShapeDtypeStruct((rows, units), BF),
            jax.ShapeDtypeStruct((rows, width), F32),
        ],
        compiler_params=VMEM,
        name="ffn_backward",
    )(grad, gate, up, *pieces, *pieces, *pieces)


def ffn_wgrad_kernel(steps, count, left, *refs):
    for i, right in enumerate(refs[:count]):

        @pl.when(pl.program_id(0) // steps == i)
        def _(right=right):
            start = 0
            for out in refs[count:]:
                size = out.shape[0]
                out[...] = matmul(left[start : start + size, :], right[...]).astype(BF)
                start += size


def ffn_wgrad(left, *rights):
    width, (rows, units), count = left.shape[0], rights[0].shape, len(rights)
    steps = 2
    tile = units // steps
    sizes = [width // 4, width // 4, width // 8, width // 8, width // 4]

    def spec(i):
        return pl.BlockSpec((rows, tile), lambda j: (0, jnp.clip(j - i * steps, 0, steps - 1)))

    return pl.pallas_call(
        lambda *refs: ffn_wgrad_kernel(steps, count, *refs),
        grid=(count * steps,),
        in_specs=[pl.BlockSpec(left.shape, lambda j: (0, 0))] + [spec(i) for i in range(count)],
        out_specs=[pl.BlockSpec((size, tile), lambda j: (0, j)) for size in sizes],
        out_shape=[jax.ShapeDtypeStruct((size, count * units), BF) for size in sizes],
        compiler_params=VMEM,
        name="ffn_wgrad",
    )(left, *rights)


def split_rows(values, parts):
    size = values.shape[0] // parts
    return [values[i * size : (i + 1) * size] for i in range(parts)]


def pick(core, first, second):
    return jnp.where(core == 0, first, second)


def shards(
    hidden_in,
    out_grad,
    block_order,
    norm_gains,
    head_gains,
    w_query,
    w_key,
    w_value,
    w_out,
    w_gate,
    w_up,
    w_down,
):
    tokens, width = hidden_in.shape
    y, z, x, core = (lax.axis_index(name) for name in CTX)
    other = 1 - core
    piece = width // 64
    units = w_gate.shape[1] // 2
    padded = (units + 127) // 128 * 128
    quarter = width // 4

    out_t, down_t = w_out.T, w_down.T

    def units_of(which):
        cut = [
            jnp.pad(lax.dynamic_slice_in_dim(w, which * units, units, 1), ((0, 0), (0, padded - units)))
            for w in (w_gate, w_up, down_t)
        ]
        return jnp.concatenate(cut, 1)

    def heads_of(which):
        cut = [lax.dynamic_slice_in_dim(w, which * HD, HD, 1) for w in (w_query, out_t)]
        return jnp.concatenate(cut + [w_key, w_value], 1)

    def chip_rows(of):
        mine, theirs = of(core), of(other)
        from_y, from_core, from_both = exchange((mine, theirs, theirs), "c")
        return pick(
            core,
            jnp.concatenate([mine, from_core, from_y, from_both], 0),
            jnp.concatenate([from_core, mine, from_both, from_y], 0),
        )

    head_rows = chip_rows(heads_of)
    ffn_rows = chip_rows(units_of)
    head_minor = after(gather_direct(head_rows, False), ffn_rows)
    head_pieces = gather_ring(head_minor, True)
    head_w = stack_rows(head_pieces)
    hidden_in = after(hidden_in, head_rows)
    query_w, out_w = head_w[:, :HD], head_w[:, HD : 2 * HD]
    key_w, value_w, pair_w = head_w[:, 2 * HD : 3 * HD], head_w[:, 3 * HD :], head_w[:, 2 * HD :]

    place = jnp.arange(width, dtype=jnp.int32)
    first, second = place // quarter, place // (quarter // 4) % 4
    z_at, x_at = (z + pick(core, second, first)) % 4, (x + pick(core, first, second)) % 4
    y_at = (y + place // (2 * piece)) % 2
    by_ring = y_at * (width // 2) + z_at * (8 * piece) + x_at * (2 * piece) + place % (2 * piece)
    to_ring = (place[:, None] == by_ring[None, :]).astype(BF)
    from_ring = (by_ring[:, None] == place[None, :]).astype(BF)

    def reorder(values, moves):
        return matmul(values, moves).astype(BF)

    def both_cores(values):
        return jnp.concatenate([values, shift(values, "c")], 0)

    def sum_parts(partial):
        low = reorder(partial.astype(BF), from_ring)
        chip = (low[:tokens].astype(F32) + shift(low[tokens:], "c").astype(F32)).astype(BF)
        return chip.astype(F32) + shift(chip, "s").astype(F32)

    offsets = jnp.arange(tokens, dtype=jnp.int32)

    def positions_of(places):
        return (block_order[places.reshape(-1)][:, None] * tokens + offsets[None, :]).reshape(-1)

    def device_of(y_at, z_at, x_at, core_at):
        return y_at * 32 + z_at * 8 + x_at * 2 + core_at

    steps = jnp.arange(4, dtype=jnp.int32)
    outer, inner = steps[:, None, None], steps[None, :, None]

    def keys_of(which):
        z_at, x_at = (z + pick(which, inner, outer)) % 4, (x + pick(which, outer, inner)) % 4
        return positions_of(device_of((y + steps[None, None, :2]) % 2, z_at, x_at, which))

    key_pos = [keys_of(core), keys_of(other)]
    own_pos = positions_of(device_of(y, z, x, core))
    chip_pos = jnp.concatenate([own_pos, positions_of(device_of(y, z, x, other))])
    cosine_table, sine_table = tables(chip_pos, HD)

    attn_val, pre_attn_back = jax.vjp(rms_scale, hidden_in, norm_gains[0])
    attn_chip = reorder(both_cores(attn_val.astype(BF)), to_ring)
    attn_ring = attn_chip[:tokens]
    key_pre = matmul(attn_ring, key_w)
    value_low = matmul(attn_ring, value_w).astype(BF)
    key_val, key_back = jax.vjp(
        lambda values, gain: rotate(rms_scale(values, gain), cosine_table[:tokens], sine_table[:tokens]),
        key_pre,
        head_gains[1],
    )
    key_low = key_val.astype(BF)
    pair_low = jnp.concatenate([key_low, value_low], 1)
    ffn_rows = after(ffn_rows, head_pieces[1], head_pieces[4])
    ffn_minor = jnp.concatenate(gather_ring(ffn_rows, False, pair_low), 0)
    pair_pieces = gather_ring(gather_minor_y(pair_low), True, ffn_minor)
    ffn_w = gather_ring(after(ffn_minor, pair_pieces[1], pair_pieces[4]), True)
    own_pairs = jnp.concatenate(pair_pieces, 0)
    pairs = [own_pairs, shift(own_pairs, "c")]

    query_pre = matmul(attn_chip, query_w)
    query_val, query_back = jax.vjp(
        lambda values, gain: rotate(rms_scale(values, gain), cosine_table, sine_table),
        query_pre,
        head_gains[0],
    )
    score_scale = HD ** (-0.5)
    queries = (query_val.astype(BF).astype(F32) * score_scale).astype(BF)
    parts = [attend(queries, pairs[part], key_pos[part], chip_pos) for part in range(2)]
    weights = [part[0] for part in parts]
    inverse_total = 1.0 / (parts[0][1] + parts[1][1])
    accum = parts[0][2] + parts[1][2]
    attn_rows = accum * inverse_total
    mixed_low = after(attn_rows.astype(BF), ffn_w[1], ffn_w[4])
    attn_out = sum_parts(inner_cols(mixed_low, out_w))
    post_attn, post_attn_back = jax.vjp(rms_scale, attn_out, norm_gains[1])
    mid_state = hidden_in + post_attn

    ffn_val, ffn_norm_back = jax.vjp(rms_scale, mid_state, norm_gains[2])
    ffn_chip = both_cores(ffn_val.astype(BF))
    gate_pre, up_pre, hidden_low, ffn_part = ffn_forward(reorder(ffn_chip, to_ring), ffn_w)
    ffn_out = sum_parts(ffn_part)
    post_ffn, post_ffn_back = jax.vjp(rms_scale, ffn_out, norm_gains[3])
    block_out = mid_state + post_ffn

    ffn_grad, gain_four = post_ffn_back(out_grad)
    ffn_grad_chip = both_cores(ffn_grad.astype(BF))
    down_chunks = ffn_wgrad(inner_cols(from_ring, ffn_grad_chip).astype(BF), hidden_low)
    ffn_grad_ring = after(reorder(ffn_grad_chip, to_ring), *down_chunks)
    gate_low, up_low, ffn_norm_part = ffn_backward(ffn_grad_ring, gate_pre, up_pre, ffn_w)
    ffn_norm_grad = sum_parts(ffn_norm_part)
    gate_up_chunks = ffn_wgrad(inner_cols(from_ring, ffn_chip).astype(BF), gate_low, up_low)
    mid_from, gain_three = ffn_norm_back(after(ffn_norm_grad, *gate_up_chunks))
    mid_grad = out_grad + mid_from

    def last_stage(values):
        parts = split_rows(values.astype(BF), 4)
        kept = [pick(core, parts[i], parts[i + 1]) for i in (0, 2)]
        sent = [pick(core, parts[i + 1], parts[i]) for i in (0, 2)]
        from_y, from_core, from_both = exchange((kept[1], sent[0], sent[1]), "c")
        return wide_sum(kept[0], from_y), wide_sum(from_core, from_both)

    attn_grad, gain_two = post_attn_back(mid_grad)
    attn_grad_chip = reorder(both_cores(attn_grad.astype(BF)), to_ring)
    rows_grad = matmul(attn_grad_chip, out_w).astype(BF)
    rows_wide = rows_grad.astype(F32)
    row_dot = jnp.sum(rows_wide * attn_rows, axis=1)[:, None]
    rows_scaled = (rows_wide * inverse_total).astype(BF)
    pair_far, query_far = attend_back(
        queries, pairs[1], weights[1], rows_grad, rows_scaled, row_dot, inverse_total
    )
    pair_near, query_near = attend_back(
        queries, pairs[0], weights[0], rows_grad, rows_scaled, row_dot, inverse_total
    )
    query_grad = query_far + query_near
    query_pre_grad, query_gain = query_back(query_grad * score_scale)
    query_gain = query_gain + shift(query_gain, "s")
    query_pre_low = query_pre_grad.astype(BF)
    early_grads = jnp.concatenate(
        [inner_rows(attn_chip, query_pre_low), inner_rows(attn_grad_chip, mixed_low)], 1
    ).astype(BF)
    pair_got = shift(pair_far, "c")
    chunks = [
        jnp.concatenate([wide_sum(near, got).astype(BF), early], 0)
        for near, got, early in zip(*(split_rows(part, 4) for part in (pair_near, pair_got, early_grads)))
    ]
    major_sum = reduce_chunks(*chunks, True).astype(BF)
    pair_chunks = split_rows(major_sum[: 8 * tokens], 4)
    early_chunks = split_rows(major_sum[8 * tokens :], 4)
    minor_sum = reduce_direct(
        [jnp.concatenate([pair, early], 0) for pair, early in zip(pair_chunks, early_chunks)], False
    )
    pair_own, pair_far_y = split_rows(minor_sum[: 2 * tokens].astype(BF), 2)
    from_y, from_shard, from_both = exchange((pair_far_y, pair_own, pair_far_y), "s")
    pair_grad = wide_sum(pair_own, from_y) + wide_sum(from_shard, from_both)
    attn_norm_sum = sum_parts(inner_cols(query_pre_low, query_w))
    key_pre_grad, key_gain = key_back(pair_grad[:, :HD])
    key_pre_low = key_pre_grad.astype(BF)
    value_grad_low = pair_grad[:, HD:].astype(BF)
    pair_part = inner_cols(jnp.concatenate([key_pre_low, value_grad_low], 1), pair_w).astype(BF)
    attn_norm_grad = attn_norm_sum + reorder(pair_part, from_ring).astype(F32)
    input_from, gain_one = pre_attn_back(attn_norm_grad)
    input_grad = mid_grad + input_from

    kept, sent = pick(core, key_pre_low, value_grad_low), pick(core, value_grad_low, key_pre_low)
    pair_chip = jnp.concatenate([kept, shift(sent, "c")], 0)
    heads = [
        jnp.pad(gain.reshape(64, HD // 64), ((0, 0), (0, piece - HD // 64))).reshape(width)
        for gain in (query_gain, key_gain)
    ]
    gains = jnp.stack([gain_one, gain_two, gain_three, gain_four] + heads, 1)
    gains = jnp.pad(gains, ((0, 0), (0, 128 - gains.shape[1]))).astype(BF)
    late_grads = jnp.concatenate([inner_rows(attn_chip, pair_chip), inner_rows(to_ring, gains)], 1).astype(BF)
    late_major = reduce_direct(split_rows(late_grads, 4), True).astype(BF)
    late_sum = reduce_direct(split_rows(late_major, 4), False)
    head_mine, head_got = last_stage(jnp.concatenate([minor_sum[2 * tokens :], late_sum], 1))

    down_major = reduce_ring(*down_chunks, True, (ffn_norm_part,), (pair_far,)).astype(BF)
    down_mine, down_got = last_stage(reduce_direct(split_rows(down_major, 4), False))
    ffn_major = reduce_ring(*gate_up_chunks, True, (major_sum,), (late_major,)).astype(BF)
    ffn_mine, ffn_got = last_stage(reduce_chunks(*split_rows(ffn_major, 4), False))

    def joined(start, size, mine, got):
        left, right = mine[:, start : start + size], got[:, start : start + size]
        return pick(core, jnp.concatenate([left, right], 1), jnp.concatenate([right, left], 1))

    gate_wgrad = joined(0, units, ffn_mine, ffn_got)
    up_wgrad = joined(padded, units, ffn_mine, ffn_got)
    down_wgrad = joined(0, units, down_mine, down_got).T

    query_wgrad = joined(0, HD, head_mine, head_got)
    out_wgrad = joined(HD, HD, head_mine, head_got).T
    pair_wgrad = joined(2 * HD, HD, head_mine, head_got)
    gain_sums = head_mine[:, 3 * HD :] + head_got[:, 3 * HD :]
    return (
        block_out,
        input_grad,
        query_wgrad,
        pair_wgrad[:, :HD],
        pair_wgrad[:, HD:],
        out_wgrad,
        gate_wgrad,
        up_wgrad,
        down_wgrad,
        gain_sums[:, :4].T,
        gain_sums[: HD // 64, 4:6].T,
    )


def solution(mesh):
    fine = Mesh(mesh.devices.reshape(2, 4, 4, 2, 2), ("y", "z", "x", "c", "s"))
    placed = (
        P(CTX, None),
        P(CTX, None),
        P(),
        P(),
        P(),
        P(CTX, "s"),
        P(CTX, None),
        P(CTX, None),
        P("s", CTX),
        P(CTX, "s"),
        P(CTX, "s"),
        P("s", CTX),
    )
    return jax.shard_map(
        shards,
        mesh=fine,
        in_specs=placed,
        out_specs=(
            P(CTX, None),
            P(CTX, None),
            P(CTX, "s"),
            P(CTX, None),
            P(CTX, None),
            P("s", CTX),
            P(CTX, "s"),
            P(CTX, "s"),
            P("s", CTX),
            P(None, CTX),
            P(None, CTX),
        ),
        check_vma=False,
    )
```

```python
import math

import jax
import jax.numpy as jnp
from jax import lax
from jax.experimental import pallas as pl
from jax.experimental.pallas import tpu as pltpu
from jax.sharding import Mesh, PartitionSpec as P

HD = 256
EPS = 1e-06
THETA = 1000000.0
BF = jnp.bfloat16
F32 = jnp.float32
CTX = ("y", "z", "x", "c")


def matmul(left, right):
    return jnp.dot(left, right, preferred_element_type=F32)


def inner_rows(left, right):
    return lax.dot_general(left, right, (((0,), (0,)), ((), ())), preferred_element_type=F32)


def inner_cols(left, right):
    return lax.dot_general(left, right, (((1,), (1,)), ((), ())), preferred_element_type=F32)


def rms_scale(values, gain):
    return values * lax.rsqrt(jnp.mean(values * values, axis=-1, keepdims=True) + EPS) * gain


def rotate(values, cosine_table, sine_table):
    half_width = values.shape[-1] // 2
    first = values[..., :half_width]
    second = values[..., half_width:]
    return jnp.concatenate(
        [first * cosine_table - second * sine_table, second * cosine_table + first * sine_table],
        axis=-1,
    )


def tables(positions, head_width):
    frequency = jnp.arange(head_width // 2, dtype=F32)
    inverse = jnp.exp(frequency * (-2.0 * math.log(THETA) / head_width))
    angles = positions.astype(F32)[:, None] * inverse[None, :]
    return (jnp.cos(angles), jnp.sin(angles))


def shift(values, axis, step=1):
    size = lax.axis_size(axis)
    return lax.ppermute(values, axis, [(i, (i + step) % size) for i in range(size)])


def ring(values, major, step, cross_y=False):
    moves = []
    for y in range(2):
        for z in range(4):
            for x in range(4):
                for core in range(2):
                    along_x = major == (core == 0)
                    to_z, to_x = (z, (x + step) % 4) if along_x else ((z + step) % 4, x)
                    to_y = 1 - y if cross_y else y
                    moves.append((y * 32 + z * 8 + x * 2 + core, to_y * 32 + to_z * 8 + to_x * 2 + core))
    return lax.ppermute(values, CTX, moves)


def gather_direct(block, major):
    return jnp.concatenate([block] + [ring(block, major, -k) for k in (1, 2, 3)], 0)


def gather_minor_y(block):
    blocks = [block if k == 0 else ring(block, False, -k) for k in range(4)]
    others = [ring(block, False, -k, True) for k in range(4)]
    return jnp.concatenate([part for pair in zip(blocks, others) for part in pair], 0)


def exchange(values, axis):
    both = [(i, 3 - i) for i in range(4)]
    return shift(values[0], "y"), shift(values[1], axis), lax.ppermute(values[2], ("y", axis), both)


def after(value, *others):
    return lax.optimization_barrier((value, *others))[0]


def gather_first(block, major):
    return ring(block, major, 1), ring(block, major, -1)


def gather_ring(block, major, *others, first=None):
    half = (block.shape[0] // 2 + 7) // 8 * 8
    previous, following = first or gather_first(block, major)
    far_low = ring(after(previous, *others)[:half], major, 1)
    far_high = ring(after(following, *others)[half:], major, -1)
    return [block, following, far_low, far_high, previous]


def wide_sum(*parts):
    return sum(part.astype(F32) for part in parts)


def reduce_direct(chunks, major):
    return wide_sum(chunks[0], *[ring(chunks[k], major, k) for k in (1, 2, 3)])


def reduce_first(far_low, far_high, major):
    return ring(far_low, major, 1), ring(far_high, major, -1)


def reduce_second(own, following, previous, from_previous, from_next, major, *others):
    half = from_previous.shape[0]
    forward = jnp.concatenate(
        [wide_sum(following[:half], from_previous).astype(BF), following[half:]], 0
    )
    backward = jnp.concatenate(
        [previous[:half], wide_sum(previous[half:], from_next).astype(BF)], 0
    )
    return wide_sum(own, ring(after(forward, *others), major, 1), ring(after(backward, *others), major, -1))


def reduce_chunks(own, following, far, previous, major):
    half = (far.shape[0] // 2 + 7) // 8 * 8
    return reduce_second(own, following, previous, *reduce_first(far[:half], far[half:], major), major)


ATTN_BLOCK = 1024
VMEM = pltpu.CompilerParams(vmem_limit_bytes=48 * 1024 * 1024)


def attend_kernel(query, pair, key_pos, query_pos, weight, total, accum):
    scores = inner_cols(query[...], pair[:, :HD])
    exps = jnp.where(query_pos[...] >= key_pos[...], jnp.exp(scores), 0.0)
    low = exps.astype(BF)
    weight[...] = low

    @pl.when(pl.program_id(0) == 0)
    def _():
        total[...] = jnp.zeros_like(total)
        accum[...] = jnp.zeros_like(accum)

    total[...] += jnp.sum(exps, axis=1, keepdims=True)
    accum[...] += matmul(low, pair[:, HD:])


def attend(queries, pairs, key_pos, query_pos):
    rows, keys = queries.shape[0], pairs.shape[0]
    whole = lambda i: (0, 0)
    return pl.pallas_call(
        attend_kernel,
        grid=(keys // ATTN_BLOCK,),
        in_specs=[
            pl.BlockSpec((rows, HD), whole),
            pl.BlockSpec((ATTN_BLOCK, 2 * HD), lambda i: (i, 0)),
            pl.BlockSpec((1, ATTN_BLOCK), lambda i: (0, i)),
            pl.BlockSpec((rows, 1), whole),
        ],
        out_specs=[
            pl.BlockSpec((rows, ATTN_BLOCK), lambda i: (0, i)),
            pl.BlockSpec((rows, 1), whole),
            pl.BlockSpec((rows, HD), whole),
        ],
        out_shape=[
            jax.ShapeDtypeStruct((rows, keys), BF),
            jax.ShapeDtypeStruct((rows, 1), F32),
            jax.ShapeDtypeStruct((rows, HD), F32),
        ],
        compiler_params=VMEM,
        name="attend",
    )(queries, pairs, key_pos[None, :], query_pos[:, None])


def attend_back_kernel(query, pair, weight, grad, scaled, dot, inverse, pair_grad, query_grad):
    weights = weight[...]
    prob_grad = inner_cols(grad[...], pair[:, HD:])
    score_grad = (weights.astype(F32) * ((prob_grad - dot[...]) * inverse[...])).astype(BF)
    pair_grad[:, :HD] = inner_rows(score_grad, query[...]).astype(BF)
    pair_grad[:, HD:] = inner_rows(weights, scaled[...]).astype(BF)

    @pl.when(pl.program_id(0) == 0)
    def _():
        query_grad[...] = jnp.zeros_like(query_grad)

    query_grad[...] += matmul(score_grad, pair[:, :HD])


def attend_back(queries, pairs, weights, grads, scaled, dot, inverse):
    rows, keys = queries.shape[0], pairs.shape[0]
    whole = lambda i: (0, 0)
    return pl.pallas_call(
        attend_back_kernel,
        grid=(keys // ATTN_BLOCK,),
        in_specs=[
            pl.BlockSpec((rows, HD), whole),
            pl.BlockSpec((ATTN_BLOCK, 2 * HD), lambda i: (i, 0)),
            pl.BlockSpec((rows, ATTN_BLOCK), lambda i: (0, i)),
            pl.BlockSpec((rows, HD), whole),
            pl.BlockSpec((rows, HD), whole),
            pl.BlockSpec((rows, 1), whole),
            pl.BlockSpec((rows, 1), whole),
        ],
        out_specs=[
            pl.BlockSpec((ATTN_BLOCK, 2 * HD), lambda i: (i, 0)),
            pl.BlockSpec((rows, HD), whole),
        ],
        out_shape=[
            jax.ShapeDtypeStruct((keys, 2 * HD), BF),
            jax.ShapeDtypeStruct((rows, HD), F32),
        ],
        compiler_params=VMEM,
        name="attend_back",
    )(queries, pairs, weights, grads, scaled, dot, inverse)


def stack_kernel(*refs):
    start = 0
    for piece in refs[:-1]:
        refs[-1][start : start + piece.shape[0], :] = piece[...]
        start += piece.shape[0]


def stack_rows(pieces, tile=256):
    rows, columns = sum(piece.shape[0] for piece in pieces), pieces[0].shape[1]
    return pl.pallas_call(
        stack_kernel,
        grid=(columns // tile,),
        in_specs=[pl.BlockSpec((piece.shape[0], tile), lambda j: (0, j)) for piece in pieces],
        out_specs=pl.BlockSpec((rows, tile), lambda j: (0, j)),
        out_shape=jax.ShapeDtypeStruct((rows, columns), pieces[0].dtype),
        compiler_params=VMEM,
        name="stack_rows",
    )(*pieces)


UNIT_TILE = 256
GELU_IN = math.sqrt(2.0 / math.pi)
GELU_CUBE = 0.044715


def joined_rows(refs):
    return jnp.concatenate([ref[...] for ref in refs], 0)


def ffn_kernel(source, *refs):
    count = (len(refs) - 4) // 3
    gate_w, up_w, down_w = (joined_rows(refs[i * count : (i + 1) * count]) for i in range(3))
    gate, up, hidden, total = refs[3 * count :]
    gate_pre = matmul(source[...], gate_w)
    up_pre = matmul(source[...], up_w)
    gate[...] = gate_pre
    up[...] = up_pre
    inner = GELU_IN * (gate_pre + GELU_CUBE * (gate_pre * gate_pre * gate_pre))
    low = (0.5 * gate_pre * (1.0 + jnp.tanh(inner)) * up_pre).astype(BF)
    hidden[...] = low

    @pl.when(pl.program_id(0) == 0)
    def _():
        total[...] = jnp.zeros_like(total)

    total[...] += inner_cols(low, down_w)


def ffn_back_kernel(grad, gate, up, *refs):
    count = (len(refs) - 3) // 3
    gate_w, up_w, down_w = (joined_rows(refs[i * count : (i + 1) * count]) for i in range(3))
    gate_grad, up_grad, total = refs[3 * count :]
    hidden_grad = matmul(grad[...], down_w)
    gate_pre = gate[...]
    square = gate_pre * gate_pre
    bend = jnp.tanh(GELU_IN * (gate_pre + GELU_CUBE * (square * gate_pre)))
    rise = 0.5 * (1.0 + bend)
    slope = rise + 0.5 * gate_pre * (1.0 - bend * bend) * (GELU_IN * (1.0 + 3.0 * GELU_CUBE * square))
    gate_low = (hidden_grad * up[...] * slope).astype(BF)
    up_low = (hidden_grad * (gate_pre * rise)).astype(BF)
    gate_grad[...] = gate_low
    up_grad[...] = up_low

    @pl.when(pl.program_id(0) == 0)
    def _():
        total[...] = jnp.zeros_like(total)

    total[...] += inner_cols(gate_low, gate_w) + inner_cols(up_low, up_w)


def unit_specs(rows, pieces, tiles):
    own = pl.BlockSpec((rows, UNIT_TILE), lambda j: (0, j))
    weights = [
        pl.BlockSpec((piece.shape[0], UNIT_TILE), lambda j, i=i: (0, j + i * tiles))
        for i in range(3)
        for piece in pieces
    ]
    return own, weights


def ffn_forward(source, pieces):
    rows, width = source.shape
    units = pieces[0].shape[1] // 3
    tiles = units // UNIT_TILE
    own, weights = unit_specs(rows, pieces, tiles)
    whole = pl.BlockSpec((rows, width), lambda j: (0, 0))
    return pl.pallas_call(
        ffn_kernel,
        grid=(tiles,),
        in_specs=[whole] + weights,
        out_specs=[own, own, own, whole],
        out_shape=[
            jax.ShapeDtypeStruct((rows, units), F32),
            jax.ShapeDtypeStruct((rows, units), F32),
            jax.ShapeDtypeStruct((rows, units), BF),
            jax.ShapeDtypeStruct((rows, width), F32),
        ],
        compiler_params=VMEM,
        name="ffn_forward",
    )(source, *pieces, *pieces, *pieces)


def ffn_backward(grad, gate, up, pieces):
    rows, width = grad.shape
    units = pieces[0].shape[1] // 3
    tiles = units // UNIT_TILE
    own, weights = unit_specs(rows, pieces, tiles)
    whole = pl.BlockSpec((rows, width), lambda j: (0, 0))
    return pl.pallas_call(
        ffn_back_kernel,
        grid=(tiles,),
        in_specs=[whole, own, own] + weights,
        out_specs=[own, own, whole],
        out_shape=[
            jax.ShapeDtypeStruct((rows, units), BF),
            jax.ShapeDtypeStruct((rows, units), BF),
            jax.ShapeDtypeStruct((rows, width), F32),
        ],
        compiler_params=VMEM,
        name="ffn_backward",
    )(grad, gate, up, *pieces, *pieces, *pieces)


def ffn_wgrad_kernel(steps, count, left, *refs):
    for i, right in enumerate(refs[:count]):

        @pl.when(pl.program_id(0) // steps == i)
        def _(right=right):
            start = 0
            for out in refs[count:]:
                size = out.shape[0]
                out[...] = matmul(left[start : start + size, :], right[...]).astype(BF)
                start += size


def ffn_wgrad(left, *rights):
    width, (rows, units), count = left.shape[0], rights[0].shape, len(rights)
    steps = 2
    tile = units // steps
    sizes = [width // 4, width // 4, width // 8, width // 8, width // 4]

    def spec(i):
        return pl.BlockSpec((rows, tile), lambda j: (0, jnp.clip(j - i * steps, 0, steps - 1)))

    return pl.pallas_call(
        lambda *refs: ffn_wgrad_kernel(steps, count, *refs),
        grid=(count * steps,),
        in_specs=[pl.BlockSpec(left.shape, lambda j: (0, 0))] + [spec(i) for i in range(count)],
        out_specs=[pl.BlockSpec((size, tile), lambda j: (0, j)) for size in sizes],
        out_shape=[jax.ShapeDtypeStruct((size, count * units), BF) for size in sizes],
        compiler_params=VMEM,
        name="ffn_wgrad",
    )(left, *rights)


def split_rows(values, parts):
    size = values.shape[0] // parts
    return [values[i * size : (i + 1) * size] for i in range(parts)]


def pick(core, first, second):
    return jnp.where(core == 0, first, second)


def shards(
    hidden_in,
    out_grad,
    block_order,
    norm_gains,
    head_gains,
    w_query,
    w_key,
    w_value,
    w_out,
    w_gate,
    w_up,
    w_down,
):
    tokens, width = hidden_in.shape
    y, z, x, core = (lax.axis_index(name) for name in CTX)
    other = 1 - core
    piece = width // 64
    units = w_gate.shape[1] // 2
    padded = (units + 127) // 128 * 128
    quarter = width // 4

    out_t, down_t = w_out.T, w_down.T

    def units_of(which):
        cut = [
            jnp.pad(lax.dynamic_slice_in_dim(w, which * units, units, 1), ((0, 0), (0, padded - units)))
            for w in (w_gate, w_up, down_t)
        ]
        return jnp.concatenate(cut, 1)

    def heads_of(which):
        cut = [lax.dynamic_slice_in_dim(w, which * HD, HD, 1) for w in (w_query, out_t)]
        return jnp.concatenate(cut + [w_key, w_value], 1)

    def chip_rows(of):
        mine, theirs = of(core), of(other)
        from_y, from_core, from_both = exchange((mine, theirs, theirs), "c")
        return pick(
            core,
            jnp.concatenate([mine, from_core, from_y, from_both], 0),
            jnp.concatenate([from_core, mine, from_both, from_y], 0),
        )

    head_rows = chip_rows(heads_of)
    ffn_rows = chip_rows(units_of)
    head_minor = after(gather_direct(head_rows, False), ffn_rows)
    head_pieces = gather_ring(head_minor, True)
    head_w = stack_rows(head_pieces)
    hidden_in = after(hidden_in, head_rows)
    query_w, out_w = head_w[:, :HD], head_w[:, HD : 2 * HD]
    key_w, value_w, pair_w = head_w[:, 2 * HD : 3 * HD], head_w[:, 3 * HD :], head_w[:, 2 * HD :]

    place = jnp.arange(width, dtype=jnp.int32)
    first, second = place // quarter, place // (quarter // 4) % 4
    z_at, x_at = (z + pick(core, second, first)) % 4, (x + pick(core, first, second)) % 4
    y_at = (y + place // (2 * piece)) % 2
    by_ring = y_at * (width // 2) + z_at * (8 * piece) + x_at * (2 * piece) + place % (2 * piece)
    to_ring = (place[:, None] == by_ring[None, :]).astype(BF)
    from_ring = (by_ring[:, None] == place[None, :]).astype(BF)

    def reorder(values, moves):
        return matmul(values, moves).astype(BF)

    def both_cores(values):
        return jnp.concatenate([values, shift(values, "c")], 0)

    def sum_parts(partial):
        low = reorder(partial.astype(BF), from_ring)
        chip = (low[:tokens].astype(F32) + shift(low[tokens:], "c").astype(F32)).astype(BF)
        return chip.astype(F32) + shift(chip, "s").astype(F32)

    offsets = jnp.arange(tokens, dtype=jnp.int32)

    def positions_of(places):
        return (block_order[places.reshape(-1)][:, None] * tokens + offsets[None, :]).reshape(-1)

    def device_of(y_at, z_at, x_at, core_at):
        return y_at * 32 + z_at * 8 + x_at * 2 + core_at

    steps = jnp.arange(4, dtype=jnp.int32)
    outer, inner = steps[:, None, None], steps[None, :, None]

    def keys_of(which):
        z_at, x_at = (z + pick(which, inner, outer)) % 4, (x + pick(which, outer, inner)) % 4
        return positions_of(device_of((y + steps[None, None, :2]) % 2, z_at, x_at, which))

    key_pos = [keys_of(core), keys_of(other)]
    own_pos = positions_of(device_of(y, z, x, core))
    chip_pos = jnp.concatenate([own_pos, positions_of(device_of(y, z, x, other))])
    cosine_table, sine_table = tables(chip_pos, HD)

    attn_val, pre_attn_back = jax.vjp(rms_scale, hidden_in, norm_gains[0])
    attn_chip = reorder(both_cores(attn_val.astype(BF)), to_ring)
    attn_ring = attn_chip[:tokens]
    key_pre = matmul(attn_ring, key_w)
    value_low = matmul(attn_ring, value_w).astype(BF)
    key_val, key_back = jax.vjp(
        lambda values, gain: rotate(rms_scale(values, gain), cosine_table[:tokens], sine_table[:tokens]),
        key_pre,
        head_gains[1],
    )
    key_low = key_val.astype(BF)
    ffn_rows = after(ffn_rows, head_pieces[1], head_pieces[4])
    ffn_first = gather_first(ffn_rows, False)
    pair_low = after(jnp.concatenate([key_low, value_low], 1), *ffn_first)
    ffn_minor = jnp.concatenate(gather_ring(ffn_rows, False, first=ffn_first), 0)
    pair_pieces = gather_ring(gather_minor_y(pair_low), True, ffn_minor)
    ffn_w = gather_ring(after(ffn_minor, pair_pieces[1], pair_pieces[4]), True)
    own_pairs = jnp.concatenate(pair_pieces, 0)
    pairs = [own_pairs, after(shift(own_pairs, "c"), ffn_w[1], ffn_w[4])]

    query_pre = matmul(attn_chip, query_w)
    query_val, query_back = jax.vjp(
        lambda values, gain: rotate(rms_scale(values, gain), cosine_table, sine_table),
        query_pre,
        head_gains[0],
    )
    score_scale = HD ** (-0.5)
    queries = (query_val.astype(BF).astype(F32) * score_scale).astype(BF)
    parts = [attend(queries, pairs[part], key_pos[part], chip_pos) for part in range(2)]
    weights = [part[0] for part in parts]
    inverse_total = 1.0 / (parts[0][1] + parts[1][1])
    accum = parts[0][2] + parts[1][2]
    attn_rows = accum * inverse_total
    mixed_low = attn_rows.astype(BF)
    attn_out = sum_parts(inner_cols(mixed_low, out_w))
    post_attn, post_attn_back = jax.vjp(rms_scale, attn_out, norm_gains[1])
    mid_state = hidden_in + post_attn

    ffn_val, ffn_norm_back = jax.vjp(rms_scale, mid_state, norm_gains[2])
    ffn_chip = both_cores(ffn_val.astype(BF))
    gate_pre, up_pre, hidden_low, ffn_part = ffn_forward(reorder(ffn_chip, to_ring), ffn_w)
    ffn_out = sum_parts(ffn_part)
    post_ffn, post_ffn_back = jax.vjp(rms_scale, ffn_out, norm_gains[3])
    block_out = mid_state + post_ffn

    ffn_grad, gain_four = post_ffn_back(out_grad)
    ffn_grad_chip = both_cores(ffn_grad.astype(BF))
    down_chunks = ffn_wgrad(inner_cols(from_ring, ffn_grad_chip).astype(BF), hidden_low)
    ffn_grad_ring = after(reorder(ffn_grad_chip, to_ring), *down_chunks)
    gate_low, up_low, ffn_norm_part = ffn_backward(ffn_grad_ring, gate_pre, up_pre, ffn_w)
    down_first = reduce_first(*down_chunks[2:4], True)
    ffn_norm_grad = sum_parts(after(ffn_norm_part, *down_first))
    down_major = reduce_second(*down_chunks[:2], down_chunks[4], *down_first, True).astype(BF)
    gate_up_chunks = ffn_wgrad(inner_cols(from_ring, ffn_chip).astype(BF), gate_low, up_low)
    mid_from, gain_three = ffn_norm_back(after(ffn_norm_grad, *gate_up_chunks))
    mid_grad = out_grad + mid_from

    def last_stage(values):
        parts = split_rows(values.astype(BF), 4)
        kept = [pick(core, parts[i], parts[i + 1]) for i in (0, 2)]
        sent = [pick(core, parts[i + 1], parts[i]) for i in (0, 2)]
        from_y, from_core, from_both = exchange((kept[1], sent[0], sent[1]), "c")
        return wide_sum(kept[0], from_y), wide_sum(from_core, from_both)

    attn_grad, gain_two = post_attn_back(mid_grad)
    attn_grad_chip = reorder(both_cores(attn_grad.astype(BF)), to_ring)
    rows_grad = after(matmul(attn_grad_chip, out_w).astype(BF), down_major)
    rows_wide = rows_grad.astype(F32)
    row_dot = jnp.sum(rows_wide * attn_rows, axis=1)[:, None]
    rows_scaled = (rows_wide * inverse_total).astype(BF)
    pair_far, query_far = attend_back(
        queries, pairs[1], weights[1], rows_grad, rows_scaled, row_dot, inverse_total
    )
    pair_near, query_near = attend_back(
        queries, pairs[0], weights[0], rows_grad, rows_scaled, row_dot, inverse_total
    )
    gate_up_first = reduce_first(*gate_up_chunks[2:4], True)
    query_grad = after(query_far + query_near, *gate_up_first)
    query_pre_grad, query_gain = query_back(query_grad * score_scale)
    query_gain = query_gain + shift(query_gain, "s")
    query_pre_low = query_pre_grad.astype(BF)
    early_grads = jnp.concatenate(
        [inner_rows(attn_chip, query_pre_low), inner_rows(attn_grad_chip, mixed_low)], 1
    ).astype(BF)
    pair_got = shift(pair_far, "c")
    chunks = [
        jnp.concatenate([wide_sum(near, got).astype(BF), early], 0)
        for near, got, early in zip(*(split_rows(part, 4) for part in (pair_near, pair_got, early_grads)))
    ]
    major_sum = reduce_chunks(*chunks, True).astype(BF)
    pair_chunks = split_rows(major_sum[: 8 * tokens], 4)
    early_chunks = split_rows(major_sum[8 * tokens :], 4)
    minor_sum = reduce_direct(
        [jnp.concatenate([pair, early], 0) for pair, early in zip(pair_chunks, early_chunks)], False
    )
    pair_own, pair_far_y = split_rows(minor_sum[: 2 * tokens].astype(BF), 2)
    from_y, from_shard, from_both = exchange((pair_far_y, pair_own, pair_far_y), "s")
    pair_grad = wide_sum(pair_own, from_y) + wide_sum(from_shard, from_both)
    attn_norm_sum = sum_parts(inner_cols(query_pre_low, query_w))
    key_pre_grad, key_gain = key_back(pair_grad[:, :HD])
    key_pre_low = key_pre_grad.astype(BF)
    value_grad_low = pair_grad[:, HD:].astype(BF)
    pair_part = inner_cols(jnp.concatenate([key_pre_low, value_grad_low], 1), pair_w).astype(BF)
    attn_norm_grad = attn_norm_sum + reorder(pair_part, from_ring).astype(F32)
    input_from, gain_one = pre_attn_back(attn_norm_grad)
    input_grad = mid_grad + input_from

    kept, sent = pick(core, key_pre_low, value_grad_low), pick(core, value_grad_low, key_pre_low)
    pair_chip = jnp.concatenate([kept, shift(sent, "c")], 0)
    heads = [
        jnp.pad(gain.reshape(64, HD // 64), ((0, 0), (0, piece - HD // 64))).reshape(width)
        for gain in (query_gain, key_gain)
    ]
    gains = jnp.stack([gain_one, gain_two, gain_three, gain_four] + heads, 1)
    gains = jnp.pad(gains, ((0, 0), (0, 128 - gains.shape[1]))).astype(BF)
    late_grads = jnp.concatenate([inner_rows(attn_chip, pair_chip), inner_rows(to_ring, gains)], 1).astype(BF)
    gate_up_major = reduce_second(
        *gate_up_chunks[:2], gate_up_chunks[4], *gate_up_first, True, major_sum
    ).astype(BF)
    late_major = after(reduce_direct(split_rows(late_grads, 4), True).astype(BF), gate_up_major)
    late_sum = reduce_direct(split_rows(late_major, 4), False)
    ffn_sum = reduce_chunks(*split_rows(jnp.concatenate([gate_up_major, down_major], 1), 4), False)
    all_mine, all_got = last_stage(jnp.concatenate([ffn_sum, minor_sum[2 * tokens :], late_sum], 1))
    ffn_mine, ffn_got = all_mine[:, : 3 * padded], all_got[:, : 3 * padded]
    head_mine, head_got = all_mine[:, 3 * padded :], all_got[:, 3 * padded :]

    def joined(start, size, mine, got):
        left, right = mine[:, start : start + size], got[:, start : start + size]
        return pick(core, jnp.concatenate([left, right], 1), jnp.concatenate([right, left], 1))

    gate_wgrad = joined(0, units, ffn_mine, ffn_got)
    up_wgrad = joined(padded, units, ffn_mine, ffn_got)
    down_wgrad = joined(2 * padded, units, ffn_mine, ffn_got).T

    query_wgrad = joined(0, HD, head_mine, head_got)
    out_wgrad = joined(HD, HD, head_mine, head_got).T
    pair_wgrad = joined(2 * HD, HD, head_mine, head_got)
    gain_sums = head_mine[:, 3 * HD :] + head_got[:, 3 * HD :]
    return (
        block_out,
        input_grad,
        query_wgrad,
        pair_wgrad[:, :HD],
        pair_wgrad[:, HD:],
        out_wgrad,
        gate_wgrad,
        up_wgrad,
        down_wgrad,
        gain_sums[:, :4].T,
        gain_sums[: HD // 64, 4:6].T,
    )


def solution(mesh):
    fine = Mesh(mesh.devices.reshape(2, 4, 4, 2, 2), ("y", "z", "x", "c", "s"))
    placed = (
        P(CTX, None),
        P(CTX, None),
        P(),
        P(),
        P(),
        P(CTX, "s"),
        P(CTX, None),
        P(CTX, None),
        P("s", CTX),
        P(CTX, "s"),
        P(CTX, "s"),
        P("s", CTX),
    )
    return jax.shard_map(
        shards,
        mesh=fine,
        in_specs=placed,
        out_specs=(
            P(CTX, None),
            P(CTX, None),
            P(CTX, "s"),
            P(CTX, None),
            P(CTX, None),
            P("s", CTX),
            P(CTX, "s"),
            P(CTX, "s"),
            P("s", CTX),
            P(None, CTX),
            P(None, CTX),
        ),
        check_vma=False,
    )
```

```python
import math

import jax
import jax.numpy as jnp
from jax import lax
from jax.experimental import pallas as pl
from jax.experimental.pallas import tpu as pltpu
from jax.sharding import Mesh, PartitionSpec as P

HD = 256
EPS = 1e-06
THETA = 1000000.0
BF = jnp.bfloat16
F32 = jnp.float32
CTX = ("y", "z", "x", "c")


def matmul(left, right):
    return jnp.dot(left, right, preferred_element_type=F32)


def inner_rows(left, right):
    return lax.dot_general(left, right, (((0,), (0,)), ((), ())), preferred_element_type=F32)


def inner_cols(left, right):
    return lax.dot_general(left, right, (((1,), (1,)), ((), ())), preferred_element_type=F32)


def rms_scale(values, gain):
    return values * lax.rsqrt(jnp.mean(values * values, axis=-1, keepdims=True) + EPS) * gain


def rotate(values, cosine_table, sine_table):
    half_width = values.shape[-1] // 2
    first = values[..., :half_width]
    second = values[..., half_width:]
    return jnp.concatenate(
        [first * cosine_table - second * sine_table, second * cosine_table + first * sine_table],
        axis=-1,
    )


def tables(positions, head_width):
    frequency = jnp.arange(head_width // 2, dtype=F32)
    inverse = jnp.exp(frequency * (-2.0 * math.log(THETA) / head_width))
    angles = positions.astype(F32)[:, None] * inverse[None, :]
    return (jnp.cos(angles), jnp.sin(angles))


def shift(values, axis, step=1):
    size = lax.axis_size(axis)
    return lax.ppermute(values, axis, [(i, (i + step) % size) for i in range(size)])


def ring(values, major, step, cross_y=False):
    moves = []
    for y in range(2):
        for z in range(4):
            for x in range(4):
                for core in range(2):
                    along_x = major == (core == 0)
                    to_z, to_x = (z, (x + step) % 4) if along_x else ((z + step) % 4, x)
                    to_y = 1 - y if cross_y else y
                    moves.append((y * 32 + z * 8 + x * 2 + core, to_y * 32 + to_z * 8 + to_x * 2 + core))
    return lax.ppermute(values, CTX, moves)


def gather_direct(block, major):
    return jnp.concatenate([block] + [ring(block, major, -k) for k in (1, 2, 3)], 0)


def gather_minor_y(block):
    blocks = [block if k == 0 else ring(block, False, -k) for k in range(4)]
    others = [ring(block, False, -k, True) for k in range(4)]
    return jnp.concatenate([part for pair in zip(blocks, others) for part in pair], 0)


def exchange(values, axis):
    both = [(i, 3 - i) for i in range(4)]
    return shift(values[0], "y"), shift(values[1], axis), lax.ppermute(values[2], ("y", axis), both)


def after(value, *others):
    return lax.optimization_barrier((value, *others))[0]


def gather_ring(block, major):
    half = (block.shape[0] // 2 + 7) // 8 * 8
    previous, following = ring(block, major, 1), ring(block, major, -1)
    far_low = ring(previous[:half], major, 1)
    far_high = ring(following[half:], major, -1)
    return [block, following, far_low, far_high, previous]


def wide_sum(*parts):
    return sum(part.astype(F32) for part in parts)


def reduce_direct(chunks, major):
    return wide_sum(chunks[0], *[ring(chunks[k], major, k) for k in (1, 2, 3)])


def reduce_first(far_low, far_high, major):
    return ring(far_low, major, 1), ring(far_high, major, -1)


def reduce_second(own, following, previous, from_previous, from_next, major):
    half = from_previous.shape[0]
    forward = jnp.concatenate(
        [wide_sum(following[:half], from_previous).astype(BF), following[half:]], 0
    )
    backward = jnp.concatenate(
        [previous[:half], wide_sum(previous[half:], from_next).astype(BF)], 0
    )
    return wide_sum(own, ring(forward, major, 1), ring(backward, major, -1))


def reduce_chunks(own, following, far, previous, major):
    half = (far.shape[0] // 2 + 7) // 8 * 8
    return reduce_second(own, following, previous, *reduce_first(far[:half], far[half:], major), major)


ATTN_BLOCK = 1024
VMEM = pltpu.CompilerParams(vmem_limit_bytes=48 * 1024 * 1024)


def attend_kernel(query, pair, key_pos, query_pos, weight, total, accum):
    scores = inner_cols(query[...], pair[:, :HD])
    exps = jnp.where(query_pos[...] >= key_pos[...], jnp.exp(scores), 0.0)
    low = exps.astype(BF)
    weight[...] = low

    @pl.when(pl.program_id(0) == 0)
    def _():
        total[...] = jnp.zeros_like(total)
        accum[...] = jnp.zeros_like(accum)

    total[...] += jnp.sum(exps, axis=1, keepdims=True)
    accum[...] += matmul(low, pair[:, HD:])


def attend(queries, pairs, key_pos, query_pos):
    rows, keys = queries.shape[0], pairs.shape[0]
    whole = lambda i: (0, 0)
    return pl.pallas_call(
        attend_kernel,
        grid=(keys // ATTN_BLOCK,),
        in_specs=[
            pl.BlockSpec((rows, HD), whole),
            pl.BlockSpec((ATTN_BLOCK, 2 * HD), lambda i: (i, 0)),
            pl.BlockSpec((1, ATTN_BLOCK), lambda i: (0, i)),
            pl.BlockSpec((rows, 1), whole),
        ],
        out_specs=[
            pl.BlockSpec((rows, ATTN_BLOCK), lambda i: (0, i)),
            pl.BlockSpec((rows, 1), whole),
            pl.BlockSpec((rows, HD), whole),
        ],
        out_shape=[
            jax.ShapeDtypeStruct((rows, keys), BF),
            jax.ShapeDtypeStruct((rows, 1), F32),
            jax.ShapeDtypeStruct((rows, HD), F32),
        ],
        compiler_params=VMEM,
        name="attend",
    )(queries, pairs, key_pos[None, :], query_pos[:, None])


def attend_back_kernel(query, pair, weight, grad, scaled, dot, inverse, pair_grad, query_grad):
    weights = weight[...]
    prob_grad = inner_cols(grad[...], pair[:, HD:])
    score_grad = (weights.astype(F32) * ((prob_grad - dot[...]) * inverse[...])).astype(BF)
    pair_grad[:, :HD] = inner_rows(score_grad, query[...]).astype(BF)
    pair_grad[:, HD:] = inner_rows(weights, scaled[...]).astype(BF)

    @pl.when(pl.program_id(0) == 0)
    def _():
        query_grad[...] = jnp.zeros_like(query_grad)

    query_grad[...] += matmul(score_grad, pair[:, :HD])


def attend_back(queries, pairs, weights, grads, scaled, dot, inverse):
    rows, keys = queries.shape[0], pairs.shape[0]
    whole = lambda i: (0, 0)
    return pl.pallas_call(
        attend_back_kernel,
        grid=(keys // ATTN_BLOCK,),
        in_specs=[
            pl.BlockSpec((rows, HD), whole),
            pl.BlockSpec((ATTN_BLOCK, 2 * HD), lambda i: (i, 0)),
            pl.BlockSpec((rows, ATTN_BLOCK), lambda i: (0, i)),
            pl.BlockSpec((rows, HD), whole),
            pl.BlockSpec((rows, HD), whole),
            pl.BlockSpec((rows, 1), whole),
            pl.BlockSpec((rows, 1), whole),
        ],
        out_specs=[
            pl.BlockSpec((ATTN_BLOCK, 2 * HD), lambda i: (i, 0)),
            pl.BlockSpec((rows, HD), whole),
        ],
        out_shape=[
            jax.ShapeDtypeStruct((keys, 2 * HD), BF),
            jax.ShapeDtypeStruct((rows, HD), F32),
        ],
        compiler_params=VMEM,
        name="attend_back",
    )(queries, pairs, weights, grads, scaled, dot, inverse)


def stack_kernel(*refs):
    start = 0
    for piece in refs[:-1]:
        refs[-1][start : start + piece.shape[0], :] = piece[...]
        start += piece.shape[0]


def stack_rows(pieces, tile=256):
    rows, columns = sum(piece.shape[0] for piece in pieces), pieces[0].shape[1]
    return pl.pallas_call(
        stack_kernel,
        grid=(columns // tile,),
        in_specs=[pl.BlockSpec((piece.shape[0], tile), lambda j: (0, j)) for piece in pieces],
        out_specs=pl.BlockSpec((rows, tile), lambda j: (0, j)),
        out_shape=jax.ShapeDtypeStruct((rows, columns), pieces[0].dtype),
        compiler_params=VMEM,
        name="stack_rows",
    )(*pieces)


UNIT_TILE = 256
GELU_IN = math.sqrt(2.0 / math.pi)
GELU_CUBE = 0.044715


def joined_rows(refs):
    return jnp.concatenate([ref[...] for ref in refs], 0)


def ffn_kernel(source, *refs):
    count = (len(refs) - 4) // 3
    gate_w, up_w, down_w = (joined_rows(refs[i * count : (i + 1) * count]) for i in range(3))
    gate, up, hidden, total = refs[3 * count :]
    gate_pre = matmul(source[...], gate_w)
    up_pre = matmul(source[...], up_w)
    gate[...] = gate_pre
    up[...] = up_pre
    inner = GELU_IN * (gate_pre + GELU_CUBE * (gate_pre * gate_pre * gate_pre))
    low = (0.5 * gate_pre * (1.0 + jnp.tanh(inner)) * up_pre).astype(BF)
    hidden[...] = low

    @pl.when(pl.program_id(0) == 0)
    def _():
        total[...] = jnp.zeros_like(total)

    total[...] += inner_cols(low, down_w)


def ffn_back_kernel(grad, gate, up, *refs):
    count = (len(refs) - 3) // 3
    gate_w, up_w, down_w = (joined_rows(refs[i * count : (i + 1) * count]) for i in range(3))
    gate_grad, up_grad, total = refs[3 * count :]
    hidden_grad = matmul(grad[...], down_w)
    gate_pre = gate[...]
    square = gate_pre * gate_pre
    bend = jnp.tanh(GELU_IN * (gate_pre + GELU_CUBE * (square * gate_pre)))
    rise = 0.5 * (1.0 + bend)
    slope = rise + 0.5 * gate_pre * (1.0 - bend * bend) * (GELU_IN * (1.0 + 3.0 * GELU_CUBE * square))
    gate_low = (hidden_grad * up[...] * slope).astype(BF)
    up_low = (hidden_grad * (gate_pre * rise)).astype(BF)
    gate_grad[...] = gate_low
    up_grad[...] = up_low

    @pl.when(pl.program_id(0) == 0)
    def _():
        total[...] = jnp.zeros_like(total)

    total[...] += inner_cols(gate_low, gate_w) + inner_cols(up_low, up_w)


def unit_specs(rows, pieces, tiles):
    own = pl.BlockSpec((rows, UNIT_TILE), lambda j: (0, j))
    weights = [
        pl.BlockSpec((piece.shape[0], UNIT_TILE), lambda j, i=i: (0, j + i * tiles))
        for i in range(3)
        for piece in pieces
    ]
    return own, weights


def ffn_forward(source, pieces):
    rows, width = source.shape
    units = pieces[0].shape[1] // 3
    tiles = units // UNIT_TILE
    own, weights = unit_specs(rows, pieces, tiles)
    whole = pl.BlockSpec((rows, width), lambda j: (0, 0))
    return pl.pallas_call(
        ffn_kernel,
        grid=(tiles,),
        in_specs=[whole] + weights,
        out_specs=[own, own, own, whole],
        out_shape=[
            jax.ShapeDtypeStruct((rows, units), F32),
            jax.ShapeDtypeStruct((rows, units), F32),
            jax.ShapeDtypeStruct((rows, units), BF),
            jax.ShapeDtypeStruct((rows, width), F32),
        ],
        compiler_params=VMEM,
        name="ffn_forward",
    )(source, *pieces, *pieces, *pieces)


def ffn_backward(grad, gate, up, pieces):
    rows, width = grad.shape
    units = pieces[0].shape[1] // 3
    tiles = units // UNIT_TILE
    own, weights = unit_specs(rows, pieces, tiles)
    whole = pl.BlockSpec((rows, width), lambda j: (0, 0))
    return pl.pallas_call(
        ffn_back_kernel,
        grid=(tiles,),
        in_specs=[whole, own, own] + weights,
        out_specs=[own, own, whole],
        out_shape=[
            jax.ShapeDtypeStruct((rows, units), BF),
            jax.ShapeDtypeStruct((rows, units), BF),
            jax.ShapeDtypeStruct((rows, width), F32),
        ],
        compiler_params=VMEM,
        name="ffn_backward",
    )(grad, gate, up, *pieces, *pieces, *pieces)


def ffn_wgrad_kernel(steps, left, gate, up, hidden, out):
    rows = gate.shape[0]
    for i, (first, right) in enumerate([(0, gate), (0, up), (rows, hidden)]):

        @pl.when(pl.program_id(0) // steps == i)
        def _(first=first, right=right):
            out[...] = matmul(left[:, first : first + rows], right[...]).astype(BF)


def ffn_wgrad(left, gate, up, hidden):
    width, (rows, units) = left.shape[0], gate.shape
    steps = 2
    tile = units // steps

    def spec(i):
        return pl.BlockSpec((rows, tile), lambda j: (0, jnp.clip(j - i * steps, 0, steps - 1)))

    return pl.pallas_call(
        lambda *refs: ffn_wgrad_kernel(steps, *refs),
        grid=(3 * steps,),
        in_specs=[pl.BlockSpec(left.shape, lambda j: (0, 0)), spec(0), spec(1), spec(2)],
        out_specs=pl.BlockSpec((width, tile), lambda j: (0, j)),
        out_shape=jax.ShapeDtypeStruct((width, 3 * units), BF),
        compiler_params=VMEM,
        name="ffn_wgrad",
    )(left, gate, up, hidden)


def split_rows(values, parts):
    size = values.shape[0] // parts
    return [values[i * size : (i + 1) * size] for i in range(parts)]


def pick(core, first, second):
    return jnp.where(core == 0, first, second)


def shards(
    hidden_in,
    out_grad,
    block_order,
    norm_gains,
    head_gains,
    w_query,
    w_key,
    w_value,
    w_out,
    w_gate,
    w_up,
    w_down,
):
    tokens, width = hidden_in.shape
    y, z, x, core = (lax.axis_index(name) for name in CTX)
    other = 1 - core
    piece = width // 64
    units = w_gate.shape[1] // 2
    padded = (units + 127) // 128 * 128
    quarter = width // 4

    out_t, down_t = w_out.T, w_down.T

    def units_of(which):
        cut = [
            jnp.pad(lax.dynamic_slice_in_dim(w, which * units, units, 1), ((0, 0), (0, padded - units)))
            for w in (w_gate, w_up, down_t)
        ]
        return jnp.concatenate(cut, 1)

    def heads_of(which):
        cut = [lax.dynamic_slice_in_dim(w, which * HD, HD, 1) for w in (w_query, out_t)]
        return jnp.concatenate(cut + [w_key, w_value], 1)

    def chip_rows(of):
        mine, theirs = of(core), of(other)
        from_y, from_core, from_both = exchange((mine, theirs, theirs), "c")
        return pick(
            core,
            jnp.concatenate([mine, from_core, from_y, from_both], 0),
            jnp.concatenate([from_core, mine, from_both, from_y], 0),
        )

    ffn_rows = chip_rows(units_of)
    ffn_w = [lax.all_gather(ffn_rows, ("z", "x"), axis=0, tiled=True)]
    head_rows = after(chip_rows(heads_of), ffn_rows)
    head_w = stack_rows(gather_ring(gather_direct(head_rows, False), True))
    hidden_in = after(hidden_in, head_rows)
    query_w, out_w = head_w[:, :HD], head_w[:, HD : 2 * HD]
    key_w, value_w, pair_w = head_w[:, 2 * HD : 3 * HD], head_w[:, 3 * HD :], head_w[:, 2 * HD :]

    place = jnp.arange(width, dtype=jnp.int32)
    first, second = place // quarter, place // (quarter // 4) % 4

    def natural(z_at, x_at):
        y_at = (y + place // (2 * piece)) % 2
        return y_at * (width // 2) + z_at * (8 * piece) + x_at * (2 * piece) + place % (2 * piece)

    by_gather = natural(first, second)
    by_ring = natural((z + pick(core, second, first)) % 4, (x + pick(core, first, second)) % 4)
    to_gather, to_ring = ((place[:, None] == by[None, :]).astype(BF) for by in (by_gather, by_ring))
    from_gather, from_ring = ((by[:, None] == place[None, :]).astype(BF) for by in (by_gather, by_ring))

    def reorder(values, moves):
        return matmul(values, moves).astype(BF)

    def both_cores(values):
        return jnp.concatenate([values, shift(values, "c")], 0)

    def sum_parts(partial, moves):
        low = reorder(partial.astype(BF), moves)
        chip = (low[:tokens].astype(F32) + shift(low[tokens:], "c").astype(F32)).astype(BF)
        return chip.astype(F32) + shift(chip, "s").astype(F32)

    offsets = jnp.arange(tokens, dtype=jnp.int32)

    def positions_of(places):
        return (block_order[places.reshape(-1)][:, None] * tokens + offsets[None, :]).reshape(-1)

    def device_of(y_at, z_at, x_at, core_at):
        return y_at * 32 + z_at * 8 + x_at * 2 + core_at

    steps = jnp.arange(4, dtype=jnp.int32)
    outer, inner = steps[:, None, None], steps[None, :, None]

    def keys_of(which):
        z_at, x_at = (z + pick(which, inner, outer)) % 4, (x + pick(which, outer, inner)) % 4
        return positions_of(device_of((y + steps[None, None, :2]) % 2, z_at, x_at, which))

    key_pos = [keys_of(core), keys_of(other)]
    own_pos = positions_of(device_of(y, z, x, core))
    chip_pos = jnp.concatenate([own_pos, positions_of(device_of(y, z, x, other))])
    cosine_table, sine_table = tables(chip_pos, HD)

    attn_val, pre_attn_back = jax.vjp(rms_scale, hidden_in, norm_gains[0])
    attn_chip = reorder(both_cores(attn_val.astype(BF)), to_ring)
    attn_ring = attn_chip[:tokens]
    key_pre = matmul(attn_ring, key_w)
    value_low = matmul(attn_ring, value_w).astype(BF)
    key_val, key_back = jax.vjp(
        lambda values, gain: rotate(rms_scale(values, gain), cosine_table[:tokens], sine_table[:tokens]),
        key_pre,
        head_gains[1],
    )
    key_low = key_val.astype(BF)
    pair_low = jnp.concatenate([key_low, value_low], 1)
    own_pairs = jnp.concatenate(gather_ring(gather_minor_y(pair_low), True), 0)
    pairs = [own_pairs, shift(own_pairs, "c")]

    query_pre = matmul(attn_chip, query_w)
    query_val, query_back = jax.vjp(
        lambda values, gain: rotate(rms_scale(values, gain), cosine_table, sine_table),
        query_pre,
        head_gains[0],
    )
    score_scale = HD ** (-0.5)
    queries = (query_val.astype(BF).astype(F32) * score_scale).astype(BF)
    parts = [attend(queries, pairs[part], key_pos[part], chip_pos) for part in range(2)]
    weights = [part[0] for part in parts]
    inverse_total = 1.0 / (parts[0][1] + parts[1][1])
    accum = parts[0][2] + parts[1][2]
    attn_rows = accum * inverse_total
    mixed_low = attn_rows.astype(BF)
    attn_out = sum_parts(inner_cols(mixed_low, out_w), from_ring)
    post_attn, post_attn_back = jax.vjp(rms_scale, attn_out, norm_gains[1])
    mid_state = hidden_in + post_attn

    ffn_val, ffn_norm_back = jax.vjp(rms_scale, mid_state, norm_gains[2])
    ffn_chip = both_cores(ffn_val.astype(BF))
    gate_pre, up_pre, hidden_low, ffn_part = ffn_forward(reorder(ffn_chip, to_gather), ffn_w)
    ffn_out = sum_parts(ffn_part, from_gather)
    post_ffn, post_ffn_back = jax.vjp(rms_scale, ffn_out, norm_gains[3])
    block_out = mid_state + post_ffn

    ffn_grad, gain_four = post_ffn_back(out_grad)
    ffn_grad_chip = both_cores(ffn_grad.astype(BF))
    gate_low, up_low, ffn_norm_part = ffn_backward(reorder(ffn_grad_chip, to_gather), gate_pre, up_pre, ffn_w)
    sources = jnp.concatenate([ffn_chip, ffn_grad_chip], 0)
    ffn_wgrads = ffn_wgrad(inner_cols(from_gather, sources).astype(BF), gate_low, up_low, hidden_low)
    ffn_sum = lax.psum_scatter(ffn_wgrads, ("z", "x"), scatter_dimension=0, tiled=True)
    ffn_norm_grad = after(sum_parts(ffn_norm_part, from_gather), ffn_wgrads)
    mid_from, gain_three = ffn_norm_back(ffn_norm_grad)
    mid_grad = out_grad + mid_from

    def last_stage(values):
        parts = split_rows(values.astype(BF), 4)
        kept = [pick(core, parts[i], parts[i + 1]) for i in (0, 2)]
        sent = [pick(core, parts[i + 1], parts[i]) for i in (0, 2)]
        from_y, from_core, from_both = exchange((kept[1], sent[0], sent[1]), "c")
        return wide_sum(kept[0], from_y), wide_sum(from_core, from_both)

    attn_grad, gain_two = post_attn_back(mid_grad)
    attn_grad_chip = reorder(both_cores(attn_grad.astype(BF)), to_ring)
    rows_grad = matmul(attn_grad_chip, out_w).astype(BF)
    rows_wide = rows_grad.astype(F32)
    row_dot = jnp.sum(rows_wide * attn_rows, axis=1)[:, None]
    rows_scaled = (rows_wide * inverse_total).astype(BF)
    pair_far, query_far = attend_back(
        queries, pairs[1], weights[1], rows_grad, rows_scaled, row_dot, inverse_total
    )
    pair_near, query_near = attend_back(
        queries, pairs[0], weights[0], rows_grad, rows_scaled, row_dot, inverse_total
    )
    query_grad = query_far + query_near
    query_pre_grad, query_gain = query_back(query_grad * score_scale)
    query_gain = query_gain + shift(query_gain, "s")
    query_pre_low = query_pre_grad.astype(BF)
    early_grads = jnp.concatenate(
        [inner_rows(attn_chip, query_pre_low), inner_rows(attn_grad_chip, mixed_low)], 1
    ).astype(BF)
    pair_got = shift(pair_far, "c")
    chunks = [
        jnp.concatenate([wide_sum(near, got).astype(BF), early], 0)
        for near, got, early in zip(*(split_rows(part, 4) for part in (pair_near, pair_got, early_grads)))
    ]
    major_sum = reduce_chunks(*chunks, True).astype(BF)
    pair_chunks = split_rows(major_sum[: 8 * tokens], 4)
    early_chunks = split_rows(major_sum[8 * tokens :], 4)
    minor_sum = reduce_direct(
        [jnp.concatenate([pair, early], 0) for pair, early in zip(pair_chunks, early_chunks)], False
    )
    pair_own, pair_far_y = split_rows(minor_sum[: 2 * tokens].astype(BF), 2)
    from_y, from_shard, from_both = exchange((pair_far_y, pair_own, pair_far_y), "s")
    pair_grad = wide_sum(pair_own, from_y) + wide_sum(from_shard, from_both)
    attn_norm_sum = sum_parts(inner_cols(query_pre_low, query_w), from_ring)
    key_pre_grad, key_gain = key_back(pair_grad[:, :HD])
    key_pre_low = key_pre_grad.astype(BF)
    value_grad_low = pair_grad[:, HD:].astype(BF)
    pair_part = inner_cols(jnp.concatenate([key_pre_low, value_grad_low], 1), pair_w).astype(BF)
    attn_norm_grad = attn_norm_sum + reorder(pair_part, from_ring).astype(F32)
    input_from, gain_one = pre_attn_back(attn_norm_grad)
    input_grad = mid_grad + input_from

    kept, sent = pick(core, key_pre_low, value_grad_low), pick(core, value_grad_low, key_pre_low)
    pair_chip = jnp.concatenate([kept, shift(sent, "c")], 0)
    heads = [
        jnp.pad(gain.reshape(64, HD // 64), ((0, 0), (0, piece - HD // 64))).reshape(width)
        for gain in (query_gain, key_gain)
    ]
    gains = jnp.stack([gain_one, gain_two, gain_three, gain_four] + heads, 1)
    gains = jnp.pad(gains, ((0, 0), (0, 128 - gains.shape[1]))).astype(BF)
    late_grads = jnp.concatenate([inner_rows(attn_chip, pair_chip), inner_rows(to_ring, gains)], 1).astype(BF)
    late_major = reduce_direct(split_rows(late_grads, 4), True).astype(BF)
    late_sum = reduce_direct(split_rows(late_major, 4), False)
    all_mine, all_got = last_stage(jnp.concatenate([ffn_sum.astype(F32), minor_sum[2 * tokens :], late_sum], 1))
    ffn_mine, ffn_got = all_mine[:, : 3 * padded], all_got[:, : 3 * padded]
    head_mine, head_got = all_mine[:, 3 * padded :], all_got[:, 3 * padded :]

    def joined(start, size, mine, got):
        left, right = mine[:, start : start + size], got[:, start : start + size]
        return pick(core, jnp.concatenate([left, right], 1), jnp.concatenate([right, left], 1))

    gate_wgrad = joined(0, units, ffn_mine, ffn_got)
    up_wgrad = joined(padded, units, ffn_mine, ffn_got)
    down_wgrad = joined(2 * padded, units, ffn_mine, ffn_got).T

    query_wgrad = joined(0, HD, head_mine, head_got)
    out_wgrad = joined(HD, HD, head_mine, head_got).T
    pair_wgrad = joined(2 * HD, HD, head_mine, head_got)
    gain_sums = head_mine[:, 3 * HD :] + head_got[:, 3 * HD :]
    return (
        block_out,
        input_grad,
        query_wgrad,
        pair_wgrad[:, :HD],
        pair_wgrad[:, HD:],
        out_wgrad,
        gate_wgrad,
        up_wgrad,
        down_wgrad,
        gain_sums[:, :4].T,
        gain_sums[: HD // 64, 4:6].T,
    )


def solution(mesh):
    fine = Mesh(mesh.devices.reshape(2, 4, 4, 2, 2), ("y", "z", "x", "c", "s"))
    placed = (
        P(CTX, None),
        P(CTX, None),
        P(),
        P(),
        P(),
        P(CTX, "s"),
        P(CTX, None),
        P(CTX, None),
        P("s", CTX),
        P(CTX, "s"),
        P(CTX, "s"),
        P("s", CTX),
    )
    return jax.shard_map(
        shards,
        mesh=fine,
        in_specs=placed,
        out_specs=(
            P(CTX, None),
            P(CTX, None),
            P(CTX, "s"),
            P(CTX, None),
            P(CTX, None),
            P("s", CTX),
            P(CTX, "s"),
            P(CTX, "s"),
            P("s", CTX),
            P(None, CTX),
            P(None, CTX),
        ),
        check_vma=False,
    )
```

```python
import math

import jax
import jax.numpy as jnp
from jax import lax
from jax.experimental import pallas as pl
from jax.experimental.pallas import tpu as pltpu
from jax.sharding import Mesh, PartitionSpec as P

HD = 256
EPS = 1e-06
THETA = 1000000.0
BF = jnp.bfloat16
F32 = jnp.float32
CTX = ("y", "z", "x", "c")


def matmul(left, right):
    return jnp.dot(left, right, preferred_element_type=F32)


def inner_rows(left, right):
    return lax.dot_general(left, right, (((0,), (0,)), ((), ())), preferred_element_type=F32)


def inner_cols(left, right):
    return lax.dot_general(left, right, (((1,), (1,)), ((), ())), preferred_element_type=F32)


def rms_scale(values, gain):
    return values * lax.rsqrt(jnp.mean(values * values, axis=-1, keepdims=True) + EPS) * gain


def rotate(values, cosine_table, sine_table):
    half_width = values.shape[-1] // 2
    first = values[..., :half_width]
    second = values[..., half_width:]
    return jnp.concatenate(
        [first * cosine_table - second * sine_table, second * cosine_table + first * sine_table],
        axis=-1,
    )


def tables(positions, head_width):
    frequency = jnp.arange(head_width // 2, dtype=F32)
    inverse = jnp.exp(frequency * (-2.0 * math.log(THETA) / head_width))
    angles = positions.astype(F32)[:, None] * inverse[None, :]
    return (jnp.cos(angles), jnp.sin(angles))


def shift(values, axis, step=1):
    size = lax.axis_size(axis)
    return lax.ppermute(values, axis, [(i, (i + step) % size) for i in range(size)])


def ring(values, major, step, cross_y=False):
    moves = []
    for y in range(2):
        for z in range(4):
            for x in range(4):
                for core in range(2):
                    along_x = major == (core == 0)
                    to_z, to_x = (z, (x + step) % 4) if along_x else ((z + step) % 4, x)
                    to_y = 1 - y if cross_y else y
                    moves.append((y * 32 + z * 8 + x * 2 + core, to_y * 32 + to_z * 8 + to_x * 2 + core))
    return lax.ppermute(values, CTX, moves)


def gather_direct(block, major):
    return jnp.concatenate([block] + [ring(block, major, -k) for k in (1, 2, 3)], 0)


def gather_minor_y(block):
    blocks = [block if k == 0 else ring(block, False, -k) for k in range(4)]
    others = [ring(block, False, -k, True) for k in range(4)]
    return jnp.concatenate([part for pair in zip(blocks, others) for part in pair], 0)


def exchange(values, axis):
    both = [(i, 3 - i) for i in range(4)]
    return shift(values[0], "y"), shift(values[1], axis), lax.ppermute(values[2], ("y", axis), both)


def after(value, *others):
    return lax.optimization_barrier((value, *others))[0]


def gather_ring(block, major):
    half = (block.shape[0] // 2 + 7) // 8 * 8
    previous, following = ring(block, major, 1), ring(block, major, -1)
    far_low = ring(previous[:half], major, 1)
    far_high = ring(following[half:], major, -1)
    return [block, following, far_low, far_high, previous]


def wide_sum(*parts):
    return sum(part.astype(F32) for part in parts)


def reduce_direct(chunks, major):
    return wide_sum(chunks[0], *[ring(chunks[k], major, k) for k in (1, 2, 3)])


def reduce_first(far_low, far_high, major):
    return ring(far_low, major, 1), ring(far_high, major, -1)


def reduce_second(own, following, previous, from_previous, from_next, major):
    half = from_previous.shape[0]
    forward = jnp.concatenate(
        [wide_sum(following[:half], from_previous).astype(BF), following[half:]], 0
    )
    backward = jnp.concatenate(
        [previous[:half], wide_sum(previous[half:], from_next).astype(BF)], 0
    )
    return wide_sum(own, ring(forward, major, 1), ring(backward, major, -1))


def reduce_chunks(own, following, far, previous, major):
    half = (far.shape[0] // 2 + 7) // 8 * 8
    return reduce_second(own, following, previous, *reduce_first(far[:half], far[half:], major), major)


ATTN_BLOCK = 1024
VMEM = pltpu.CompilerParams(vmem_limit_bytes=48 * 1024 * 1024)


def attend_kernel(query, pair, key_pos, query_pos, weight, total, accum):
    scores = inner_cols(query[...], pair[:, :HD])
    exps = jnp.where(query_pos[...] >= key_pos[...], jnp.exp(scores), 0.0)
    low = exps.astype(BF)
    weight[...] = low

    @pl.when(pl.program_id(0) == 0)
    def _():
        total[...] = jnp.zeros_like(total)
        accum[...] = jnp.zeros_like(accum)

    total[...] += jnp.sum(exps, axis=1, keepdims=True)
    accum[...] += matmul(low, pair[:, HD:])


def attend(queries, pairs, key_pos, query_pos):
    rows, keys = queries.shape[0], pairs.shape[0]
    whole = lambda i: (0, 0)
    return pl.pallas_call(
        attend_kernel,
        grid=(keys // ATTN_BLOCK,),
        in_specs=[
            pl.BlockSpec((rows, HD), whole),
            pl.BlockSpec((ATTN_BLOCK, 2 * HD), lambda i: (i, 0)),
            pl.BlockSpec((1, ATTN_BLOCK), lambda i: (0, i)),
            pl.BlockSpec((rows, 1), whole),
        ],
        out_specs=[
            pl.BlockSpec((rows, ATTN_BLOCK), lambda i: (0, i)),
            pl.BlockSpec((rows, 1), whole),
            pl.BlockSpec((rows, HD), whole),
        ],
        out_shape=[
            jax.ShapeDtypeStruct((rows, keys), BF),
            jax.ShapeDtypeStruct((rows, 1), F32),
            jax.ShapeDtypeStruct((rows, HD), F32),
        ],
        compiler_params=VMEM,
        name="attend",
    )(queries, pairs, key_pos[None, :], query_pos[:, None])


def attend_back_kernel(query, pair, weight, grad, scaled, dot, inverse, pair_grad, query_grad):
    weights = weight[...]
    prob_grad = inner_cols(grad[...], pair[:, HD:])
    score_grad = (weights.astype(F32) * ((prob_grad - dot[...]) * inverse[...])).astype(BF)
    pair_grad[:, :HD] = inner_rows(score_grad, query[...]).astype(BF)
    pair_grad[:, HD:] = inner_rows(weights, scaled[...]).astype(BF)

    @pl.when(pl.program_id(0) == 0)
    def _():
        query_grad[...] = jnp.zeros_like(query_grad)

    query_grad[...] += matmul(score_grad, pair[:, :HD])


def attend_back(queries, pairs, weights, grads, scaled, dot, inverse):
    rows, keys = queries.shape[0], pairs.shape[0]
    whole = lambda i: (0, 0)
    return pl.pallas_call(
        attend_back_kernel,
        grid=(keys // ATTN_BLOCK,),
        in_specs=[
            pl.BlockSpec((rows, HD), whole),
            pl.BlockSpec((ATTN_BLOCK, 2 * HD), lambda i: (i, 0)),
            pl.BlockSpec((rows, ATTN_BLOCK), lambda i: (0, i)),
            pl.BlockSpec((rows, HD), whole),
            pl.BlockSpec((rows, HD), whole),
            pl.BlockSpec((rows, 1), whole),
            pl.BlockSpec((rows, 1), whole),
        ],
        out_specs=[
            pl.BlockSpec((ATTN_BLOCK, 2 * HD), lambda i: (i, 0)),
            pl.BlockSpec((rows, HD), whole),
        ],
        out_shape=[
            jax.ShapeDtypeStruct((keys, 2 * HD), BF),
            jax.ShapeDtypeStruct((rows, HD), F32),
        ],
        compiler_params=VMEM,
        name="attend_back",
    )(queries, pairs, weights, grads, scaled, dot, inverse)


def stack_kernel(*refs):
    start = 0
    for piece in refs[:-1]:
        refs[-1][start : start + piece.shape[0], :] = piece[...]
        start += piece.shape[0]


def stack_rows(pieces, tile=256):
    rows, columns = sum(piece.shape[0] for piece in pieces), pieces[0].shape[1]
    return pl.pallas_call(
        stack_kernel,
        grid=(columns // tile,),
        in_specs=[pl.BlockSpec((piece.shape[0], tile), lambda j: (0, j)) for piece in pieces],
        out_specs=pl.BlockSpec((rows, tile), lambda j: (0, j)),
        out_shape=jax.ShapeDtypeStruct((rows, columns), pieces[0].dtype),
        compiler_params=VMEM,
        name="stack_rows",
    )(*pieces)


UNIT_TILE = 256
GELU_IN = math.sqrt(2.0 / math.pi)
GELU_CUBE = 0.044715


def joined_rows(refs):
    return jnp.concatenate([ref[...] for ref in refs], 0)


def ffn_kernel(source, *refs):
    count = (len(refs) - 4) // 3
    gate_w, up_w, down_w = (joined_rows(refs[i * count : (i + 1) * count]) for i in range(3))
    gate, up, hidden, total = refs[3 * count :]
    gate_pre = matmul(source[...], gate_w)
    up_pre = matmul(source[...], up_w)
    gate[...] = gate_pre
    up[...] = up_pre
    inner = GELU_IN * (gate_pre + GELU_CUBE * (gate_pre * gate_pre * gate_pre))
    low = (0.5 * gate_pre * (1.0 + jnp.tanh(inner)) * up_pre).astype(BF)
    hidden[...] = low

    @pl.when(pl.program_id(0) == 0)
    def _():
        total[...] = jnp.zeros_like(total)

    total[...] += inner_cols(low, down_w)


def ffn_back_kernel(grad, gate, up, *refs):
    count = (len(refs) - 3) // 3
    gate_w, up_w, down_w = (joined_rows(refs[i * count : (i + 1) * count]) for i in range(3))
    gate_grad, up_grad, total = refs[3 * count :]
    hidden_grad = matmul(grad[...], down_w)
    gate_pre = gate[...]
    square = gate_pre * gate_pre
    bend = jnp.tanh(GELU_IN * (gate_pre + GELU_CUBE * (square * gate_pre)))
    rise = 0.5 * (1.0 + bend)
    slope = rise + 0.5 * gate_pre * (1.0 - bend * bend) * (GELU_IN * (1.0 + 3.0 * GELU_CUBE * square))
    gate_low = (hidden_grad * up[...] * slope).astype(BF)
    up_low = (hidden_grad * (gate_pre * rise)).astype(BF)
    gate_grad[...] = gate_low
    up_grad[...] = up_low

    @pl.when(pl.program_id(0) == 0)
    def _():
        total[...] = jnp.zeros_like(total)

    total[...] += inner_cols(gate_low, gate_w) + inner_cols(up_low, up_w)


def unit_specs(rows, pieces, tiles):
    own = pl.BlockSpec((rows, UNIT_TILE), lambda j: (0, j))
    weights = [
        pl.BlockSpec((piece.shape[0], UNIT_TILE), lambda j, i=i: (0, j + i * tiles))
        for i in range(3)
        for piece in pieces
    ]
    return own, weights


def ffn_forward(source, pieces):
    rows, width = source.shape
    units = pieces[0].shape[1] // 3
    tiles = units // UNIT_TILE
    own, weights = unit_specs(rows, pieces, tiles)
    whole = pl.BlockSpec((rows, width), lambda j: (0, 0))
    return pl.pallas_call(
        ffn_kernel,
        grid=(tiles,),
        in_specs=[whole] + weights,
        out_specs=[own, own, own, whole],
        out_shape=[
            jax.ShapeDtypeStruct((rows, units), F32),
            jax.ShapeDtypeStruct((rows, units), F32),
            jax.ShapeDtypeStruct((rows, units), BF),
            jax.ShapeDtypeStruct((rows, width), F32),
        ],
        compiler_params=VMEM,
        name="ffn_forward",
    )(source, *pieces, *pieces, *pieces)


def ffn_backward(grad, gate, up, pieces):
    rows, width = grad.shape
    units = pieces[0].shape[1] // 3
    tiles = units // UNIT_TILE
    own, weights = unit_specs(rows, pieces, tiles)
    whole = pl.BlockSpec((rows, width), lambda j: (0, 0))
    return pl.pallas_call(
        ffn_back_kernel,
        grid=(tiles,),
        in_specs=[whole, own, own] + weights,
        out_specs=[own, own, whole],
        out_shape=[
            jax.ShapeDtypeStruct((rows, units), BF),
            jax.ShapeDtypeStruct((rows, units), BF),
            jax.ShapeDtypeStruct((rows, width), F32),
        ],
        compiler_params=VMEM,
        name="ffn_backward",
    )(grad, gate, up, *pieces, *pieces, *pieces)


def ffn_wgrad_kernel(steps, left, gate, up, hidden, out):
    rows = gate.shape[0]
    for i, (first, right) in enumerate([(0, gate), (0, up), (rows, hidden)]):

        @pl.when(pl.program_id(0) // steps == i)
        def _(first=first, right=right):
            out[...] = matmul(left[:, first : first + rows], right[...]).astype(BF)


def ffn_wgrad(left, gate, up, hidden):
    width, (rows, units) = left.shape[0], gate.shape
    steps = 2
    tile = units // steps

    def spec(i):
        return pl.BlockSpec((rows, tile), lambda j: (0, jnp.clip(j - i * steps, 0, steps - 1)))

    return pl.pallas_call(
        lambda *refs: ffn_wgrad_kernel(steps, *refs),
        grid=(3 * steps,),
        in_specs=[pl.BlockSpec(left.shape, lambda j: (0, 0)), spec(0), spec(1), spec(2)],
        out_specs=pl.BlockSpec((width, tile), lambda j: (0, j)),
        out_shape=jax.ShapeDtypeStruct((width, 3 * units), BF),
        compiler_params=VMEM,
        name="ffn_wgrad",
    )(left, gate, up, hidden)


def split_rows(values, parts):
    size = values.shape[0] // parts
    return [values[i * size : (i + 1) * size] for i in range(parts)]


def pick(core, first, second):
    return jnp.where(core == 0, first, second)


def shards(
    hidden_in,
    out_grad,
    block_order,
    norm_gains,
    head_gains,
    w_query,
    w_key,
    w_value,
    w_out,
    w_gate,
    w_up,
    w_down,
):
    tokens, width = hidden_in.shape
    y, z, x, core = (lax.axis_index(name) for name in CTX)
    other = 1 - core
    piece = width // 64
    units = w_gate.shape[1] // 2
    padded = (units + 127) // 128 * 128
    quarter = width // 4

    out_t, down_t = w_out.T, w_down.T

    def units_of(which):
        cut = [
            jnp.pad(lax.dynamic_slice_in_dim(w, which * units, units, 1), ((0, 0), (0, padded - units)))
            for w in (w_gate, w_up, down_t)
        ]
        return jnp.concatenate(cut, 1)

    def heads_of(which):
        cut = [lax.dynamic_slice_in_dim(w, which * HD, HD, 1) for w in (w_query, out_t)]
        return jnp.concatenate(cut + [w_key, w_value], 1)

    def chip_rows(of):
        mine, theirs = of(core), of(other)
        from_y, from_core, from_both = exchange((mine, theirs, theirs), "c")
        return pick(
            core,
            jnp.concatenate([mine, from_core, from_y, from_both], 0),
            jnp.concatenate([from_core, mine, from_both, from_y], 0),
        )

    head_rows = chip_rows(heads_of)
    ffn_rows = chip_rows(units_of)
    ffn_w = [lax.all_gather(ffn_rows, ("z", "x"), axis=0, tiled=True)]
    head_w = stack_rows(gather_ring(after(gather_direct(head_rows, False), ffn_rows), True))
    hidden_in = after(hidden_in, head_rows)
    query_w, out_w = head_w[:, :HD], head_w[:, HD : 2 * HD]
    key_w, value_w, pair_w = head_w[:, 2 * HD : 3 * HD], head_w[:, 3 * HD :], head_w[:, 2 * HD :]

    place = jnp.arange(width, dtype=jnp.int32)
    first, second = place // quarter, place // (quarter // 4) % 4

    def natural(z_at, x_at):
        y_at = (y + place // (2 * piece)) % 2
        return y_at * (width // 2) + z_at * (8 * piece) + x_at * (2 * piece) + place % (2 * piece)

    by_gather = natural(first, second)
    by_ring = natural((z + pick(core, second, first)) % 4, (x + pick(core, first, second)) % 4)
    to_gather, to_ring = ((place[:, None] == by[None, :]).astype(BF) for by in (by_gather, by_ring))
    from_gather, from_ring = ((by[:, None] == place[None, :]).astype(BF) for by in (by_gather, by_ring))

    def reorder(values, moves):
        return matmul(values, moves).astype(BF)

    def both_cores(values):
        return jnp.concatenate([values, shift(values, "c")], 0)

    def sum_cores(partial, moves):
        low = reorder(partial.astype(BF), moves)
        return wide_sum(low[:tokens], shift(low[tokens:], "c")).astype(BF)

    def sum_parts(partial, moves):
        chip = sum_cores(partial, moves)
        return wide_sum(chip, shift(chip, "s"))

    offsets = jnp.arange(tokens, dtype=jnp.int32)

    def positions_of(places):
        return (block_order[places.reshape(-1)][:, None] * tokens + offsets[None, :]).reshape(-1)

    def device_of(y_at, z_at, x_at, core_at):
        return y_at * 32 + z_at * 8 + x_at * 2 + core_at

    steps = jnp.arange(4, dtype=jnp.int32)
    outer, inner = steps[:, None, None], steps[None, :, None]

    def keys_of(which):
        z_at, x_at = (z + pick(which, inner, outer)) % 4, (x + pick(which, outer, inner)) % 4
        return positions_of(device_of((y + steps[None, None, :2]) % 2, z_at, x_at, which))

    key_pos = [keys_of(core), keys_of(other)]
    own_pos = positions_of(device_of(y, z, x, core))
    chip_pos = jnp.concatenate([own_pos, positions_of(device_of(y, z, x, other))])
    cosine_table, sine_table = tables(chip_pos, HD)

    attn_val, pre_attn_back = jax.vjp(rms_scale, hidden_in, norm_gains[0])
    attn_chip = reorder(both_cores(attn_val.astype(BF)), to_ring)
    attn_ring = attn_chip[:tokens]
    key_pre = matmul(attn_ring, key_w)
    value_low = matmul(attn_ring, value_w).astype(BF)
    key_val, key_back = jax.vjp(
        lambda values, gain: rotate(rms_scale(values, gain), cosine_table[:tokens], sine_table[:tokens]),
        key_pre,
        head_gains[1],
    )
    key_low = key_val.astype(BF)
    pair_low = jnp.concatenate([key_low, value_low], 1)
    own_pairs = jnp.concatenate(gather_ring(gather_minor_y(pair_low), True), 0)
    pairs = [own_pairs, shift(own_pairs, "c")]

    query_pre = matmul(attn_chip, query_w)
    query_val, query_back = jax.vjp(
        lambda values, gain: rotate(rms_scale(values, gain), cosine_table, sine_table),
        query_pre,
        head_gains[0],
    )
    score_scale = HD ** (-0.5)
    queries = (query_val.astype(BF).astype(F32) * score_scale).astype(BF)
    parts = [attend(queries, pairs[part], key_pos[part], chip_pos) for part in range(2)]
    weights = [part[0] for part in parts]
    inverse_total = 1.0 / (parts[0][1] + parts[1][1])
    accum = parts[0][2] + parts[1][2]
    attn_rows = accum * inverse_total
    mixed_low = attn_rows.astype(BF)
    attn_out = sum_parts(inner_cols(mixed_low, out_w), from_ring)
    post_attn, post_attn_back = jax.vjp(rms_scale, attn_out, norm_gains[1])
    mid_state = hidden_in + post_attn

    ffn_val, ffn_norm_back = jax.vjp(rms_scale, mid_state, norm_gains[2])
    ffn_chip = both_cores(ffn_val.astype(BF))
    gate_pre, up_pre, hidden_low, ffn_part = ffn_forward(reorder(ffn_chip, to_gather), ffn_w)
    ffn_out = sum_parts(ffn_part, from_gather)
    post_ffn, post_ffn_back = jax.vjp(rms_scale, ffn_out, norm_gains[3])
    block_out = mid_state + post_ffn

    ffn_grad, gain_four = post_ffn_back(out_grad)
    ffn_grad_chip = both_cores(ffn_grad.astype(BF))
    gate_low, up_low, ffn_norm_part = ffn_backward(reorder(ffn_grad_chip, to_gather), gate_pre, up_pre, ffn_w)
    sources = jnp.concatenate([ffn_chip, ffn_grad_chip], 0)
    ffn_norm_chip = sum_cores(ffn_norm_part, from_gather)
    left = after(inner_cols(from_gather, sources).astype(BF), ffn_norm_chip)
    ffn_wgrads = ffn_wgrad(left, gate_low, up_low, hidden_low)
    ffn_sum = lax.psum_scatter(ffn_wgrads, ("z", "x"), scatter_dimension=0, tiled=True)
    ffn_norm_grad = after(wide_sum(ffn_norm_chip, shift(ffn_norm_chip, "s")), ffn_wgrads)
    mid_from, gain_three = ffn_norm_back(ffn_norm_grad)
    mid_grad = out_grad + mid_from

    def last_stage(values):
        parts = split_rows(values.astype(BF), 4)
        kept = [pick(core, parts[i], parts[i + 1]) for i in (0, 2)]
        sent = [pick(core, parts[i + 1], parts[i]) for i in (0, 2)]
        from_y, from_core, from_both = exchange((kept[1], sent[0], sent[1]), "c")
        return wide_sum(kept[0], from_y), wide_sum(from_core, from_both)

    attn_grad, gain_two = post_attn_back(mid_grad)
    attn_grad_chip = reorder(both_cores(attn_grad.astype(BF)), to_ring)
    rows_grad = matmul(attn_grad_chip, out_w).astype(BF)
    rows_wide = rows_grad.astype(F32)
    row_dot = jnp.sum(rows_wide * attn_rows, axis=1)[:, None]
    rows_scaled = (rows_wide * inverse_total).astype(BF)
    pair_far, query_far = attend_back(
        queries, pairs[1], weights[1], rows_grad, rows_scaled, row_dot, inverse_total
    )
    pair_near, query_near = attend_back(
        queries, pairs[0], weights[0], rows_grad, rows_scaled, row_dot, inverse_total
    )
    query_grad = query_far + query_near
    query_pre_grad, query_gain = query_back(query_grad * score_scale)
    query_gain = query_gain + shift(query_gain, "s")
    query_pre_low = query_pre_grad.astype(BF)
    early_grads = jnp.concatenate(
        [inner_rows(attn_chip, query_pre_low), inner_rows(attn_grad_chip, mixed_low)], 1
    ).astype(BF)
    pair_got = shift(pair_far, "c")
    chunks = [
        jnp.concatenate([wide_sum(near, got).astype(BF), early], 0)
        for near, got, early in zip(*(split_rows(part, 4) for part in (pair_near, pair_got, early_grads)))
    ]
    major_sum = reduce_chunks(*chunks, True).astype(BF)
    pair_chunks = split_rows(major_sum[: 8 * tokens], 4)
    early_chunks = split_rows(major_sum[8 * tokens :], 4)
    minor_sum = reduce_direct(
        [jnp.concatenate([pair, early], 0) for pair, early in zip(pair_chunks, early_chunks)], False
    )
    pair_own, pair_far_y = split_rows(minor_sum[: 2 * tokens].astype(BF), 2)
    from_y, from_shard, from_both = exchange((pair_far_y, pair_own, pair_far_y), "s")
    pair_grad = wide_sum(pair_own, from_y) + wide_sum(from_shard, from_both)
    attn_norm_sum = sum_parts(inner_cols(query_pre_low, query_w), from_ring)
    key_pre_grad, key_gain = key_back(pair_grad[:, :HD])
    key_pre_low = key_pre_grad.astype(BF)
    value_grad_low = pair_grad[:, HD:].astype(BF)
    pair_part = inner_cols(jnp.concatenate([key_pre_low, value_grad_low], 1), pair_w).astype(BF)
    attn_norm_grad = attn_norm_sum + reorder(pair_part, from_ring).astype(F32)
    input_from, gain_one = pre_attn_back(attn_norm_grad)
    input_grad = mid_grad + input_from

    kept, sent = pick(core, key_pre_low, value_grad_low), pick(core, value_grad_low, key_pre_low)
    pair_chip = jnp.concatenate([kept, shift(sent, "c")], 0)
    heads = [
        jnp.pad(gain.reshape(64, HD // 64), ((0, 0), (0, piece - HD // 64))).reshape(width)
        for gain in (query_gain, key_gain)
    ]
    gains = jnp.stack([gain_one, gain_two, gain_three, gain_four] + heads, 1)
    gains = jnp.pad(gains, ((0, 0), (0, 128 - gains.shape[1]))).astype(BF)
    late_grads = jnp.concatenate([inner_rows(attn_chip, pair_chip), inner_rows(to_ring, gains)], 1).astype(BF)
    ffn_mine, ffn_got = last_stage(after(ffn_sum, minor_sum))
    late_major = after(reduce_direct(split_rows(late_grads, 4), True).astype(BF), ffn_mine, ffn_got)
    late_sum = reduce_direct(split_rows(late_major, 4), False)
    head_mine, head_got = last_stage(jnp.concatenate([minor_sum[2 * tokens :], late_sum], 1))

    def joined(start, size, mine, got):
        left, right = mine[:, start : start + size], got[:, start : start + size]
        return pick(core, jnp.concatenate([left, right], 1), jnp.concatenate([right, left], 1))

    gate_wgrad = joined(0, units, ffn_mine, ffn_got)
    up_wgrad = joined(padded, units, ffn_mine, ffn_got)
    down_wgrad = joined(2 * padded, units, ffn_mine, ffn_got).T

    query_wgrad = joined(0, HD, head_mine, head_got)
    out_wgrad = joined(HD, HD, head_mine, head_got).T
    pair_wgrad = joined(2 * HD, HD, head_mine, head_got)
    gain_sums = head_mine[:, 3 * HD :] + head_got[:, 3 * HD :]
    return (
        block_out,
        input_grad,
        query_wgrad,
        pair_wgrad[:, :HD],
        pair_wgrad[:, HD:],
        out_wgrad,
        gate_wgrad,
        up_wgrad,
        down_wgrad,
        gain_sums[:, :4].T,
        gain_sums[: HD // 64, 4:6].T,
    )


def solution(mesh):
    fine = Mesh(mesh.devices.reshape(2, 4, 4, 2, 2), ("y", "z", "x", "c", "s"))
    placed = (
        P(CTX, None),
        P(CTX, None),
        P(),
        P(),
        P(),
        P(CTX, "s"),
        P(CTX, None),
        P(CTX, None),
        P("s", CTX),
        P(CTX, "s"),
        P(CTX, "s"),
        P("s", CTX),
    )
    return jax.shard_map(
        shards,
        mesh=fine,
        in_specs=placed,
        out_specs=(
            P(CTX, None),
            P(CTX, None),
            P(CTX, "s"),
            P(CTX, None),
            P(CTX, None),
            P("s", CTX),
            P(CTX, "s"),
            P(CTX, "s"),
            P("s", CTX),
            P(None, CTX),
            P(None, CTX),
        ),
        check_vma=False,
    )
```

```python
import math

import jax
import jax.numpy as jnp
from jax import lax
from jax.experimental import pallas as pl
from jax.experimental.pallas import tpu as pltpu
from jax.sharding import Mesh, PartitionSpec as P

HD = 256
EPS = 1e-06
THETA = 1000000.0
BF = jnp.bfloat16
F32 = jnp.float32
CTX = ("y", "z", "x", "c")


def matmul(left, right):
    return jnp.dot(left, right, preferred_element_type=F32)


def inner_rows(left, right):
    return lax.dot_general(left, right, (((0,), (0,)), ((), ())), preferred_element_type=F32)


def inner_cols(left, right):
    return lax.dot_general(left, right, (((1,), (1,)), ((), ())), preferred_element_type=F32)


def rms_scale(values, gain):
    return values * lax.rsqrt(jnp.mean(values * values, axis=-1, keepdims=True) + EPS) * gain


def rotate(values, cosine_table, sine_table):
    half_width = values.shape[-1] // 2
    first = values[..., :half_width]
    second = values[..., half_width:]
    return jnp.concatenate(
        [first * cosine_table - second * sine_table, second * cosine_table + first * sine_table],
        axis=-1,
    )


def tables(positions, head_width):
    frequency = jnp.arange(head_width // 2, dtype=F32)
    inverse = jnp.exp(frequency * (-2.0 * math.log(THETA) / head_width))
    angles = positions.astype(F32)[:, None] * inverse[None, :]
    return (jnp.cos(angles), jnp.sin(angles))


def shift(values, axis, step=1):
    size = lax.axis_size(axis)
    return lax.ppermute(values, axis, [(i, (i + step) % size) for i in range(size)])


def ring(values, major, step, cross_y=False):
    moves = []
    for y in range(2):
        for z in range(4):
            for x in range(4):
                for core in range(2):
                    along_x = major == (core == 0)
                    to_z, to_x = (z, (x + step) % 4) if along_x else ((z + step) % 4, x)
                    to_y = 1 - y if cross_y else y
                    moves.append((y * 32 + z * 8 + x * 2 + core, to_y * 32 + to_z * 8 + to_x * 2 + core))
    return lax.ppermute(values, CTX, moves)


def gather_direct(block, major):
    return jnp.concatenate([block] + [ring(block, major, -k) for k in (1, 2, 3)], 0)


def gather_minor_y(block):
    blocks = [block if k == 0 else ring(block, False, -k) for k in range(4)]
    others = [ring(block, False, -k, True) for k in range(4)]
    return jnp.concatenate([part for pair in zip(blocks, others) for part in pair], 0)


def exchange(values, axis):
    both = [(i, 3 - i) for i in range(4)]
    return shift(values[0], "y"), shift(values[1], axis), lax.ppermute(values[2], ("y", axis), both)


def after(value, *others):
    return lax.optimization_barrier((value, *others))[0]


def gather_ring(block, major):
    half = (block.shape[0] // 2 + 7) // 8 * 8
    previous, following = ring(block, major, 1), ring(block, major, -1)
    far_low = ring(previous[:half], major, 1)
    far_high = ring(following[half:], major, -1)
    return [block, following, far_low, far_high, previous]


def wide_sum(*parts):
    return sum(part.astype(F32) for part in parts)


def reduce_direct(chunks, major):
    return wide_sum(chunks[0], *[ring(chunks[k], major, k) for k in (1, 2, 3)])


def reduce_first(far_low, far_high, major):
    return ring(far_low, major, 1), ring(far_high, major, -1)


def reduce_second(own, following, previous, from_previous, from_next, major):
    half = from_previous.shape[0]
    forward = jnp.concatenate(
        [wide_sum(following[:half], from_previous).astype(BF), following[half:]], 0
    )
    backward = jnp.concatenate(
        [previous[:half], wide_sum(previous[half:], from_next).astype(BF)], 0
    )
    return wide_sum(own, ring(forward, major, 1), ring(backward, major, -1))


def reduce_chunks(own, following, far, previous, major):
    half = (far.shape[0] // 2 + 7) // 8 * 8
    return reduce_second(own, following, previous, *reduce_first(far[:half], far[half:], major), major)


ATTN_BLOCK = 1024
VMEM = pltpu.CompilerParams(vmem_limit_bytes=48 * 1024 * 1024)


def attend_kernel(query, pair, key_pos, query_pos, weight, total, accum):
    scores = inner_cols(query[...], pair[:, :HD])
    exps = jnp.where(query_pos[...] >= key_pos[...], jnp.exp(scores), 0.0)
    low = exps.astype(BF)
    weight[...] = low

    @pl.when(pl.program_id(0) == 0)
    def _():
        total[...] = jnp.zeros_like(total)
        accum[...] = jnp.zeros_like(accum)

    total[...] += jnp.sum(exps, axis=1, keepdims=True)
    accum[...] += matmul(low, pair[:, HD:])


def attend(queries, pairs, key_pos, query_pos):
    rows, keys = queries.shape[0], pairs.shape[0]
    whole = lambda i: (0, 0)
    return pl.pallas_call(
        attend_kernel,
        grid=(keys // ATTN_BLOCK,),
        in_specs=[
            pl.BlockSpec((rows, HD), whole),
            pl.BlockSpec((ATTN_BLOCK, 2 * HD), lambda i: (i, 0)),
            pl.BlockSpec((1, ATTN_BLOCK), lambda i: (0, i)),
            pl.BlockSpec((rows, 1), whole),
        ],
        out_specs=[
            pl.BlockSpec((rows, ATTN_BLOCK), lambda i: (0, i)),
            pl.BlockSpec((rows, 1), whole),
            pl.BlockSpec((rows, HD), whole),
        ],
        out_shape=[
            jax.ShapeDtypeStruct((rows, keys), BF),
            jax.ShapeDtypeStruct((rows, 1), F32),
            jax.ShapeDtypeStruct((rows, HD), F32),
        ],
        compiler_params=VMEM,
        name="attend",
    )(queries, pairs, key_pos[None, :], query_pos[:, None])


def attend_back_kernel(query, pair, weight, grad, scaled, dot, inverse, pair_grad, query_grad):
    weights = weight[...]
    prob_grad = inner_cols(grad[...], pair[:, HD:])
    score_grad = (weights.astype(F32) * ((prob_grad - dot[...]) * inverse[...])).astype(BF)
    pair_grad[:, :HD] = inner_rows(score_grad, query[...]).astype(BF)
    pair_grad[:, HD:] = inner_rows(weights, scaled[...]).astype(BF)

    @pl.when(pl.program_id(0) == 0)
    def _():
        query_grad[...] = jnp.zeros_like(query_grad)

    query_grad[...] += matmul(score_grad, pair[:, :HD])


def attend_back(queries, pairs, weights, grads, scaled, dot, inverse):
    rows, keys = queries.shape[0], pairs.shape[0]
    whole = lambda i: (0, 0)
    return pl.pallas_call(
        attend_back_kernel,
        grid=(keys // ATTN_BLOCK,),
        in_specs=[
            pl.BlockSpec((rows, HD), whole),
            pl.BlockSpec((ATTN_BLOCK, 2 * HD), lambda i: (i, 0)),
            pl.BlockSpec((rows, ATTN_BLOCK), lambda i: (0, i)),
            pl.BlockSpec((rows, HD), whole),
            pl.BlockSpec((rows, HD), whole),
            pl.BlockSpec((rows, 1), whole),
            pl.BlockSpec((rows, 1), whole),
        ],
        out_specs=[
            pl.BlockSpec((ATTN_BLOCK, 2 * HD), lambda i: (i, 0)),
            pl.BlockSpec((rows, HD), whole),
        ],
        out_shape=[
            jax.ShapeDtypeStruct((keys, 2 * HD), BF),
            jax.ShapeDtypeStruct((rows, HD), F32),
        ],
        compiler_params=VMEM,
        name="attend_back",
    )(queries, pairs, weights, grads, scaled, dot, inverse)


def stack_kernel(*refs):
    start = 0
    for piece in refs[:-1]:
        refs[-1][start : start + piece.shape[0], :] = piece[...]
        start += piece.shape[0]


def stack_rows(pieces, tile=256):
    rows, columns = sum(piece.shape[0] for piece in pieces), pieces[0].shape[1]
    return pl.pallas_call(
        stack_kernel,
        grid=(columns // tile,),
        in_specs=[pl.BlockSpec((piece.shape[0], tile), lambda j: (0, j)) for piece in pieces],
        out_specs=pl.BlockSpec((rows, tile), lambda j: (0, j)),
        out_shape=jax.ShapeDtypeStruct((rows, columns), pieces[0].dtype),
        compiler_params=VMEM,
        name="stack_rows",
    )(*pieces)


UNIT_TILE = 256
GELU_IN = math.sqrt(2.0 / math.pi)
GELU_CUBE = 0.044715


def joined_rows(refs):
    return jnp.concatenate([ref[...] for ref in refs], 0)


def ffn_kernel(source, *refs):
    count = (len(refs) - 4) // 3
    gate_w, up_w, down_w = (joined_rows(refs[i * count : (i + 1) * count]) for i in range(3))
    gate, up, hidden, total = refs[3 * count :]
    gate_pre = matmul(source[...], gate_w)
    up_pre = matmul(source[...], up_w)
    gate[...] = gate_pre
    up[...] = up_pre
    inner = GELU_IN * (gate_pre + GELU_CUBE * (gate_pre * gate_pre * gate_pre))
    low = (0.5 * gate_pre * (1.0 + jnp.tanh(inner)) * up_pre).astype(BF)
    hidden[...] = low

    @pl.when(pl.program_id(0) == 0)
    def _():
        total[...] = jnp.zeros_like(total)

    total[...] += inner_cols(low, down_w)


def ffn_back_kernel(grad, gate, up, *refs):
    count = (len(refs) - 3) // 3
    gate_w, up_w, down_w = (joined_rows(refs[i * count : (i + 1) * count]) for i in range(3))
    gate_grad, up_grad, total = refs[3 * count :]
    hidden_grad = matmul(grad[...], down_w)
    gate_pre = gate[...]
    square = gate_pre * gate_pre
    bend = jnp.tanh(GELU_IN * (gate_pre + GELU_CUBE * (square * gate_pre)))
    rise = 0.5 * (1.0 + bend)
    slope = rise + 0.5 * gate_pre * (1.0 - bend * bend) * (GELU_IN * (1.0 + 3.0 * GELU_CUBE * square))
    gate_low = (hidden_grad * up[...] * slope).astype(BF)
    up_low = (hidden_grad * (gate_pre * rise)).astype(BF)
    gate_grad[...] = gate_low
    up_grad[...] = up_low

    @pl.when(pl.program_id(0) == 0)
    def _():
        total[...] = jnp.zeros_like(total)

    total[...] += inner_cols(gate_low, gate_w) + inner_cols(up_low, up_w)


def unit_specs(rows, pieces, tiles):
    own = pl.BlockSpec((rows, UNIT_TILE), lambda j: (0, j))
    weights = [
        pl.BlockSpec((piece.shape[0], UNIT_TILE), lambda j, i=i: (0, j + i * tiles))
        for i in range(3)
        for piece in pieces
    ]
    return own, weights


def ffn_forward(source, pieces):
    rows, width = source.shape
    units = pieces[0].shape[1] // 3
    tiles = units // UNIT_TILE
    own, weights = unit_specs(rows, pieces, tiles)
    whole = pl.BlockSpec((rows, width), lambda j: (0, 0))
    return pl.pallas_call(
        ffn_kernel,
        grid=(tiles,),
        in_specs=[whole] + weights,
        out_specs=[own, own, own, whole],
        out_shape=[
            jax.ShapeDtypeStruct((rows, units), F32),
            jax.ShapeDtypeStruct((rows, units), F32),
            jax.ShapeDtypeStruct((rows, units), BF),
            jax.ShapeDtypeStruct((rows, width), F32),
        ],
        compiler_params=VMEM,
        name="ffn_forward",
    )(source, *pieces, *pieces, *pieces)


def ffn_backward(grad, gate, up, pieces):
    rows, width = grad.shape
    units = pieces[0].shape[1] // 3
    tiles = units // UNIT_TILE
    own, weights = unit_specs(rows, pieces, tiles)
    whole = pl.BlockSpec((rows, width), lambda j: (0, 0))
    return pl.pallas_call(
        ffn_back_kernel,
        grid=(tiles,),
        in_specs=[whole, own, own] + weights,
        out_specs=[own, own, whole],
        out_shape=[
            jax.ShapeDtypeStruct((rows, units), BF),
            jax.ShapeDtypeStruct((rows, units), BF),
            jax.ShapeDtypeStruct((rows, width), F32),
        ],
        compiler_params=VMEM,
        name="ffn_backward",
    )(grad, gate, up, *pieces, *pieces, *pieces)


def ffn_wgrad_kernel(steps, left, gate, up, hidden, out):
    rows = gate.shape[0]
    for i, (first, right) in enumerate([(0, gate), (0, up), (rows, hidden)]):

        @pl.when(pl.program_id(0) // steps == i)
        def _(first=first, right=right):
            out[...] = matmul(left[:, first : first + rows], right[...]).astype(BF)


def ffn_wgrad(left, gate, up, hidden):
    width, (rows, units) = left.shape[0], gate.shape
    steps = 2
    tile = units // steps

    def spec(i):
        return pl.BlockSpec((rows, tile), lambda j: (0, jnp.clip(j - i * steps, 0, steps - 1)))

    return pl.pallas_call(
        lambda *refs: ffn_wgrad_kernel(steps, *refs),
        grid=(3 * steps,),
        in_specs=[pl.BlockSpec(left.shape, lambda j: (0, 0)), spec(0), spec(1), spec(2)],
        out_specs=pl.BlockSpec((width, tile), lambda j: (0, j)),
        out_shape=jax.ShapeDtypeStruct((width, 3 * units), BF),
        compiler_params=VMEM,
        name="ffn_wgrad",
    )(left, gate, up, hidden)


def split_rows(values, parts):
    size = values.shape[0] // parts
    return [values[i * size : (i + 1) * size] for i in range(parts)]


def pick(core, first, second):
    return jnp.where(core == 0, first, second)


def shards(
    hidden_in,
    out_grad,
    block_order,
    norm_gains,
    head_gains,
    w_query,
    w_key,
    w_value,
    w_out,
    w_gate,
    w_up,
    w_down,
):
    tokens, width = hidden_in.shape
    y, z, x, core = (lax.axis_index(name) for name in CTX)
    other = 1 - core
    piece = width // 64
    units = w_gate.shape[1] // 2
    padded = (units + 127) // 128 * 128
    quarter = width // 4

    out_t, down_t = w_out.T, w_down.T

    def units_of(which):
        cut = [
            jnp.pad(lax.dynamic_slice_in_dim(w, which * units, units, 1), ((0, 0), (0, padded - units)))
            for w in (w_gate, w_up, down_t)
        ]
        return jnp.concatenate(cut, 1)

    def heads_of(which):
        cut = [lax.dynamic_slice_in_dim(w, which * HD, HD, 1) for w in (w_query, out_t)]
        return jnp.concatenate(cut + [w_key, w_value], 1)

    def chip_rows(of, *others):
        mine, theirs = after(of(core), *others), after(of(other), *others)
        from_y, from_core, from_both = exchange((mine, theirs, theirs), "c")
        return pick(
            core,
            jnp.concatenate([mine, from_core, from_y, from_both], 0),
            jnp.concatenate([from_core, mine, from_both, from_y], 0),
        )

    head_rows = chip_rows(heads_of)
    ffn_rows = chip_rows(units_of, head_rows)
    ffn_w = [lax.all_gather(ffn_rows, ("z", "x"), axis=0, tiled=True)]
    head_w = stack_rows(gather_ring(after(gather_direct(head_rows, False), ffn_rows), True))
    hidden_in = after(hidden_in, head_rows)
    query_w, out_w = head_w[:, :HD], head_w[:, HD : 2 * HD]
    key_w, value_w, pair_w = head_w[:, 2 * HD : 3 * HD], head_w[:, 3 * HD :], head_w[:, 2 * HD :]

    place = jnp.arange(width, dtype=jnp.int32)
    first, second = place // quarter, place // (quarter // 4) % 4

    def natural(z_at, x_at):
        y_at = (y + place // (2 * piece)) % 2
        return y_at * (width // 2) + z_at * (8 * piece) + x_at * (2 * piece) + place % (2 * piece)

    by_gather = natural(first, second)
    by_ring = natural((z + pick(core, second, first)) % 4, (x + pick(core, first, second)) % 4)
    to_gather, to_ring = ((place[:, None] == by[None, :]).astype(BF) for by in (by_gather, by_ring))
    from_gather, from_ring = ((by[:, None] == place[None, :]).astype(BF) for by in (by_gather, by_ring))

    def reorder(values, moves):
        return matmul(values, moves).astype(BF)

    def both_cores(values):
        return jnp.concatenate([values, shift(values, "c")], 0)

    def sum_cores(partial, moves):
        low = reorder(partial.astype(BF), moves)
        return wide_sum(low[:tokens], shift(low[tokens:], "c")).astype(BF)

    def sum_parts(partial, moves):
        chip = sum_cores(partial, moves)
        return wide_sum(chip, shift(chip, "s"))

    offsets = jnp.arange(tokens, dtype=jnp.int32)

    def positions_of(places):
        return (block_order[places.reshape(-1)][:, None] * tokens + offsets[None, :]).reshape(-1)

    def device_of(y_at, z_at, x_at, core_at):
        return y_at * 32 + z_at * 8 + x_at * 2 + core_at

    steps = jnp.arange(4, dtype=jnp.int32)
    outer, inner = steps[:, None, None], steps[None, :, None]

    def keys_of(which):
        z_at, x_at = (z + pick(which, inner, outer)) % 4, (x + pick(which, outer, inner)) % 4
        return positions_of(device_of((y + steps[None, None, :2]) % 2, z_at, x_at, which))

    key_pos = [keys_of(core), keys_of(other)]
    own_pos = positions_of(device_of(y, z, x, core))
    chip_pos = jnp.concatenate([own_pos, positions_of(device_of(y, z, x, other))])
    cosine_table, sine_table = tables(chip_pos, HD)

    attn_val, pre_attn_back = jax.vjp(rms_scale, hidden_in, norm_gains[0])
    attn_chip = reorder(both_cores(attn_val.astype(BF)), to_ring)
    attn_ring = attn_chip[:tokens]
    key_pre = matmul(attn_ring, key_w)
    value_low = matmul(attn_ring, value_w).astype(BF)
    key_val, key_back = jax.vjp(
        lambda values, gain: rotate(rms_scale(values, gain), cosine_table[:tokens], sine_table[:tokens]),
        key_pre,
        head_gains[1],
    )
    key_low = key_val.astype(BF)
    pair_low = jnp.concatenate([key_low, value_low], 1)
    own_pairs = jnp.concatenate(gather_ring(gather_minor_y(pair_low), True), 0)
    pairs = [own_pairs, shift(own_pairs, "c")]

    query_pre = matmul(attn_chip, query_w)
    query_val, query_back = jax.vjp(
        lambda values, gain: rotate(rms_scale(values, gain), cosine_table, sine_table),
        query_pre,
        head_gains[0],
    )
    score_scale = HD ** (-0.5)
    queries = (query_val.astype(BF).astype(F32) * score_scale).astype(BF)
    parts = [attend(queries, pairs[part], key_pos[part], chip_pos) for part in range(2)]
    weights = [part[0] for part in parts]
    inverse_total = 1.0 / (parts[0][1] + parts[1][1])
    accum = parts[0][2] + parts[1][2]
    attn_rows = accum * inverse_total
    mixed_low = attn_rows.astype(BF)
    attn_out = sum_parts(inner_cols(mixed_low, out_w), from_ring)
    post_attn, post_attn_back = jax.vjp(rms_scale, attn_out, norm_gains[1])
    mid_state = hidden_in + post_attn

    ffn_val, ffn_norm_back = jax.vjp(rms_scale, mid_state, norm_gains[2])
    ffn_chip = both_cores(ffn_val.astype(BF))
    gate_pre, up_pre, hidden_low, ffn_part = ffn_forward(reorder(ffn_chip, to_gather), ffn_w)
    ffn_out = sum_parts(ffn_part, from_gather)
    post_ffn, post_ffn_back = jax.vjp(rms_scale, ffn_out, norm_gains[3])
    block_out = mid_state + post_ffn

    ffn_grad, gain_four = post_ffn_back(out_grad)
    ffn_grad_chip = both_cores(ffn_grad.astype(BF))
    gate_low, up_low, ffn_norm_part = ffn_backward(reorder(ffn_grad_chip, to_gather), gate_pre, up_pre, ffn_w)
    sources = jnp.concatenate([ffn_chip, ffn_grad_chip], 0)
    ffn_norm_chip = sum_cores(ffn_norm_part, from_gather)
    left = after(inner_cols(from_gather, sources).astype(BF), ffn_norm_chip)
    ffn_wgrads = ffn_wgrad(left, gate_low, up_low, hidden_low)
    ffn_sum = lax.psum_scatter(ffn_wgrads, ("z", "x"), scatter_dimension=0, tiled=True)
    ffn_norm_grad = after(wide_sum(ffn_norm_chip, shift(ffn_norm_chip, "s")), ffn_wgrads)
    mid_from, gain_three = ffn_norm_back(ffn_norm_grad)
    mid_grad = out_grad + mid_from

    def last_stage(values):
        parts = split_rows(values.astype(BF), 4)
        kept = [pick(core, parts[i], parts[i + 1]) for i in (0, 2)]
        sent = [pick(core, parts[i + 1], parts[i]) for i in (0, 2)]
        from_y, from_core, from_both = exchange((kept[1], sent[0], sent[1]), "c")
        return wide_sum(kept[0], from_y), wide_sum(from_core, from_both)

    attn_grad, gain_two = post_attn_back(mid_grad)
    attn_grad_chip = reorder(both_cores(attn_grad.astype(BF)), to_ring)
    rows_grad = matmul(attn_grad_chip, out_w).astype(BF)
    rows_wide = rows_grad.astype(F32)
    row_dot = jnp.sum(rows_wide * attn_rows, axis=1)[:, None]
    rows_scaled = (rows_wide * inverse_total).astype(BF)
    pair_far, query_far = attend_back(
        queries, pairs[1], weights[1], rows_grad, rows_scaled, row_dot, inverse_total
    )
    pair_near, query_near = attend_back(
        queries, pairs[0], weights[0], rows_grad, rows_scaled, row_dot, inverse_total
    )
    query_grad = query_far + query_near
    query_pre_grad, query_gain = query_back(query_grad * score_scale)
    query_gain = query_gain + shift(query_gain, "s")
    query_pre_low = query_pre_grad.astype(BF)
    early_grads = jnp.concatenate(
        [inner_rows(attn_chip, query_pre_low), inner_rows(attn_grad_chip, mixed_low)], 1
    ).astype(BF)
    pair_got = shift(pair_far, "c")
    chunks = [
        jnp.concatenate([wide_sum(near, got).astype(BF), early], 0)
        for near, got, early in zip(*(split_rows(part, 4) for part in (pair_near, pair_got, early_grads)))
    ]
    major_sum = reduce_chunks(*chunks, True).astype(BF)
    pair_chunks = split_rows(major_sum[: 8 * tokens], 4)
    early_chunks = split_rows(major_sum[8 * tokens :], 4)
    minor_sum = reduce_direct(
        [jnp.concatenate([pair, early], 0) for pair, early in zip(pair_chunks, early_chunks)], False
    )
    pair_own, pair_far_y = split_rows(minor_sum[: 2 * tokens].astype(BF), 2)
    from_y, from_shard, from_both = exchange((pair_far_y, pair_own, pair_far_y), "s")
    pair_grad = wide_sum(pair_own, from_y) + wide_sum(from_shard, from_both)
    attn_norm_sum = sum_parts(inner_cols(query_pre_low, query_w), from_ring)
    key_pre_grad, key_gain = key_back(pair_grad[:, :HD])
    key_pre_low = key_pre_grad.astype(BF)
    value_grad_low = pair_grad[:, HD:].astype(BF)
    pair_part = inner_cols(jnp.concatenate([key_pre_low, value_grad_low], 1), pair_w).astype(BF)
    attn_norm_grad = attn_norm_sum + reorder(pair_part, from_ring).astype(F32)
    input_from, _ = pre_attn_back(attn_norm_grad)
    input_grad = mid_grad + input_from

    kept, sent = pick(core, key_pre_low, value_grad_low), pick(core, value_grad_low, key_pre_low)
    pair_chip = jnp.concatenate([kept, shift(sent, "c")], 0)
    heads = [
        jnp.pad(gain.reshape(64, HD // 64), ((0, 0), (0, piece - HD // 64))).reshape(width)
        for gain in (query_gain, key_gain)
    ]
    gains = jnp.stack([gain_two, gain_three, gain_four] + heads, 1)
    gains = jnp.pad(gains, ((0, 0), (0, 128 - gains.shape[1]))).astype(BF)
    late_grads = jnp.concatenate([inner_rows(attn_chip, pair_chip), inner_rows(to_ring, gains)], 1).astype(BF)
    early_mine, early_got = last_stage(
        jnp.concatenate([after(ffn_sum, minor_sum).astype(F32), minor_sum[2 * tokens :]], 1)
    )
    late_grads = after(late_grads, early_mine, early_got)
    late_major = reduce_direct(split_rows(late_grads, 4), True).astype(BF)
    late_sum = reduce_direct(split_rows(late_major, 4), False)
    late_mine, late_got = last_stage(late_sum)

    def joined(start, size, mine, got):
        left, right = mine[:, start : start + size], got[:, start : start + size]
        return pick(core, jnp.concatenate([left, right], 1), jnp.concatenate([right, left], 1))

    gate_wgrad = joined(0, units, early_mine, early_got)
    up_wgrad = joined(padded, units, early_mine, early_got)
    down_wgrad = joined(2 * padded, units, early_mine, early_got).T

    query_wgrad = joined(3 * padded, HD, early_mine, early_got)
    out_wgrad = joined(3 * padded + HD, HD, early_mine, early_got).T
    pair_wgrad = joined(0, HD, late_mine, late_got)
    key_wgrad, value_wgrad = pair_wgrad[:, :HD], pair_wgrad[:, HD:]
    gain_sums = late_mine[:, HD:] + late_got[:, HD:]

    def along(weight, grad):
        return jnp.sum(weight.astype(F32) * grad, axis=1)

    query_part = along(w_query, query_wgrad)
    attn_part = query_part + shift(query_part, "s") + along(w_key, key_wgrad) + along(w_value, value_wgrad)
    own_gain = lax.dynamic_slice_in_dim(norm_gains[0], device_of(y, z, x, core) * piece, piece)
    gain_one = attn_part / own_gain
    return (
        block_out,
        input_grad,
        query_wgrad,
        key_wgrad,
        value_wgrad,
        out_wgrad,
        gate_wgrad,
        up_wgrad,
        down_wgrad,
        jnp.concatenate([gain_one[None, :], gain_sums[:, :3].T], 0),
        gain_sums[: HD // 64, 3:5].T,
    )


def solution(mesh):
    fine = Mesh(mesh.devices.reshape(2, 4, 4, 2, 2), ("y", "z", "x", "c", "s"))
    placed = (
        P(CTX, None),
        P(CTX, None),
        P(),
        P(),
        P(),
        P(CTX, "s"),
        P(CTX, None),
        P(CTX, None),
        P("s", CTX),
        P(CTX, "s"),
        P(CTX, "s"),
        P("s", CTX),
    )
    return jax.shard_map(
        shards,
        mesh=fine,
        in_specs=placed,
        out_specs=(
            P(CTX, None),
            P(CTX, None),
            P(CTX, "s"),
            P(CTX, None),
            P(CTX, None),
            P("s", CTX),
            P(CTX, "s"),
            P(CTX, "s"),
            P("s", CTX),
            P(None, CTX),
            P(None, CTX),
        ),
        check_vma=False,
    )
```

```python
import math

import jax
import jax.numpy as jnp
from jax import lax
from jax.experimental import pallas as pl
from jax.experimental.pallas import tpu as pltpu
from jax.sharding import Mesh, PartitionSpec as P

HD = 256
EPS = 1e-06
THETA = 1000000.0
BF = jnp.bfloat16
F32 = jnp.float32
CTX = ("y", "z", "x", "c")


def matmul(left, right):
    return jnp.dot(left, right, preferred_element_type=F32)


def inner_rows(left, right):
    return lax.dot_general(left, right, (((0,), (0,)), ((), ())), preferred_element_type=F32)


def inner_cols(left, right):
    return lax.dot_general(left, right, (((1,), (1,)), ((), ())), preferred_element_type=F32)


def rms_scale(values, gain):
    return values * lax.rsqrt(jnp.mean(values * values, axis=-1, keepdims=True) + EPS) * gain


def rotate(values, cosine_table, sine_table):
    half_width = values.shape[-1] // 2
    first = values[..., :half_width]
    second = values[..., half_width:]
    return jnp.concatenate(
        [first * cosine_table - second * sine_table, second * cosine_table + first * sine_table],
        axis=-1,
    )


def tables(positions, head_width):
    frequency = jnp.arange(head_width // 2, dtype=F32)
    inverse = jnp.exp(frequency * (-2.0 * math.log(THETA) / head_width))
    angles = positions.astype(F32)[:, None] * inverse[None, :]
    return (jnp.cos(angles), jnp.sin(angles))


def shift(values, axis, step=1):
    size = lax.axis_size(axis)
    return lax.ppermute(values, axis, [(i, (i + step) % size) for i in range(size)])


def ring(values, major, step, cross_y=False):
    moves = []
    for y in range(2):
        for z in range(4):
            for x in range(4):
                for core in range(2):
                    along_x = major == (core == 0)
                    to_z, to_x = (z, (x + step) % 4) if along_x else ((z + step) % 4, x)
                    to_y = 1 - y if cross_y else y
                    moves.append((y * 32 + z * 8 + x * 2 + core, to_y * 32 + to_z * 8 + to_x * 2 + core))
    return lax.ppermute(values, CTX, moves)


def gather_direct(block, major):
    return jnp.concatenate([block] + [ring(block, major, -k) for k in (1, 2, 3)], 0)


def gather_minor_y(block):
    blocks = [block if k == 0 else ring(block, False, -k) for k in range(4)]
    others = [ring(block, False, -k, True) for k in range(4)]
    return jnp.concatenate([part for pair in zip(blocks, others) for part in pair], 0)


def exchange(values, axis):
    both = [(i, 3 - i) for i in range(4)]
    return shift(values[0], "y"), shift(values[1], axis), lax.ppermute(values[2], ("y", axis), both)


def after(value, *others):
    return lax.optimization_barrier((value, *others))[0]


def gather_ring(block, major):
    half = (block.shape[0] // 2 + 7) // 8 * 8
    previous, following = ring(block, major, 1), ring(block, major, -1)
    far_low = ring(previous[:half], major, 1)
    far_high = ring(following[half:], major, -1)
    return [block, following, far_low, far_high, previous]


def wide_sum(*parts):
    return sum(part.astype(F32) for part in parts)


def reduce_direct(chunks, major):
    return wide_sum(chunks[0], *[ring(chunks[k], major, k) for k in (1, 2, 3)])


def reduce_first(far_low, far_high, major):
    return ring(far_low, major, 1), ring(far_high, major, -1)


def reduce_second(own, following, previous, from_previous, from_next, major):
    half = from_previous.shape[0]
    forward = jnp.concatenate(
        [wide_sum(following[:half], from_previous).astype(BF), following[half:]], 0
    )
    backward = jnp.concatenate(
        [previous[:half], wide_sum(previous[half:], from_next).astype(BF)], 0
    )
    return wide_sum(own, ring(forward, major, 1), ring(backward, major, -1))


def reduce_chunks(own, following, far, previous, major):
    half = (far.shape[0] // 2 + 7) // 8 * 8
    return reduce_second(own, following, previous, *reduce_first(far[:half], far[half:], major), major)


ATTN_BLOCK = 1024
VMEM = pltpu.CompilerParams(vmem_limit_bytes=48 * 1024 * 1024)


def attend_kernel(query, pair, key_pos, query_pos, weight, total, accum):
    scores = inner_cols(query[...], pair[:, :HD])
    exps = jnp.where(query_pos[...] >= key_pos[...], jnp.exp(scores), 0.0)
    low = exps.astype(BF)
    weight[...] = low

    @pl.when(pl.program_id(0) == 0)
    def _():
        total[...] = jnp.zeros_like(total)
        accum[...] = jnp.zeros_like(accum)

    total[...] += jnp.sum(exps, axis=1, keepdims=True)
    accum[...] += matmul(low, pair[:, HD:])


def attend(queries, pairs, key_pos, query_pos):
    rows, keys = queries.shape[0], pairs.shape[0]
    whole = lambda i: (0, 0)
    return pl.pallas_call(
        attend_kernel,
        grid=(keys // ATTN_BLOCK,),
        in_specs=[
            pl.BlockSpec((rows, HD), whole),
            pl.BlockSpec((ATTN_BLOCK, 2 * HD), lambda i: (i, 0)),
            pl.BlockSpec((1, ATTN_BLOCK), lambda i: (0, i)),
            pl.BlockSpec((rows, 1), whole),
        ],
        out_specs=[
            pl.BlockSpec((rows, ATTN_BLOCK), lambda i: (0, i)),
            pl.BlockSpec((rows, 1), whole),
            pl.BlockSpec((rows, HD), whole),
        ],
        out_shape=[
            jax.ShapeDtypeStruct((rows, keys), BF),
            jax.ShapeDtypeStruct((rows, 1), F32),
            jax.ShapeDtypeStruct((rows, HD), F32),
        ],
        compiler_params=VMEM,
        name="attend",
    )(queries, pairs, key_pos[None, :], query_pos[:, None])


def attend_back_kernel(query, pair, weight, grad, scaled, dot, inverse, pair_grad, query_grad):
    weights = weight[...]
    prob_grad = inner_cols(grad[...], pair[:, HD:])
    score_grad = (weights.astype(F32) * ((prob_grad - dot[...]) * inverse[...])).astype(BF)
    pair_grad[:, :HD] = inner_rows(score_grad, query[...]).astype(BF)
    pair_grad[:, HD:] = inner_rows(weights, scaled[...]).astype(BF)

    @pl.when(pl.program_id(0) == 0)
    def _():
        query_grad[...] = jnp.zeros_like(query_grad)

    query_grad[...] += matmul(score_grad, pair[:, :HD])


def attend_back(queries, pairs, weights, grads, scaled, dot, inverse):
    rows, keys = queries.shape[0], pairs.shape[0]
    whole = lambda i: (0, 0)
    return pl.pallas_call(
        attend_back_kernel,
        grid=(keys // ATTN_BLOCK,),
        in_specs=[
            pl.BlockSpec((rows, HD), whole),
            pl.BlockSpec((ATTN_BLOCK, 2 * HD), lambda i: (i, 0)),
            pl.BlockSpec((rows, ATTN_BLOCK), lambda i: (0, i)),
            pl.BlockSpec((rows, HD), whole),
            pl.BlockSpec((rows, HD), whole),
            pl.BlockSpec((rows, 1), whole),
            pl.BlockSpec((rows, 1), whole),
        ],
        out_specs=[
            pl.BlockSpec((ATTN_BLOCK, 2 * HD), lambda i: (i, 0)),
            pl.BlockSpec((rows, HD), whole),
        ],
        out_shape=[
            jax.ShapeDtypeStruct((keys, 2 * HD), BF),
            jax.ShapeDtypeStruct((rows, HD), F32),
        ],
        compiler_params=VMEM,
        name="attend_back",
    )(queries, pairs, weights, grads, scaled, dot, inverse)


def stack_kernel(*refs):
    start = 0
    for piece in refs[:-1]:
        refs[-1][start : start + piece.shape[0], :] = piece[...]
        start += piece.shape[0]


def stack_rows(pieces, tile=256):
    rows, columns = sum(piece.shape[0] for piece in pieces), pieces[0].shape[1]
    return pl.pallas_call(
        stack_kernel,
        grid=(columns // tile,),
        in_specs=[pl.BlockSpec((piece.shape[0], tile), lambda j: (0, j)) for piece in pieces],
        out_specs=pl.BlockSpec((rows, tile), lambda j: (0, j)),
        out_shape=jax.ShapeDtypeStruct((rows, columns), pieces[0].dtype),
        compiler_params=VMEM,
        name="stack_rows",
    )(*pieces)


UNIT_TILE = 256
GELU_IN = math.sqrt(2.0 / math.pi)
GELU_CUBE = 0.044715


def ffn_kernel(source, gate_w, up_w, down_w, gate, up, hidden, total):
    gate_pre = matmul(source[...], gate_w[...])
    up_pre = matmul(source[...], up_w[...])
    gate[...] = gate_pre
    up[...] = up_pre
    inner = GELU_IN * (gate_pre + GELU_CUBE * (gate_pre * gate_pre * gate_pre))
    low = (0.5 * gate_pre * (1.0 + jnp.tanh(inner)) * up_pre).astype(BF)
    hidden[...] = low

    @pl.when(pl.program_id(0) == 0)
    def _():
        total[...] = jnp.zeros_like(total)

    total[...] += inner_cols(low, down_w[...])


def ffn_back_kernel(grad, gate, up, gate_w, up_w, down_w, gate_grad, up_grad, total):
    hidden_grad = matmul(grad[...], down_w[...])
    gate_pre = gate[...]
    square = gate_pre * gate_pre
    bend = jnp.tanh(GELU_IN * (gate_pre + GELU_CUBE * (square * gate_pre)))
    rise = 0.5 * (1.0 + bend)
    slope = rise + 0.5 * gate_pre * (1.0 - bend * bend) * (GELU_IN * (1.0 + 3.0 * GELU_CUBE * square))
    gate_low = (hidden_grad * up[...] * slope).astype(BF)
    up_low = (hidden_grad * (gate_pre * rise)).astype(BF)
    gate_grad[...] = gate_low
    up_grad[...] = up_low

    @pl.when(pl.program_id(0) == 0)
    def _():
        total[...] = jnp.zeros_like(total)

    total[...] += inner_cols(gate_low, gate_w[...]) + inner_cols(up_low, up_w[...])


def unit_specs(rows, width, tiles):
    own = pl.BlockSpec((rows, UNIT_TILE), lambda j: (0, j))
    weights = [pl.BlockSpec((width, UNIT_TILE), lambda j, i=i: (0, j + i * tiles)) for i in (0, 1, 0)]
    return own, weights


def ffn_forward(source, gate_up_w, down_w):
    (rows, width), units = source.shape, down_w.shape[1]
    tiles = units // UNIT_TILE
    own, weights = unit_specs(rows, width, tiles)
    whole = pl.BlockSpec((rows, width), lambda j: (0, 0))
    return pl.pallas_call(
        ffn_kernel,
        grid=(tiles,),
        in_specs=[whole] + weights,
        out_specs=[own, own, own, whole],
        out_shape=[
            jax.ShapeDtypeStruct((rows, units), F32),
            jax.ShapeDtypeStruct((rows, units), F32),
            jax.ShapeDtypeStruct((rows, units), BF),
            jax.ShapeDtypeStruct((rows, width), F32),
        ],
        compiler_params=VMEM,
        name="ffn_forward",
    )(source, gate_up_w, gate_up_w, down_w)


def ffn_backward(grad, gate, up, gate_up_w, down_w):
    (rows, width), units = grad.shape, down_w.shape[1]
    tiles = units // UNIT_TILE
    own, weights = unit_specs(rows, width, tiles)
    whole = pl.BlockSpec((rows, width), lambda j: (0, 0))
    return pl.pallas_call(
        ffn_back_kernel,
        grid=(tiles,),
        in_specs=[whole, own, own] + weights,
        out_specs=[own, own, whole],
        out_shape=[
            jax.ShapeDtypeStruct((rows, units), BF),
            jax.ShapeDtypeStruct((rows, units), BF),
            jax.ShapeDtypeStruct((rows, width), F32),
        ],
        compiler_params=VMEM,
        name="ffn_backward",
    )(grad, gate, up, gate_up_w, gate_up_w, down_w)


def ffn_wgrad_kernel(steps, left, gate, up, hidden, out):
    rows = gate.shape[0]
    for i, (first, right) in enumerate([(0, gate), (0, up), (rows, hidden)]):

        @pl.when(pl.program_id(0) // steps == i)
        def _(first=first, right=right):
            out[...] = matmul(left[:, first : first + rows], right[...]).astype(BF)


def ffn_wgrad(left, gate, up, hidden):
    width, (rows, units) = left.shape[0], gate.shape
    steps = 2
    tile = units // steps

    def spec(i):
        return pl.BlockSpec((rows, tile), lambda j: (0, jnp.clip(j - i * steps, 0, steps - 1)))

    return pl.pallas_call(
        lambda *refs: ffn_wgrad_kernel(steps, *refs),
        grid=(3 * steps,),
        in_specs=[pl.BlockSpec(left.shape, lambda j: (0, 0)), spec(0), spec(1), spec(2)],
        out_specs=pl.BlockSpec((width, tile), lambda j: (0, j)),
        out_shape=jax.ShapeDtypeStruct((width, 3 * units), BF),
        compiler_params=VMEM,
        name="ffn_wgrad",
    )(left, gate, up, hidden)


def split_rows(values, parts):
    size = values.shape[0] // parts
    return [values[i * size : (i + 1) * size] for i in range(parts)]


def pick(core, first, second):
    return jnp.where(core == 0, first, second)


def shards(
    hidden_in,
    out_grad,
    block_order,
    norm_gains,
    head_gains,
    w_query,
    w_key,
    w_value,
    w_out,
    w_gate,
    w_up,
    w_down,
):
    tokens, width = hidden_in.shape
    y, z, x, core = (lax.axis_index(name) for name in CTX)
    other = 1 - core
    piece = width // 64
    units = w_gate.shape[1] // 2
    padded = (units + 127) // 128 * 128
    quarter = width // 4

    out_t, down_t = w_out.T, w_down.T

    def units_of(which):
        cut = [
            jnp.pad(lax.dynamic_slice_in_dim(w, which * units, units, 1), ((0, 0), (0, padded - units)))
            for w in (w_gate, w_up, down_t)
        ]
        return jnp.concatenate(cut, 1)

    def heads_of(which):
        cut = [lax.dynamic_slice_in_dim(w, which * HD, HD, 1) for w in (w_query, out_t)]
        return jnp.concatenate(cut + [w_key, w_value], 1)

    def chip_rows(of):
        mine, theirs = of(core), of(other)
        from_y, from_core, from_both = exchange((mine, theirs, theirs), "c")
        return pick(
            core,
            jnp.concatenate([mine, from_core, from_y, from_both], 0),
            jnp.concatenate([from_core, mine, from_both, from_y], 0),
        )

    head_rows = chip_rows(heads_of)
    ffn_rows = chip_rows(units_of)
    gate_up_w = lax.all_gather(ffn_rows[:, : 2 * padded], ("z", "x"), axis=0, tiled=True)
    head_w = stack_rows(gather_ring(after(gather_direct(head_rows, False), ffn_rows), True))
    hidden_in = after(hidden_in, head_rows)
    query_w, out_w = head_w[:, :HD], head_w[:, HD : 2 * HD]
    key_w, value_w, pair_w = head_w[:, 2 * HD : 3 * HD], head_w[:, 3 * HD :], head_w[:, 2 * HD :]

    place = jnp.arange(width, dtype=jnp.int32)
    first, second = place // quarter, place // (quarter // 4) % 4

    def natural(z_at, x_at):
        y_at = (y + place // (2 * piece)) % 2
        return y_at * (width // 2) + z_at * (8 * piece) + x_at * (2 * piece) + place % (2 * piece)

    by_gather = natural(first, second)
    by_ring = natural((z + pick(core, second, first)) % 4, (x + pick(core, first, second)) % 4)
    to_gather, to_ring = ((place[:, None] == by[None, :]).astype(BF) for by in (by_gather, by_ring))
    from_gather, from_ring = ((by[:, None] == place[None, :]).astype(BF) for by in (by_gather, by_ring))

    def reorder(values, moves):
        return matmul(values, moves).astype(BF)

    def both_cores(values):
        return jnp.concatenate([values, shift(values, "c")], 0)

    def sum_cores(partial, moves):
        low = reorder(partial.astype(BF), moves)
        return wide_sum(low[:tokens], shift(low[tokens:], "c")).astype(BF)

    def sum_parts(partial, moves):
        chip = sum_cores(partial, moves)
        return wide_sum(chip, shift(chip, "s"))

    offsets = jnp.arange(tokens, dtype=jnp.int32)

    def positions_of(places):
        return (block_order[places.reshape(-1)][:, None] * tokens + offsets[None, :]).reshape(-1)

    def device_of(y_at, z_at, x_at, core_at):
        return y_at * 32 + z_at * 8 + x_at * 2 + core_at

    steps = jnp.arange(4, dtype=jnp.int32)
    outer, inner = steps[:, None, None], steps[None, :, None]

    def keys_of(which):
        z_at, x_at = (z + pick(which, inner, outer)) % 4, (x + pick(which, outer, inner)) % 4
        return positions_of(device_of((y + steps[None, None, :2]) % 2, z_at, x_at, which))

    key_pos = [keys_of(core), keys_of(other)]
    own_pos = positions_of(device_of(y, z, x, core))
    chip_pos = jnp.concatenate([own_pos, positions_of(device_of(y, z, x, other))])
    cosine_table, sine_table = tables(chip_pos, HD)

    attn_val, pre_attn_back = jax.vjp(rms_scale, hidden_in, norm_gains[0])
    attn_chip = reorder(both_cores(attn_val.astype(BF)), to_ring)
    attn_ring = attn_chip[:tokens]
    key_pre = matmul(attn_ring, key_w)
    value_low = matmul(attn_ring, value_w).astype(BF)
    key_val, key_back = jax.vjp(
        lambda values, gain: rotate(rms_scale(values, gain), cosine_table[:tokens], sine_table[:tokens]),
        key_pre,
        head_gains[1],
    )
    key_low = key_val.astype(BF)
    pair_low = jnp.concatenate([key_low, value_low], 1)
    pair_pieces = gather_ring(gather_minor_y(pair_low), True)
    down_rows = after(ffn_rows[:, 2 * padded :], pair_pieces[1], pair_pieces[4])
    down_w = lax.all_gather(down_rows, ("z", "x"), axis=0, tiled=True)
    own_pairs = jnp.concatenate(pair_pieces, 0)
    pairs = [own_pairs, shift(own_pairs, "c")]

    query_pre = matmul(attn_chip, query_w)
    query_val, query_back = jax.vjp(
        lambda values, gain: rotate(rms_scale(values, gain), cosine_table, sine_table),
        query_pre,
        head_gains[0],
    )
    score_scale = HD ** (-0.5)
    queries = (query_val.astype(BF).astype(F32) * score_scale).astype(BF)
    parts = [attend(queries, pairs[part], key_pos[part], chip_pos) for part in range(2)]
    weights = [part[0] for part in parts]
    inverse_total = 1.0 / (parts[0][1] + parts[1][1])
    accum = parts[0][2] + parts[1][2]
    attn_rows = accum * inverse_total
    mixed_low = attn_rows.astype(BF)
    attn_out = sum_parts(inner_cols(mixed_low, out_w), from_ring)
    post_attn, post_attn_back = jax.vjp(rms_scale, attn_out, norm_gains[1])
    mid_state = hidden_in + post_attn

    ffn_val, ffn_norm_back = jax.vjp(rms_scale, mid_state, norm_gains[2])
    ffn_chip = both_cores(ffn_val.astype(BF))
    gate_pre, up_pre, hidden_low, ffn_part = ffn_forward(reorder(ffn_chip, to_gather), gate_up_w, down_w)
    ffn_out = sum_parts(ffn_part, from_gather)
    post_ffn, post_ffn_back = jax.vjp(rms_scale, ffn_out, norm_gains[3])
    block_out = mid_state + post_ffn

    ffn_grad, gain_four = post_ffn_back(out_grad)
    ffn_grad_chip = both_cores(ffn_grad.astype(BF))
    gate_low, up_low, ffn_norm_part = ffn_backward(reorder(ffn_grad_chip, to_gather), gate_pre, up_pre, gate_up_w, down_w)
    sources = jnp.concatenate([ffn_chip, ffn_grad_chip], 0)
    ffn_norm_chip = sum_cores(ffn_norm_part, from_gather)
    left = after(inner_cols(from_gather, sources).astype(BF), ffn_norm_chip)
    ffn_wgrads = ffn_wgrad(left, gate_low, up_low, hidden_low)
    ffn_sum = lax.psum_scatter(ffn_wgrads, ("z", "x"), scatter_dimension=0, tiled=True)
    ffn_norm_grad = after(wide_sum(ffn_norm_chip, shift(ffn_norm_chip, "s")), ffn_wgrads)
    mid_from, gain_three = ffn_norm_back(ffn_norm_grad)
    mid_grad = out_grad + mid_from

    def last_stage(values):
        parts = split_rows(values.astype(BF), 4)
        kept = [pick(core, parts[i], parts[i + 1]) for i in (0, 2)]
        sent = [pick(core, parts[i + 1], parts[i]) for i in (0, 2)]
        from_y, from_core, from_both = exchange((kept[1], sent[0], sent[1]), "c")
        return wide_sum(kept[0], from_y), wide_sum(from_core, from_both)

    attn_grad, gain_two = post_attn_back(mid_grad)
    attn_grad_chip = reorder(both_cores(attn_grad.astype(BF)), to_ring)
    rows_grad = matmul(attn_grad_chip, out_w).astype(BF)
    rows_wide = rows_grad.astype(F32)
    row_dot = jnp.sum(rows_wide * attn_rows, axis=1)[:, None]
    rows_scaled = (rows_wide * inverse_total).astype(BF)
    pair_far, query_far = attend_back(
        queries, pairs[1], weights[1], rows_grad, rows_scaled, row_dot, inverse_total
    )
    pair_near, query_near = attend_back(
        queries, pairs[0], weights[0], rows_grad, rows_scaled, row_dot, inverse_total
    )
    query_grad = query_far + query_near
    query_pre_grad, query_gain = query_back(query_grad * score_scale)
    query_gain = query_gain + shift(query_gain, "s")
    query_pre_low = query_pre_grad.astype(BF)
    early_grads = jnp.concatenate(
        [inner_rows(attn_chip, query_pre_low), inner_rows(attn_grad_chip, mixed_low)], 1
    ).astype(BF)
    pair_got = shift(pair_far, "c")
    chunks = [
        jnp.concatenate([wide_sum(near, got).astype(BF), early], 0)
        for near, got, early in zip(*(split_rows(part, 4) for part in (pair_near, pair_got, early_grads)))
    ]
    major_sum = reduce_chunks(*chunks, True).astype(BF)
    pair_chunks = split_rows(major_sum[: 8 * tokens], 4)
    early_chunks = split_rows(major_sum[8 * tokens :], 4)
    minor_sum = reduce_direct(
        [jnp.concatenate([pair, early], 0) for pair, early in zip(pair_chunks, early_chunks)], False
    )
    pair_own, pair_far_y = split_rows(minor_sum[: 2 * tokens].astype(BF), 2)
    from_y, from_shard, from_both = exchange((pair_far_y, pair_own, pair_far_y), "s")
    early_mine, early_got = last_stage(
        jnp.concatenate([after(ffn_sum, minor_sum).astype(F32), minor_sum[2 * tokens :]], 1)
    )
    pair_grad = after(wide_sum(pair_own, from_y) + wide_sum(from_shard, from_both), early_mine, early_got)
    attn_norm_sum = sum_parts(inner_cols(query_pre_low, query_w), from_ring)
    key_pre_grad, key_gain = key_back(pair_grad[:, :HD])
    key_pre_low = key_pre_grad.astype(BF)
    value_grad_low = pair_grad[:, HD:].astype(BF)
    pair_part = inner_cols(jnp.concatenate([key_pre_low, value_grad_low], 1), pair_w).astype(BF)

    kept, sent = pick(core, key_pre_low, value_grad_low), pick(core, value_grad_low, key_pre_low)
    pair_chip = jnp.concatenate([kept, shift(sent, "c")], 0)
    heads = [
        jnp.pad(gain.reshape(64, HD // 64), ((0, 0), (0, piece - HD // 64))).reshape(width)
        for gain in (query_gain, key_gain)
    ]
    gains = jnp.stack([gain_two, gain_three, gain_four] + heads, 1)
    gains = jnp.pad(gains, ((0, 0), (0, 128 - gains.shape[1]))).astype(BF)
    late_grads = jnp.concatenate([inner_rows(attn_chip, pair_chip), inner_rows(to_ring, gains)], 1).astype(BF)
    late_major = reduce_direct(split_rows(late_grads, 4), True).astype(BF)
    attn_norm_grad = attn_norm_sum + reorder(after(pair_part, late_major), from_ring).astype(F32)
    input_from, _ = pre_attn_back(attn_norm_grad)
    input_grad = mid_grad + input_from
    late_sum = reduce_direct(split_rows(late_major, 4), False)
    late_mine, late_got = last_stage(late_sum)

    def joined(start, size, mine, got):
        left, right = mine[:, start : start + size], got[:, start : start + size]
        return pick(core, jnp.concatenate([left, right], 1), jnp.concatenate([right, left], 1))

    gate_wgrad = joined(0, units, early_mine, early_got)
    up_wgrad = joined(padded, units, early_mine, early_got)
    down_wgrad = joined(2 * padded, units, early_mine, early_got).T

    query_wgrad = joined(3 * padded, HD, early_mine, early_got)
    out_wgrad = joined(3 * padded + HD, HD, early_mine, early_got).T
    pair_wgrad = joined(0, HD, late_mine, late_got)
    key_wgrad, value_wgrad = pair_wgrad[:, :HD], pair_wgrad[:, HD:]
    gain_sums = late_mine[:, HD:] + late_got[:, HD:]

    def along(weight, grad):
        return jnp.sum(weight.astype(F32) * grad, axis=1)

    query_part = along(w_query, query_wgrad)
    attn_part = query_part + shift(query_part, "s") + along(w_key, key_wgrad) + along(w_value, value_wgrad)
    own_gain = lax.dynamic_slice_in_dim(norm_gains[0], device_of(y, z, x, core) * piece, piece)
    gain_one = attn_part / own_gain
    return (
        block_out,
        input_grad,
        query_wgrad,
        key_wgrad,
        value_wgrad,
        out_wgrad,
        gate_wgrad,
        up_wgrad,
        down_wgrad,
        jnp.concatenate([gain_one[None, :], gain_sums[:, :3].T], 0),
        gain_sums[: HD // 64, 3:5].T,
    )


def solution(mesh):
    fine = Mesh(mesh.devices.reshape(2, 4, 4, 2, 2), ("y", "z", "x", "c", "s"))
    placed = (
        P(CTX, None),
        P(CTX, None),
        P(),
        P(),
        P(),
        P(CTX, "s"),
        P(CTX, None),
        P(CTX, None),
        P("s", CTX),
        P(CTX, "s"),
        P(CTX, "s"),
        P("s", CTX),
    )
    return jax.shard_map(
        shards,
        mesh=fine,
        in_specs=placed,
        out_specs=(
            P(CTX, None),
            P(CTX, None),
            P(CTX, "s"),
            P(CTX, None),
            P(CTX, None),
            P("s", CTX),
            P(CTX, "s"),
            P(CTX, "s"),
            P("s", CTX),
            P(None, CTX),
            P(None, CTX),
        ),
        check_vma=False,
    )
```

```python
import math

import jax
import jax.numpy as jnp
from jax import lax
from jax.experimental import pallas as pl
from jax.experimental.pallas import tpu as pltpu
from jax.sharding import Mesh, PartitionSpec as P

HD = 256
EPS = 1e-06
THETA = 1000000.0
BF = jnp.bfloat16
F32 = jnp.float32
CTX = ("y", "z", "x", "c")


def matmul(left, right):
    return jnp.dot(left, right, preferred_element_type=F32)


def inner_rows(left, right):
    return lax.dot_general(left, right, (((0,), (0,)), ((), ())), preferred_element_type=F32)


def inner_cols(left, right):
    return lax.dot_general(left, right, (((1,), (1,)), ((), ())), preferred_element_type=F32)


def rms_scale(values, gain):
    return values * lax.rsqrt(jnp.mean(values * values, axis=-1, keepdims=True) + EPS) * gain


def rotate(values, cosine_table, sine_table):
    half_width = values.shape[-1] // 2
    first = values[..., :half_width]
    second = values[..., half_width:]
    return jnp.concatenate(
        [first * cosine_table - second * sine_table, second * cosine_table + first * sine_table],
        axis=-1,
    )


def tables(positions, head_width):
    frequency = jnp.arange(head_width // 2, dtype=F32)
    inverse = jnp.exp(frequency * (-2.0 * math.log(THETA) / head_width))
    angles = positions.astype(F32)[:, None] * inverse[None, :]
    return (jnp.cos(angles), jnp.sin(angles))


def shift(values, axis, step=1):
    size = lax.axis_size(axis)
    return lax.ppermute(values, axis, [(i, (i + step) % size) for i in range(size)])


def ring(values, major, step, cross_y=False):
    moves = []
    for y in range(2):
        for z in range(4):
            for x in range(4):
                for core in range(2):
                    along_x = major == (core == 0)
                    to_z, to_x = (z, (x + step) % 4) if along_x else ((z + step) % 4, x)
                    to_y = 1 - y if cross_y else y
                    moves.append((y * 32 + z * 8 + x * 2 + core, to_y * 32 + to_z * 8 + to_x * 2 + core))
    return lax.ppermute(values, CTX, moves)


def gather_direct(block, major):
    return jnp.concatenate([block] + [ring(block, major, -k) for k in (1, 2, 3)], 0)


def gather_minor_y(block):
    blocks = [block if k == 0 else ring(block, False, -k) for k in range(4)]
    others = [ring(block, False, -k, True) for k in range(4)]
    return jnp.concatenate([part for pair in zip(blocks, others) for part in pair], 0)


def exchange(values, axis):
    both = [(i, 3 - i) for i in range(4)]
    return shift(values[0], "y"), shift(values[1], axis), lax.ppermute(values[2], ("y", axis), both)


def after(value, *others):
    return lax.optimization_barrier((value, *others))[0]


def gather_ring(block, major):
    half = (block.shape[0] // 2 + 7) // 8 * 8
    previous, following = ring(block, major, 1), ring(block, major, -1)
    far_low = ring(previous[:half], major, 1)
    far_high = ring(following[half:], major, -1)
    return [block, following, far_low, far_high, previous]


def wide_sum(*parts):
    return sum(part.astype(F32) for part in parts)


def reduce_direct(chunks, major):
    return wide_sum(chunks[0], *[ring(chunks[k], major, k) for k in (1, 2, 3)])


def reduce_first(far_low, far_high, major):
    return ring(far_low, major, 1), ring(far_high, major, -1)


def reduce_second(own, following, previous, from_previous, from_next, major):
    half = from_previous.shape[0]
    forward = jnp.concatenate(
        [wide_sum(following[:half], from_previous).astype(BF), following[half:]], 0
    )
    backward = jnp.concatenate(
        [previous[:half], wide_sum(previous[half:], from_next).astype(BF)], 0
    )
    return wide_sum(own, ring(forward, major, 1), ring(backward, major, -1))


def reduce_chunks(own, following, far, previous, major):
    half = (far.shape[0] // 2 + 7) // 8 * 8
    return reduce_second(own, following, previous, *reduce_first(far[:half], far[half:], major), major)


ATTN_BLOCK = 1024
VMEM = pltpu.CompilerParams(vmem_limit_bytes=48 * 1024 * 1024)


def attend_kernel(query, pair, key_pos, query_pos, weight, total, accum):
    scores = inner_cols(query[...], pair[:, :HD])
    exps = jnp.where(query_pos[...] >= key_pos[...], jnp.exp(scores), 0.0)
    low = exps.astype(BF)
    weight[...] = low

    @pl.when(pl.program_id(0) == 0)
    def _():
        total[...] = jnp.zeros_like(total)
        accum[...] = jnp.zeros_like(accum)

    total[...] += jnp.sum(exps, axis=1, keepdims=True)
    accum[...] += matmul(low, pair[:, HD:])


def attend(queries, pairs, key_pos, query_pos):
    rows, keys = queries.shape[0], pairs.shape[0]
    whole = lambda i: (0, 0)
    return pl.pallas_call(
        attend_kernel,
        grid=(keys // ATTN_BLOCK,),
        in_specs=[
            pl.BlockSpec((rows, HD), whole),
            pl.BlockSpec((ATTN_BLOCK, 2 * HD), lambda i: (i, 0)),
            pl.BlockSpec((1, ATTN_BLOCK), lambda i: (0, i)),
            pl.BlockSpec((rows, 1), whole),
        ],
        out_specs=[
            pl.BlockSpec((rows, ATTN_BLOCK), lambda i: (0, i)),
            pl.BlockSpec((rows, 1), whole),
            pl.BlockSpec((rows, HD), whole),
        ],
        out_shape=[
            jax.ShapeDtypeStruct((rows, keys), BF),
            jax.ShapeDtypeStruct((rows, 1), F32),
            jax.ShapeDtypeStruct((rows, HD), F32),
        ],
        compiler_params=VMEM,
        name="attend",
    )(queries, pairs, key_pos[None, :], query_pos[:, None])


def attend_back_kernel(query, pair, weight, grad, scaled, dot, inverse, pair_grad, query_grad):
    weights = weight[...]
    prob_grad = inner_cols(grad[...], pair[:, HD:])
    score_grad = (weights.astype(F32) * ((prob_grad - dot[...]) * inverse[...])).astype(BF)
    pair_grad[:, :HD] = inner_rows(score_grad, query[...]).astype(BF)
    pair_grad[:, HD:] = inner_rows(weights, scaled[...]).astype(BF)

    @pl.when(pl.program_id(0) == 0)
    def _():
        query_grad[...] = jnp.zeros_like(query_grad)

    query_grad[...] += matmul(score_grad, pair[:, :HD])


def attend_back(queries, pairs, weights, grads, scaled, dot, inverse):
    rows, keys = queries.shape[0], pairs.shape[0]
    whole = lambda i: (0, 0)
    return pl.pallas_call(
        attend_back_kernel,
        grid=(keys // ATTN_BLOCK,),
        in_specs=[
            pl.BlockSpec((rows, HD), whole),
            pl.BlockSpec((ATTN_BLOCK, 2 * HD), lambda i: (i, 0)),
            pl.BlockSpec((rows, ATTN_BLOCK), lambda i: (0, i)),
            pl.BlockSpec((rows, HD), whole),
            pl.BlockSpec((rows, HD), whole),
            pl.BlockSpec((rows, 1), whole),
            pl.BlockSpec((rows, 1), whole),
        ],
        out_specs=[
            pl.BlockSpec((ATTN_BLOCK, 2 * HD), lambda i: (i, 0)),
            pl.BlockSpec((rows, HD), whole),
        ],
        out_shape=[
            jax.ShapeDtypeStruct((keys, 2 * HD), BF),
            jax.ShapeDtypeStruct((rows, HD), F32),
        ],
        compiler_params=VMEM,
        name="attend_back",
    )(queries, pairs, weights, grads, scaled, dot, inverse)


def stack_kernel(*refs):
    start = 0
    for piece in refs[:-1]:
        refs[-1][start : start + piece.shape[0], :] = piece[...]
        start += piece.shape[0]


def stack_rows(pieces, tile=256):
    rows, columns = sum(piece.shape[0] for piece in pieces), pieces[0].shape[1]
    return pl.pallas_call(
        stack_kernel,
        grid=(columns // tile,),
        in_specs=[pl.BlockSpec((piece.shape[0], tile), lambda j: (0, j)) for piece in pieces],
        out_specs=pl.BlockSpec((rows, tile), lambda j: (0, j)),
        out_shape=jax.ShapeDtypeStruct((rows, columns), pieces[0].dtype),
        compiler_params=VMEM,
        name="stack_rows",
    )(*pieces)


UNIT_TILE = 256
GELU_IN = math.sqrt(2.0 / math.pi)
GELU_CUBE = 0.044715


def ffn_kernel(source, gate_w, up_w, down_w, gate, up, hidden, total):
    gate_pre = matmul(source[...], gate_w[...])
    up_pre = matmul(source[...], up_w[...])
    gate[...] = gate_pre
    up[...] = up_pre
    inner = GELU_IN * (gate_pre + GELU_CUBE * (gate_pre * gate_pre * gate_pre))
    low = (0.5 * gate_pre * (1.0 + jnp.tanh(inner)) * up_pre).astype(BF)
    hidden[...] = low

    @pl.when(pl.program_id(0) == 0)
    def _():
        total[...] = jnp.zeros_like(total)

    total[...] += inner_cols(low, down_w[...])


def ffn_back_kernel(grad, gate, up, gate_w, up_w, down_w, gate_grad, up_grad, total):
    hidden_grad = matmul(grad[...], down_w[...])
    gate_pre = gate[...]
    square = gate_pre * gate_pre
    bend = jnp.tanh(GELU_IN * (gate_pre + GELU_CUBE * (square * gate_pre)))
    rise = 0.5 * (1.0 + bend)
    slope = rise + 0.5 * gate_pre * (1.0 - bend * bend) * (GELU_IN * (1.0 + 3.0 * GELU_CUBE * square))
    gate_low = (hidden_grad * up[...] * slope).astype(BF)
    up_low = (hidden_grad * (gate_pre * rise)).astype(BF)
    gate_grad[...] = gate_low
    up_grad[...] = up_low

    @pl.when(pl.program_id(0) == 0)
    def _():
        total[...] = jnp.zeros_like(total)

    total[...] += inner_cols(gate_low, gate_w[...]) + inner_cols(up_low, up_w[...])


def unit_specs(rows, width, tiles):
    own = pl.BlockSpec((rows, UNIT_TILE), lambda j: (0, j))
    weights = [pl.BlockSpec((width, UNIT_TILE), lambda j, i=i: (0, j + i * tiles)) for i in (0, 1, 0)]
    return own, weights


def ffn_forward(source, gate_up_w, down_w):
    (rows, width), units = source.shape, down_w.shape[1]
    tiles = units // UNIT_TILE
    own, weights = unit_specs(rows, width, tiles)
    whole = pl.BlockSpec((rows, width), lambda j: (0, 0))
    return pl.pallas_call(
        ffn_kernel,
        grid=(tiles,),
        in_specs=[whole] + weights,
        out_specs=[own, own, own, whole],
        out_shape=[
            jax.ShapeDtypeStruct((rows, units), F32),
            jax.ShapeDtypeStruct((rows, units), F32),
            jax.ShapeDtypeStruct((rows, units), BF),
            jax.ShapeDtypeStruct((rows, width), F32),
        ],
        compiler_params=VMEM,
        name="ffn_forward",
    )(source, gate_up_w, gate_up_w, down_w)


def ffn_backward(grad, gate, up, gate_up_w, down_w):
    (rows, width), units = grad.shape, down_w.shape[1]
    tiles = units // UNIT_TILE
    own, weights = unit_specs(rows, width, tiles)
    whole = pl.BlockSpec((rows, width), lambda j: (0, 0))
    return pl.pallas_call(
        ffn_back_kernel,
        grid=(tiles,),
        in_specs=[whole, own, own] + weights,
        out_specs=[own, own, whole],
        out_shape=[
            jax.ShapeDtypeStruct((rows, units), BF),
            jax.ShapeDtypeStruct((rows, units), BF),
            jax.ShapeDtypeStruct((rows, width), F32),
        ],
        compiler_params=VMEM,
        name="ffn_backward",
    )(grad, gate, up, gate_up_w, gate_up_w, down_w)


def ffn_wgrad_kernel(steps, left, gate, up, hidden, out):
    rows = gate.shape[0]
    for i, (first, right) in enumerate([(0, gate), (0, up), (rows, hidden)]):

        @pl.when(pl.program_id(0) // steps == i)
        def _(first=first, right=right):
            out[...] = matmul(left[:, first : first + rows], right[...]).astype(BF)


def ffn_wgrad(left, gate, up, hidden):
    width, (rows, units) = left.shape[0], gate.shape
    steps = 2
    tile = units // steps

    def spec(i):
        return pl.BlockSpec((rows, tile), lambda j: (0, jnp.clip(j - i * steps, 0, steps - 1)))

    return pl.pallas_call(
        lambda *refs: ffn_wgrad_kernel(steps, *refs),
        grid=(3 * steps,),
        in_specs=[pl.BlockSpec(left.shape, lambda j: (0, 0)), spec(0), spec(1), spec(2)],
        out_specs=pl.BlockSpec((width, tile), lambda j: (0, j)),
        out_shape=jax.ShapeDtypeStruct((width, 3 * units), BF),
        compiler_params=VMEM,
        name="ffn_wgrad",
    )(left, gate, up, hidden)


def split_rows(values, parts):
    size = values.shape[0] // parts
    return [values[i * size : (i + 1) * size] for i in range(parts)]


def pick(core, first, second):
    return jnp.where(core == 0, first, second)


def shards(
    hidden_in,
    out_grad,
    block_order,
    norm_gains,
    head_gains,
    w_query,
    w_key,
    w_value,
    w_out,
    w_gate,
    w_up,
    w_down,
):
    tokens, width = hidden_in.shape
    y, z, x, core = (lax.axis_index(name) for name in CTX)
    other = 1 - core
    piece = width // 64
    units = w_gate.shape[1] // 2
    padded = (units + 127) // 128 * 128
    quarter = width // 4

    out_t, down_t = w_out.T, w_down.T

    def units_of(which):
        cut = [
            jnp.pad(lax.dynamic_slice_in_dim(w, which * units, units, 1), ((0, 0), (0, padded - units)))
            for w in (w_gate, w_up, down_t)
        ]
        return jnp.concatenate(cut, 1)

    def heads_of(which):
        cut = [lax.dynamic_slice_in_dim(w, which * HD, HD, 1) for w in (w_query, out_t)]
        return jnp.concatenate(cut + [w_key, w_value], 1)

    def chip_rows(of):
        mine, theirs = of(core), of(other)
        from_y, from_core, from_both = exchange((mine, theirs, theirs), "c")
        return pick(
            core,
            jnp.concatenate([mine, from_core, from_y, from_both], 0),
            jnp.concatenate([from_core, mine, from_both, from_y], 0),
        )

    head_rows = chip_rows(heads_of)
    ffn_rows = chip_rows(units_of)
    gate_up_w = lax.all_gather(ffn_rows[:, : 2 * padded], ("z", "x"), axis=0, tiled=True)
    down_rows = after(ffn_rows[:, 2 * padded :], gate_up_w)
    down_w = lax.all_gather(down_rows, ("z", "x"), axis=0, tiled=True)
    head_w = stack_rows(gather_ring(after(gather_direct(head_rows, False), ffn_rows), True))
    hidden_in = after(hidden_in, head_rows)
    query_w, out_w = head_w[:, :HD], head_w[:, HD : 2 * HD]
    key_w, value_w, pair_w = head_w[:, 2 * HD : 3 * HD], head_w[:, 3 * HD :], head_w[:, 2 * HD :]

    place = jnp.arange(width, dtype=jnp.int32)
    first, second = place // quarter, place // (quarter // 4) % 4

    def natural(z_at, x_at):
        y_at = (y + place // (2 * piece)) % 2
        return y_at * (width // 2) + z_at * (8 * piece) + x_at * (2 * piece) + place % (2 * piece)

    by_gather = natural(first, second)
    by_ring = natural((z + pick(core, second, first)) % 4, (x + pick(core, first, second)) % 4)
    to_gather, to_ring = ((place[:, None] == by[None, :]).astype(BF) for by in (by_gather, by_ring))
    from_gather, from_ring = ((by[:, None] == place[None, :]).astype(BF) for by in (by_gather, by_ring))

    def reorder(values, moves):
        return matmul(values, moves).astype(BF)

    def both_cores(values):
        return jnp.concatenate([values, shift(values, "c")], 0)

    def sum_cores(partial, moves):
        low = reorder(partial.astype(BF), moves)
        return wide_sum(low[:tokens], shift(low[tokens:], "c")).astype(BF)

    def sum_parts(partial, moves):
        chip = sum_cores(partial, moves)
        return wide_sum(chip, shift(chip, "s"))

    offsets = jnp.arange(tokens, dtype=jnp.int32)

    def positions_of(places):
        return (block_order[places.reshape(-1)][:, None] * tokens + offsets[None, :]).reshape(-1)

    def device_of(y_at, z_at, x_at, core_at):
        return y_at * 32 + z_at * 8 + x_at * 2 + core_at

    steps = jnp.arange(4, dtype=jnp.int32)
    outer, inner = steps[:, None, None], steps[None, :, None]

    def keys_of(which):
        z_at, x_at = (z + pick(which, inner, outer)) % 4, (x + pick(which, outer, inner)) % 4
        return positions_of(device_of((y + steps[None, None, :2]) % 2, z_at, x_at, which))

    key_pos = [keys_of(core), keys_of(other)]
    own_pos = positions_of(device_of(y, z, x, core))
    chip_pos = jnp.concatenate([own_pos, positions_of(device_of(y, z, x, other))])
    cosine_table, sine_table = tables(chip_pos, HD)

    attn_val, pre_attn_back = jax.vjp(rms_scale, hidden_in, norm_gains[0])
    attn_chip = reorder(both_cores(attn_val.astype(BF)), to_ring)
    attn_ring = attn_chip[:tokens]
    key_pre = matmul(attn_ring, key_w)
    value_low = matmul(attn_ring, value_w).astype(BF)
    key_val, key_back = jax.vjp(
        lambda values, gain: rotate(rms_scale(values, gain), cosine_table[:tokens], sine_table[:tokens]),
        key_pre,
        head_gains[1],
    )
    key_low = key_val.astype(BF)
    pair_low = jnp.concatenate([key_low, value_low], 1)
    pair_pieces = gather_ring(gather_minor_y(pair_low), True)
    own_pairs = jnp.concatenate(pair_pieces, 0)
    pairs = [own_pairs, shift(own_pairs, "c")]

    query_pre = matmul(attn_chip, query_w)
    query_val, query_back = jax.vjp(
        lambda values, gain: rotate(rms_scale(values, gain), cosine_table, sine_table),
        query_pre,
        head_gains[0],
    )
    score_scale = HD ** (-0.5)
    queries = (query_val.astype(BF).astype(F32) * score_scale).astype(BF)
    parts = [attend(queries, pairs[part], key_pos[part], chip_pos) for part in range(2)]
    weights = [part[0] for part in parts]
    inverse_total = 1.0 / (parts[0][1] + parts[1][1])
    accum = parts[0][2] + parts[1][2]
    attn_rows = accum * inverse_total
    mixed_low = attn_rows.astype(BF)
    attn_out = sum_parts(inner_cols(mixed_low, out_w), from_ring)
    post_attn, post_attn_back = jax.vjp(rms_scale, attn_out, norm_gains[1])
    mid_state = hidden_in + post_attn

    ffn_val, ffn_norm_back = jax.vjp(rms_scale, mid_state, norm_gains[2])
    ffn_chip = both_cores(ffn_val.astype(BF))
    gate_pre, up_pre, hidden_low, ffn_part = ffn_forward(reorder(ffn_chip, to_gather), gate_up_w, down_w)
    ffn_out = sum_parts(ffn_part, from_gather)
    post_ffn, post_ffn_back = jax.vjp(rms_scale, ffn_out, norm_gains[3])
    block_out = mid_state + post_ffn

    ffn_grad, gain_four = post_ffn_back(out_grad)
    ffn_grad_chip = both_cores(ffn_grad.astype(BF))
    gate_low, up_low, ffn_norm_part = ffn_backward(reorder(ffn_grad_chip, to_gather), gate_pre, up_pre, gate_up_w, down_w)
    sources = jnp.concatenate([ffn_chip, ffn_grad_chip], 0)
    ffn_norm_chip = sum_cores(ffn_norm_part, from_gather)
    left = after(inner_cols(from_gather, sources).astype(BF), ffn_norm_chip)
    ffn_wgrads = ffn_wgrad(left, gate_low, up_low, hidden_low)
    ffn_sum = lax.psum_scatter(ffn_wgrads, ("z", "x"), scatter_dimension=0, tiled=True)
    ffn_norm_grad = after(wide_sum(ffn_norm_chip, shift(ffn_norm_chip, "s")), ffn_wgrads)
    mid_from, gain_three = ffn_norm_back(ffn_norm_grad)
    mid_grad = out_grad + mid_from

    def last_stage(values):
        parts = split_rows(values.astype(BF), 4)
        kept = [pick(core, parts[i], parts[i + 1]) for i in (0, 2)]
        sent = [pick(core, parts[i + 1], parts[i]) for i in (0, 2)]
        from_y, from_core, from_both = exchange((kept[1], sent[0], sent[1]), "c")
        return wide_sum(kept[0], from_y), wide_sum(from_core, from_both)

    attn_grad, gain_two = post_attn_back(mid_grad)
    attn_grad_chip = reorder(both_cores(attn_grad.astype(BF)), to_ring)
    rows_grad = matmul(attn_grad_chip, out_w).astype(BF)
    rows_wide = rows_grad.astype(F32)
    row_dot = jnp.sum(rows_wide * attn_rows, axis=1)[:, None]
    rows_scaled = (rows_wide * inverse_total).astype(BF)
    pair_far, query_far = attend_back(
        queries, pairs[1], weights[1], rows_grad, rows_scaled, row_dot, inverse_total
    )
    pair_near, query_near = attend_back(
        queries, pairs[0], weights[0], rows_grad, rows_scaled, row_dot, inverse_total
    )
    query_grad = query_far + query_near
    query_pre_grad, query_gain = query_back(query_grad * score_scale)
    query_gain = query_gain + shift(query_gain, "s")
    query_pre_low = query_pre_grad.astype(BF)
    early_grads = jnp.concatenate(
        [inner_rows(attn_chip, query_pre_low), inner_rows(attn_grad_chip, mixed_low)], 1
    ).astype(BF)
    pair_got = shift(pair_far, "c")
    chunks = [
        jnp.concatenate([wide_sum(near, got).astype(BF), early], 0)
        for near, got, early in zip(*(split_rows(part, 4) for part in (pair_near, pair_got, early_grads)))
    ]
    major_sum = reduce_chunks(*chunks, True).astype(BF)
    pair_chunks = split_rows(major_sum[: 8 * tokens], 4)
    early_chunks = split_rows(major_sum[8 * tokens :], 4)
    minor_sum = reduce_direct(
        [jnp.concatenate([pair, early], 0) for pair, early in zip(pair_chunks, early_chunks)], False
    )
    pair_own, pair_far_y = split_rows(minor_sum[: 2 * tokens].astype(BF), 2)
    from_y, from_shard, from_both = exchange((pair_far_y, pair_own, pair_far_y), "s")
    pair_grad = wide_sum(pair_own, from_y) + wide_sum(from_shard, from_both)
    attn_norm_sum = sum_parts(inner_cols(query_pre_low, query_w), from_ring)
    key_pre_grad, key_gain = key_back(pair_grad[:, :HD])
    key_pre_low = key_pre_grad.astype(BF)
    value_grad_low = pair_grad[:, HD:].astype(BF)
    pair_part = inner_cols(jnp.concatenate([key_pre_low, value_grad_low], 1), pair_w).astype(BF)

    kept, sent = pick(core, key_pre_low, value_grad_low), pick(core, value_grad_low, key_pre_low)
    pair_chip = jnp.concatenate([kept, shift(sent, "c")], 0)
    spare = jnp.zeros((8, width), F32)
    norm_rows = jnp.concatenate([gain_two[None], gain_three[None], gain_four[None], spare[:5]], 0)
    head_rows = jnp.concatenate(
        [spare[:3, :HD], query_gain[None], key_gain[None], spare[:3, :HD]], 0
    )
    share = HD // 64
    at_piece, in_piece = by_ring // piece, by_ring % piece
    head_at = jnp.where(in_piece < share, at_piece * share + in_piece, -1)
    head_moves = (head_at[:, None] == jnp.arange(HD, dtype=jnp.int32)[None, :]).astype(BF)
    gains = inner_cols(from_ring, norm_rows.astype(BF)) + inner_cols(head_moves, head_rows.astype(BF))
    gains = jnp.pad(gains, ((0, 0), (0, 120)))
    late_grads = jnp.concatenate([inner_rows(attn_chip, pair_chip), gains], 1).astype(BF)
    late_major = reduce_direct(split_rows(late_grads, 4), True).astype(BF)
    attn_norm_grad = attn_norm_sum + reorder(after(pair_part, late_major), from_ring).astype(F32)
    input_from, _ = pre_attn_back(attn_norm_grad)
    input_grad = mid_grad + input_from
    late_sum = reduce_direct(split_rows(late_major, 4), False)
    early_mine, early_got = last_stage(
        jnp.concatenate([after(ffn_sum, minor_sum).astype(F32), minor_sum[2 * tokens :]], 1)
    )
    late_mine, late_got = last_stage(after(late_sum, early_mine, early_got))

    def joined(start, size, mine, got):
        left, right = mine[:, start : start + size], got[:, start : start + size]
        return pick(core, jnp.concatenate([left, right], 1), jnp.concatenate([right, left], 1))

    gate_wgrad = joined(0, units, early_mine, early_got)
    up_wgrad = joined(padded, units, early_mine, early_got)
    down_wgrad = joined(2 * padded, units, early_mine, early_got).T

    query_wgrad = joined(3 * padded, HD, early_mine, early_got)
    out_wgrad = joined(3 * padded + HD, HD, early_mine, early_got).T
    pair_wgrad = joined(0, HD, late_mine, late_got)
    key_wgrad, value_wgrad = pair_wgrad[:, :HD], pair_wgrad[:, HD:]
    gain_sums = late_mine[:, HD:] + late_got[:, HD:]

    def along(weight, grad):
        return jnp.sum(weight.astype(F32) * grad, axis=1)

    query_part = along(w_query, query_wgrad)
    attn_part = query_part + shift(query_part, "s") + along(w_key, key_wgrad) + along(w_value, value_wgrad)
    own_gain = lax.dynamic_slice_in_dim(norm_gains[0], device_of(y, z, x, core) * piece, piece)
    gain_one = attn_part / own_gain
    return (
        block_out,
        input_grad,
        query_wgrad,
        key_wgrad,
        value_wgrad,
        out_wgrad,
        gate_wgrad,
        up_wgrad,
        down_wgrad,
        jnp.concatenate([gain_one[None, :], gain_sums[:, :3].T], 0),
        gain_sums[: HD // 64, 3:5].T,
    )


def solution(mesh):
    fine = Mesh(mesh.devices.reshape(2, 4, 4, 2, 2), ("y", "z", "x", "c", "s"))
    placed = (
        P(CTX, None),
        P(CTX, None),
        P(),
        P(),
        P(),
        P(CTX, "s"),
        P(CTX, None),
        P(CTX, None),
        P("s", CTX),
        P(CTX, "s"),
        P(CTX, "s"),
        P("s", CTX),
    )
    return jax.shard_map(
        shards,
        mesh=fine,
        in_specs=placed,
        out_specs=(
            P(CTX, None),
            P(CTX, None),
            P(CTX, "s"),
            P(CTX, None),
            P(CTX, None),
            P("s", CTX),
            P(CTX, "s"),
            P(CTX, "s"),
            P("s", CTX),
            P(None, CTX),
            P(None, CTX),
        ),
        check_vma=False,
    )
```

```python
import math

import jax
import jax.numpy as jnp
from jax import lax
from jax.experimental import pallas as pl
from jax.experimental.pallas import tpu as pltpu
from jax.sharding import Mesh, PartitionSpec as P

HD = 256
EPS = 1e-06
THETA = 1000000.0
BF = jnp.bfloat16
F32 = jnp.float32
CTX = ("y", "z", "x", "c")


def matmul(left, right):
    return jnp.dot(left, right, preferred_element_type=F32)


def inner_rows(left, right):
    return lax.dot_general(left, right, (((0,), (0,)), ((), ())), preferred_element_type=F32)


def inner_cols(left, right):
    return lax.dot_general(left, right, (((1,), (1,)), ((), ())), preferred_element_type=F32)


def rms_scale(values, gain):
    return values * lax.rsqrt(jnp.mean(values * values, axis=-1, keepdims=True) + EPS) * gain


def rotate(values, cosine_table, sine_table):
    half_width = values.shape[-1] // 2
    first = values[..., :half_width]
    second = values[..., half_width:]
    return jnp.concatenate(
        [first * cosine_table - second * sine_table, second * cosine_table + first * sine_table],
        axis=-1,
    )


def tables(positions, head_width):
    frequency = jnp.arange(head_width // 2, dtype=F32)
    inverse = jnp.exp(frequency * (-2.0 * math.log(THETA) / head_width))
    angles = positions.astype(F32)[:, None] * inverse[None, :]
    return (jnp.cos(angles), jnp.sin(angles))


def shift(values, axis, step=1):
    size = lax.axis_size(axis)
    return lax.ppermute(values, axis, [(i, (i + step) % size) for i in range(size)])


def ring(values, major, step, cross_y=False):
    moves = []
    for y in range(2):
        for z in range(4):
            for x in range(4):
                for core in range(2):
                    along_x = major == (core == 0)
                    to_z, to_x = (z, (x + step) % 4) if along_x else ((z + step) % 4, x)
                    to_y = 1 - y if cross_y else y
                    moves.append((y * 32 + z * 8 + x * 2 + core, to_y * 32 + to_z * 8 + to_x * 2 + core))
    return lax.ppermute(values, CTX, moves)


def gather_direct(block, major):
    return jnp.concatenate([block] + [ring(block, major, -k) for k in (1, 2, 3)], 0)


def gather_minor_y(block):
    blocks = [block if k == 0 else ring(block, False, -k) for k in range(4)]
    others = [ring(block, False, -k, True) for k in range(4)]
    return jnp.concatenate([part for pair in zip(blocks, others) for part in pair], 0)


def exchange(values, axis):
    both = [(i, 3 - i) for i in range(4)]
    return shift(values[0], "y"), shift(values[1], axis), lax.ppermute(values[2], ("y", axis), both)


def after(value, *others):
    return lax.optimization_barrier((value, *others))[0]


def gather_ring(block, major):
    half = (block.shape[0] // 2 + 7) // 8 * 8
    previous, following = ring(block, major, 1), ring(block, major, -1)
    far_low = ring(previous[:half], major, 1)
    far_high = ring(following[half:], major, -1)
    return [block, following, far_low, far_high, previous]


def wide_sum(*parts):
    return sum(part.astype(F32) for part in parts)


def reduce_direct(chunks, major):
    return wide_sum(chunks[0], *[ring(chunks[k], major, k) for k in (1, 2, 3)])


def reduce_first(far_low, far_high, major):
    return ring(far_low, major, 1), ring(far_high, major, -1)


def reduce_second(own, following, previous, from_previous, from_next, major):
    half = from_previous.shape[0]
    forward = jnp.concatenate(
        [wide_sum(following[:half], from_previous).astype(BF), following[half:]], 0
    )
    backward = jnp.concatenate(
        [previous[:half], wide_sum(previous[half:], from_next).astype(BF)], 0
    )
    return wide_sum(own, ring(forward, major, 1), ring(backward, major, -1))


def reduce_chunks(own, following, far, previous, major):
    half = (far.shape[0] // 2 + 7) // 8 * 8
    return reduce_second(own, following, previous, *reduce_first(far[:half], far[half:], major), major)


ATTN_BLOCK = 1024
VMEM = pltpu.CompilerParams(vmem_limit_bytes=48 * 1024 * 1024)


def attend_kernel(query, pair, key_pos, query_pos, weight, total, accum):
    scores = inner_cols(query[...], pair[:, :HD])
    exps = jnp.where(query_pos[...] >= key_pos[...], jnp.exp(scores), 0.0)
    low = exps.astype(BF)
    weight[...] = low

    @pl.when(pl.program_id(0) == 0)
    def _():
        total[...] = jnp.zeros_like(total)
        accum[...] = jnp.zeros_like(accum)

    total[...] += jnp.sum(exps, axis=1, keepdims=True)
    accum[...] += matmul(low, pair[:, HD:])


def attend(queries, pairs, key_pos, query_pos):
    rows, keys = queries.shape[0], pairs.shape[0]
    whole = lambda i: (0, 0)
    return pl.pallas_call(
        attend_kernel,
        grid=(keys // ATTN_BLOCK,),
        in_specs=[
            pl.BlockSpec((rows, HD), whole),
            pl.BlockSpec((ATTN_BLOCK, 2 * HD), lambda i: (i, 0)),
            pl.BlockSpec((1, ATTN_BLOCK), lambda i: (0, i)),
            pl.BlockSpec((rows, 1), whole),
        ],
        out_specs=[
            pl.BlockSpec((rows, ATTN_BLOCK), lambda i: (0, i)),
            pl.BlockSpec((rows, 1), whole),
            pl.BlockSpec((rows, HD), whole),
        ],
        out_shape=[
            jax.ShapeDtypeStruct((rows, keys), BF),
            jax.ShapeDtypeStruct((rows, 1), F32),
            jax.ShapeDtypeStruct((rows, HD), F32),
        ],
        compiler_params=VMEM,
        name="attend",
    )(queries, pairs, key_pos[None, :], query_pos[:, None])


def attend_back_kernel(query, pair, weight, grad, scaled, dot, inverse, pair_grad, query_grad):
    weights = weight[...]
    prob_grad = inner_cols(grad[...], pair[:, HD:])
    score_grad = (weights.astype(F32) * ((prob_grad - dot[...]) * inverse[...])).astype(BF)
    pair_grad[:, :HD] = inner_rows(score_grad, query[...]).astype(BF)
    pair_grad[:, HD:] = inner_rows(weights, scaled[...]).astype(BF)

    @pl.when(pl.program_id(0) == 0)
    def _():
        query_grad[...] = jnp.zeros_like(query_grad)

    query_grad[...] += matmul(score_grad, pair[:, :HD])


def attend_back(queries, pairs, weights, grads, scaled, dot, inverse):
    rows, keys = queries.shape[0], pairs.shape[0]
    whole = lambda i: (0, 0)
    return pl.pallas_call(
        attend_back_kernel,
        grid=(keys // ATTN_BLOCK,),
        in_specs=[
            pl.BlockSpec((rows, HD), whole),
            pl.BlockSpec((ATTN_BLOCK, 2 * HD), lambda i: (i, 0)),
            pl.BlockSpec((rows, ATTN_BLOCK), lambda i: (0, i)),
            pl.BlockSpec((rows, HD), whole),
            pl.BlockSpec((rows, HD), whole),
            pl.BlockSpec((rows, 1), whole),
            pl.BlockSpec((rows, 1), whole),
        ],
        out_specs=[
            pl.BlockSpec((ATTN_BLOCK, 2 * HD), lambda i: (i, 0)),
            pl.BlockSpec((rows, HD), whole),
        ],
        out_shape=[
            jax.ShapeDtypeStruct((keys, 2 * HD), BF),
            jax.ShapeDtypeStruct((rows, HD), F32),
        ],
        compiler_params=VMEM,
        name="attend_back",
    )(queries, pairs, weights, grads, scaled, dot, inverse)


def stack_kernel(*refs):
    start = 0
    for piece in refs[:-1]:
        refs[-1][start : start + piece.shape[0], :] = piece[...]
        start += piece.shape[0]


def stack_rows(pieces, tile=256):
    rows, columns = sum(piece.shape[0] for piece in pieces), pieces[0].shape[1]
    return pl.pallas_call(
        stack_kernel,
        grid=(columns // tile,),
        in_specs=[pl.BlockSpec((piece.shape[0], tile), lambda j: (0, j)) for piece in pieces],
        out_specs=pl.BlockSpec((rows, tile), lambda j: (0, j)),
        out_shape=jax.ShapeDtypeStruct((rows, columns), pieces[0].dtype),
        compiler_params=VMEM,
        name="stack_rows",
    )(*pieces)


UNIT_TILE = 256
GELU_IN = math.sqrt(2.0 / math.pi)
GELU_CUBE = 0.044715


def ffn_kernel(source, gate_w, up_w, gate, up, hidden):
    gate_pre = matmul(source[...], gate_w[...])
    up_pre = matmul(source[...], up_w[...])
    gate[...] = gate_pre
    up[...] = up_pre
    inner = GELU_IN * (gate_pre + GELU_CUBE * (gate_pre * gate_pre * gate_pre))
    hidden[...] = (0.5 * gate_pre * (1.0 + jnp.tanh(inner)) * up_pre).astype(BF)


def ffn_back_kernel(grad, gate, up, gate_w, up_w, down_w, gate_grad, up_grad, total):
    hidden_grad = matmul(grad[...], down_w[...])
    gate_pre = gate[...]
    square = gate_pre * gate_pre
    bend = jnp.tanh(GELU_IN * (gate_pre + GELU_CUBE * (square * gate_pre)))
    rise = 0.5 * (1.0 + bend)
    slope = rise + 0.5 * gate_pre * (1.0 - bend * bend) * (GELU_IN * (1.0 + 3.0 * GELU_CUBE * square))
    gate_low = (hidden_grad * up[...] * slope).astype(BF)
    up_low = (hidden_grad * (gate_pre * rise)).astype(BF)
    gate_grad[...] = gate_low
    up_grad[...] = up_low

    @pl.when(pl.program_id(0) == 0)
    def _():
        total[...] = jnp.zeros_like(total)

    total[...] += inner_cols(gate_low, gate_w[...]) + inner_cols(up_low, up_w[...])


def unit_specs(rows, width, tiles):
    own = pl.BlockSpec((rows, UNIT_TILE), lambda j: (0, j))
    weights = [pl.BlockSpec((width, UNIT_TILE), lambda j, i=i: (0, j + i * tiles)) for i in (0, 1, 0)]
    return own, weights


def ffn_forward(source, gate_up_w):
    (rows, width), units = source.shape, gate_up_w.shape[1] // 2
    tiles = units // UNIT_TILE
    own, weights = unit_specs(rows, width, tiles)
    whole = pl.BlockSpec((rows, width), lambda j: (0, 0))
    return pl.pallas_call(
        ffn_kernel,
        grid=(tiles,),
        in_specs=[whole] + weights[:2],
        out_specs=[own, own, own],
        out_shape=[
            jax.ShapeDtypeStruct((rows, units), F32),
            jax.ShapeDtypeStruct((rows, units), F32),
            jax.ShapeDtypeStruct((rows, units), BF),
        ],
        compiler_params=VMEM,
        name="ffn_forward",
    )(source, gate_up_w, gate_up_w)


def ffn_backward(grad, gate, up, gate_up_w, down_w):
    (rows, width), units = grad.shape, down_w.shape[1]
    tiles = units // UNIT_TILE
    own, weights = unit_specs(rows, width, tiles)
    whole = pl.BlockSpec((rows, width), lambda j: (0, 0))
    return pl.pallas_call(
        ffn_back_kernel,
        grid=(tiles,),
        in_specs=[whole, own, own] + weights,
        out_specs=[own, own, whole],
        out_shape=[
            jax.ShapeDtypeStruct((rows, units), BF),
            jax.ShapeDtypeStruct((rows, units), BF),
            jax.ShapeDtypeStruct((rows, width), F32),
        ],
        compiler_params=VMEM,
        name="ffn_backward",
    )(grad, gate, up, gate_up_w, gate_up_w, down_w)


def ffn_wgrad_kernel(steps, left, gate, up, hidden, out):
    rows = gate.shape[0]
    for i, (first, right) in enumerate([(0, gate), (0, up), (rows, hidden)]):

        @pl.when(pl.program_id(0) // steps == i)
        def _(first=first, right=right):
            out[...] = matmul(left[:, first : first + rows], right[...]).astype(BF)


def ffn_wgrad(left, gate, up, hidden):
    width, (rows, units) = left.shape[0], gate.shape
    steps = 2
    tile = units // steps

    def spec(i):
        return pl.BlockSpec((rows, tile), lambda j: (0, jnp.clip(j - i * steps, 0, steps - 1)))

    return pl.pallas_call(
        lambda *refs: ffn_wgrad_kernel(steps, *refs),
        grid=(3 * steps,),
        in_specs=[pl.BlockSpec(left.shape, lambda j: (0, 0)), spec(0), spec(1), spec(2)],
        out_specs=pl.BlockSpec((width, tile), lambda j: (0, j)),
        out_shape=jax.ShapeDtypeStruct((width, 3 * units), BF),
        compiler_params=VMEM,
        name="ffn_wgrad",
    )(left, gate, up, hidden)


def split_rows(values, parts):
    size = values.shape[0] // parts
    return [values[i * size : (i + 1) * size] for i in range(parts)]


def pick(core, first, second):
    return jnp.where(core == 0, first, second)


def shards(
    hidden_in,
    out_grad,
    block_order,
    norm_gains,
    head_gains,
    w_query,
    w_key,
    w_value,
    w_out,
    w_gate,
    w_up,
    w_down,
):
    tokens, width = hidden_in.shape
    y, z, x, core = (lax.axis_index(name) for name in CTX)
    other = 1 - core
    piece = width // 64
    units = w_gate.shape[1] // 2
    padded = (units + 127) // 128 * 128
    quarter = width // 4

    out_t, down_t = w_out.T, w_down.T

    def units_of(which):
        cut = [
            jnp.pad(lax.dynamic_slice_in_dim(w, which * units, units, 1), ((0, 0), (0, padded - units)))
            for w in (w_gate, w_up, down_t)
        ]
        return jnp.concatenate(cut, 1)

    def heads_of(which):
        cut = [lax.dynamic_slice_in_dim(w, which * HD, HD, 1) for w in (w_query, out_t)]
        return jnp.concatenate(cut + [w_key, w_value], 1)

    def chip_rows(of):
        mine, theirs = of(core), of(other)
        from_y, from_core, from_both = exchange((mine, theirs, theirs), "c")
        return pick(
            core,
            jnp.concatenate([mine, from_core, from_y, from_both], 0),
            jnp.concatenate([from_core, mine, from_both, from_y], 0),
        )

    head_rows = chip_rows(heads_of)
    ffn_rows = chip_rows(units_of)
    gate_up_w = lax.all_gather(ffn_rows[:, : 2 * padded], ("z", "x"), axis=0, tiled=True)
    down_rows = after(ffn_rows[:, 2 * padded :], gate_up_w)
    down_w = lax.all_gather(down_rows, ("z", "x"), axis=0, tiled=True)
    head_w = stack_rows(gather_ring(after(gather_direct(head_rows, False), ffn_rows), True))
    hidden_in = after(hidden_in, head_rows)
    query_w, out_w = head_w[:, :HD], head_w[:, HD : 2 * HD]
    key_w, value_w, pair_w = head_w[:, 2 * HD : 3 * HD], head_w[:, 3 * HD :], head_w[:, 2 * HD :]

    place = jnp.arange(width, dtype=jnp.int32)
    first, second = place // quarter, place // (quarter // 4) % 4

    def natural(z_at, x_at):
        y_at = (y + place // (2 * piece)) % 2
        return y_at * (width // 2) + z_at * (8 * piece) + x_at * (2 * piece) + place % (2 * piece)

    by_gather = natural(first, second)
    by_ring = natural((z + pick(core, second, first)) % 4, (x + pick(core, first, second)) % 4)
    to_gather, to_ring = ((place[:, None] == by[None, :]).astype(BF) for by in (by_gather, by_ring))
    from_gather, from_ring = ((by[:, None] == place[None, :]).astype(BF) for by in (by_gather, by_ring))

    def reorder(values, moves):
        return matmul(values, moves).astype(BF)

    def both_cores(values):
        return jnp.concatenate([values, shift(values, "c")], 0)

    def sum_cores(partial, moves):
        low = reorder(partial.astype(BF), moves)
        return wide_sum(low[:tokens], shift(low[tokens:], "c")).astype(BF)

    def sum_parts(partial, moves):
        chip = sum_cores(partial, moves)
        return wide_sum(chip, shift(chip, "s"))

    offsets = jnp.arange(tokens, dtype=jnp.int32)

    def positions_of(places):
        return (block_order[places.reshape(-1)][:, None] * tokens + offsets[None, :]).reshape(-1)

    def device_of(y_at, z_at, x_at, core_at):
        return y_at * 32 + z_at * 8 + x_at * 2 + core_at

    steps = jnp.arange(4, dtype=jnp.int32)
    outer, inner = steps[:, None, None], steps[None, :, None]

    def keys_of(which):
        z_at, x_at = (z + pick(which, inner, outer)) % 4, (x + pick(which, outer, inner)) % 4
        return positions_of(device_of((y + steps[None, None, :2]) % 2, z_at, x_at, which))

    key_pos = [keys_of(core), keys_of(other)]
    own_pos = positions_of(device_of(y, z, x, core))
    chip_pos = jnp.concatenate([own_pos, positions_of(device_of(y, z, x, other))])
    cosine_table, sine_table = tables(chip_pos, HD)

    attn_val, pre_attn_back = jax.vjp(rms_scale, hidden_in, norm_gains[0])
    attn_chip = reorder(both_cores(attn_val.astype(BF)), to_ring)
    attn_ring = attn_chip[:tokens]
    key_pre = matmul(attn_ring, key_w)
    value_low = matmul(attn_ring, value_w).astype(BF)
    key_val, key_back = jax.vjp(
        lambda values, gain: rotate(rms_scale(values, gain), cosine_table[:tokens], sine_table[:tokens]),
        key_pre,
        head_gains[1],
    )
    key_low = key_val.astype(BF)
    pair_low = jnp.concatenate([key_low, value_low], 1)
    pair_pieces = gather_ring(gather_minor_y(pair_low), True)
    own_pairs = jnp.concatenate(pair_pieces, 0)
    pairs = [own_pairs, shift(own_pairs, "c")]

    query_pre = matmul(attn_chip, query_w)
    query_val, query_back = jax.vjp(
        lambda values, gain: rotate(rms_scale(values, gain), cosine_table, sine_table),
        query_pre,
        head_gains[0],
    )
    score_scale = HD ** (-0.5)
    queries = (query_val.astype(BF).astype(F32) * score_scale).astype(BF)
    parts = [attend(queries, pairs[part], key_pos[part], chip_pos) for part in range(2)]
    weights = [part[0] for part in parts]
    inverse_total = 1.0 / (parts[0][1] + parts[1][1])
    accum = parts[0][2] + parts[1][2]
    attn_rows = accum * inverse_total
    mixed_low = attn_rows.astype(BF)
    attn_out = sum_parts(inner_cols(mixed_low, out_w), from_ring)
    post_attn, post_attn_back = jax.vjp(rms_scale, attn_out, norm_gains[1])
    mid_state = hidden_in + post_attn

    ffn_val, ffn_norm_back = jax.vjp(rms_scale, mid_state, norm_gains[2])
    ffn_chip = both_cores(ffn_val.astype(BF))
    gate_pre, up_pre, hidden_low = ffn_forward(reorder(ffn_chip, to_gather), gate_up_w)
    ffn_out = sum_parts(inner_cols(hidden_low, down_w), from_gather)
    post_ffn, post_ffn_back = jax.vjp(rms_scale, ffn_out, norm_gains[3])
    block_out = mid_state + post_ffn

    ffn_grad, gain_four = post_ffn_back(out_grad)
    ffn_grad_chip = both_cores(ffn_grad.astype(BF))
    gate_low, up_low, ffn_norm_part = ffn_backward(reorder(ffn_grad_chip, to_gather), gate_pre, up_pre, gate_up_w, down_w)
    sources = jnp.concatenate([ffn_chip, ffn_grad_chip], 0)
    ffn_norm_chip = sum_cores(ffn_norm_part, from_gather)
    left = after(inner_cols(from_gather, sources).astype(BF), ffn_norm_chip)
    ffn_wgrads = ffn_wgrad(left, gate_low, up_low, hidden_low)
    ffn_sum = lax.psum_scatter(ffn_wgrads, ("z", "x"), scatter_dimension=0, tiled=True)
    ffn_norm_grad = after(wide_sum(ffn_norm_chip, shift(ffn_norm_chip, "s")), ffn_wgrads)
    mid_from, gain_three = ffn_norm_back(ffn_norm_grad)
    mid_grad = out_grad + mid_from

    def last_stage(values):
        parts = split_rows(values.astype(BF), 4)
        kept = [pick(core, parts[i], parts[i + 1]) for i in (0, 2)]
        sent = [pick(core, parts[i + 1], parts[i]) for i in (0, 2)]
        from_y, from_core, from_both = exchange((kept[1], sent[0], sent[1]), "c")
        return wide_sum(kept[0], from_y), wide_sum(from_core, from_both)

    attn_grad, gain_two = post_attn_back(mid_grad)
    attn_grad_chip = reorder(both_cores(attn_grad.astype(BF)), to_ring)
    rows_grad = matmul(attn_grad_chip, out_w).astype(BF)
    rows_wide = rows_grad.astype(F32)
    row_dot = jnp.sum(rows_wide * attn_rows, axis=1)[:, None]
    rows_scaled = (rows_wide * inverse_total).astype(BF)
    pair_far, query_far = attend_back(
        queries, pairs[1], weights[1], rows_grad, rows_scaled, row_dot, inverse_total
    )
    pair_near, query_near = attend_back(
        queries, pairs[0], weights[0], rows_grad, rows_scaled, row_dot, inverse_total
    )
    query_grad = query_far + query_near
    query_pre_grad, query_gain = query_back(query_grad * score_scale)
    query_gain = query_gain + shift(query_gain, "s")
    query_pre_low = query_pre_grad.astype(BF)
    early_grads = jnp.concatenate(
        [inner_rows(attn_chip, query_pre_low), inner_rows(attn_grad_chip, mixed_low)], 1
    ).astype(BF)
    pair_got = shift(pair_far, "c")
    chunks = [
        jnp.concatenate([wide_sum(near, got).astype(BF), early], 0)
        for near, got, early in zip(*(split_rows(part, 4) for part in (pair_near, pair_got, early_grads)))
    ]
    major_sum = reduce_chunks(*chunks, True).astype(BF)
    pair_chunks = split_rows(major_sum[: 8 * tokens], 4)
    early_chunks = split_rows(major_sum[8 * tokens :], 4)
    minor_sum = reduce_direct(
        [jnp.concatenate([pair, early], 0) for pair, early in zip(pair_chunks, early_chunks)], False
    )
    pair_own, pair_far_y = split_rows(minor_sum[: 2 * tokens].astype(BF), 2)
    from_y, from_shard, from_both = exchange((pair_far_y, pair_own, pair_far_y), "s")
    pair_grad = wide_sum(pair_own, from_y) + wide_sum(from_shard, from_both)
    attn_norm_sum = sum_parts(inner_cols(query_pre_low, query_w), from_ring)
    key_pre_grad, key_gain = key_back(pair_grad[:, :HD])
    key_pre_low = key_pre_grad.astype(BF)
    value_grad_low = pair_grad[:, HD:].astype(BF)
    pair_part = inner_cols(jnp.concatenate([key_pre_low, value_grad_low], 1), pair_w).astype(BF)

    kept, sent = pick(core, key_pre_low, value_grad_low), pick(core, value_grad_low, key_pre_low)
    pair_chip = jnp.concatenate([kept, shift(sent, "c")], 0)
    spare = jnp.zeros((8, width), F32)
    norm_rows = jnp.concatenate([gain_two[None], gain_three[None], gain_four[None], spare[:5]], 0)
    head_rows = jnp.concatenate(
        [spare[:3, :HD], query_gain[None], key_gain[None], spare[:3, :HD]], 0
    )
    share = HD // 64
    at_piece, in_piece = by_ring // piece, by_ring % piece
    head_at = jnp.where(in_piece < share, at_piece * share + in_piece, -1)
    head_moves = (head_at[:, None] == jnp.arange(HD, dtype=jnp.int32)[None, :]).astype(BF)
    gains = inner_cols(from_ring, norm_rows.astype(BF)) + inner_cols(head_moves, head_rows.astype(BF))
    gains = jnp.pad(gains, ((0, 0), (0, 120)))
    late_grads = jnp.concatenate([inner_rows(attn_chip, pair_chip), gains], 1).astype(BF)
    ffn_sum = after(ffn_sum, minor_sum)
    first_mine, first_got = last_stage(ffn_sum[:, : 2 * padded])
    late_major = reduce_direct(split_rows(late_grads, 4), True).astype(BF)
    late_major = after(late_major, first_mine, first_got)
    attn_norm_grad = attn_norm_sum + reorder(after(pair_part, late_major), from_ring).astype(F32)
    input_from, _ = pre_attn_back(attn_norm_grad)
    input_grad = mid_grad + input_from
    late_sum = reduce_direct(split_rows(late_major, 4), False)
    early_mine, early_got = last_stage(
        jnp.concatenate([ffn_sum[:, 2 * padded :].astype(F32), minor_sum[2 * tokens :]], 1)
    )
    late_mine, late_got = last_stage(after(late_sum, early_mine, early_got))

    def joined(start, size, mine, got):
        left, right = mine[:, start : start + size], got[:, start : start + size]
        return pick(core, jnp.concatenate([left, right], 1), jnp.concatenate([right, left], 1))

    gate_wgrad = joined(0, units, first_mine, first_got)
    up_wgrad = joined(padded, units, first_mine, first_got)
    down_wgrad = joined(0, units, early_mine, early_got).T

    query_wgrad = joined(padded, HD, early_mine, early_got)
    out_wgrad = joined(padded + HD, HD, early_mine, early_got).T
    pair_wgrad = joined(0, HD, late_mine, late_got)
    key_wgrad, value_wgrad = pair_wgrad[:, :HD], pair_wgrad[:, HD:]
    gain_sums = late_mine[:, HD:] + late_got[:, HD:]

    def along(weight, grad):
        return jnp.sum(weight.astype(F32) * grad, axis=1)

    query_part = along(w_query, query_wgrad)
    attn_part = query_part + shift(query_part, "s") + along(w_key, key_wgrad) + along(w_value, value_wgrad)
    own_gain = lax.dynamic_slice_in_dim(norm_gains[0], device_of(y, z, x, core) * piece, piece)
    gain_one = attn_part / own_gain
    return (
        block_out,
        input_grad,
        query_wgrad,
        key_wgrad,
        value_wgrad,
        out_wgrad,
        gate_wgrad,
        up_wgrad,
        down_wgrad,
        jnp.concatenate([gain_one[None, :], gain_sums[:, :3].T], 0),
        gain_sums[: HD // 64, 3:5].T,
    )


def solution(mesh):
    fine = Mesh(mesh.devices.reshape(2, 4, 4, 2, 2), ("y", "z", "x", "c", "s"))
    placed = (
        P(CTX, None),
        P(CTX, None),
        P(),
        P(),
        P(),
        P(CTX, "s"),
        P(CTX, None),
        P(CTX, None),
        P("s", CTX),
        P(CTX, "s"),
        P(CTX, "s"),
        P("s", CTX),
    )
    return jax.shard_map(
        shards,
        mesh=fine,
        in_specs=placed,
        out_specs=(
            P(CTX, None),
            P(CTX, None),
            P(CTX, "s"),
            P(CTX, None),
            P(CTX, None),
            P("s", CTX),
            P(CTX, "s"),
            P(CTX, "s"),
            P("s", CTX),
            P(None, CTX),
            P(None, CTX),
        ),
        check_vma=False,
    )
```
